768 devices in a mesh: lon: 48 (over z_lo, x, core), lat: 16 (over z_hi, y).
Axes of the slice: x: 4, y: 8, z: 12 (z_hi: 2, z_lo: 6; z = z_hi * 6 + z_lo), core: 2. Of those that a mesh axis runs over, the one named last changes fastest.
Arguments:
- tokens: bfloat16 [768, 512, 128], P('lon', 'lat'), may hold values from -24 to 24
- grad_out: bfloat16 [768, 512, 128], P('lon', 'lat'), may hold values from -6 to 6
- window_ids: int32 [768, 512], P('lon', 'lat'), may hold values from 0 to 2
- qkv_weight: bfloat16 [128, 384], replicated, may hold values from -0.5 to 0.5
- proj_weight: bfloat16 [128, 128], replicated, may hold values from -0.5 to 0.5
- up_weight: bfloat16 [128, 512], replicated, may hold values from -0.5 to 0.5
- down_weight: bfloat16 [512, 128], replicated, may hold values from -0.25 to 0.25
- conv_weight: bfloat16 [9, 128, 128], replicated, may hold values from -0.1875 to 0.1875
- gain_one: float32 [128], replicated, may hold values from 0.1 to 1.9
- gain_two: float32 [128], replicated, may hold values from 0.1 to 1.9
- position_bias: float32 [4, 15, 15], replicated, may hold values from -6 to 330
Outputs:
- downscaled: bfloat16 [768, 512, 128], P('lon', 'lat')
- grad_tokens: bfloat16 [768, 512, 128], P('lon', 'lat')
- grad_qkv: float32 [128, 384], replicated
- grad_proj: float32 [128, 128], replicated
- grad_up: float32 [128, 512], replicated
- grad_down: float32 [512, 128], replicated
- grad_conv: float32 [9, 128, 128], replicated
- grad_gain_one: float32 [128], replicated
- grad_gain_two: float32 [128], replicated
- grad_bias: float32 [4, 15, 15], replicated
The draws below stay inside these ranges and needn't reach their ends.
All inputs are finite; a program needn't handle non-finite values.
Results may differ from the reference program's by a relative error of at most 0.018.
Values may be sent and summed in bfloat16 or wider, within the bound.
No kernel may reach another device: no remote copies, remote signals or barrier semaphores. Data moves between devices by JAX's collectives and lax.ppermute only.
A program may use at most 32 MiB of HBM per device.

```python
import math
import jax
import jax.numpy as jnp
from jax import lax

C = 128
HEADS = 4
FFH = 512
WIN = 8
SHIFT = 4
SPAN = 15
HEAD_DIM = 32
NLON = 768
NLAT = 512
TOKENS = 393216


def draw_tokens(key, part):
    key = jax.random.fold_in(key, 11)
    noise_key, row_key, col_key = jax.random.split(key, 3)
    noise = jax.random.normal(noise_key, (NLON, NLAT, C), jnp.float32)
    row_scale = jnp.exp(jax.random.uniform(row_key, (NLON, NLAT, 1), jnp.float32, math.log(0.3), math.log(3.0)))
    col_scale = jnp.exp(jax.random.uniform(col_key, (1, 1, C), jnp.float32, math.log(0.3), math.log(3.0)))
    return jnp.clip(noise * row_scale * col_scale, -24.0, 24.0).astype(jnp.bfloat16)


def draw_position_bias(key, part):
    key = jax.random.fold_in(key, 23)
    base_key = jax.random.fold_in(key, 0)
    return jnp.clip(jax.random.normal(base_key, (HEADS, SPAN, SPAN), jnp.float32), -6.0, 6.0)


def set_ends(array, key, least, top_value):
    extent = array.shape
    index_at = [jax.random.randint(jax.random.fold_in(key, axis), (), 0, extent[axis]) for axis in range(len(extent))]
    array = array.at[tuple(index_at)].set(least)
    longest = extent.index(max(extent))
    index_at[longest] = (index_at[longest] + 1) % extent[longest]
    return array.at[tuple(index_at)].set(top_value)


def block_scale(own_key, dims, cuts, least, high):
    factor_of, own = 1.0, jax.random.fold_in(own_key, 6)
    for dim, parts in cuts:
        draws = jnp.exp(jax.random.uniform(jax.random.fold_in(own, dim), (parts,), jnp.float32, least / len(cuts), high / len(cuts)))
        factor_of = factor_of * jnp.repeat(draws, dims[dim] // parts).reshape([-1 if axis == dim else 1 for axis in range(len(dims))])
    return factor_of


def normal_values(key, dims, scale, limit, shards=(), kind=jnp.bfloat16):
    array = scale * jax.random.normal(key, dims, jnp.float32)
    if shards:
        array = array * block_scale(key, dims, shards, -0.22, 0.18)
    return jnp.clip(array, -limit, limit).astype(kind)


def setup_inputs(seed: int = 0) -> dict:
    arg_keys = jax.random.split(jax.random.key(seed), 12)
    tokens = draw_tokens(jax.random.fold_in(arg_keys[11], 71), 0)
    grad_out = normal_values(arg_keys[1], (NLON, NLAT, C), 1.0, 6.0, ((0, 48), (1, 16)))
    window_ids = set_ends(jax.random.randint(arg_keys[2], (NLON, NLAT), 0, 3), jax.random.fold_in(arg_keys[2], 1), 0, 2).astype(jnp.int32)
    qkv_weight = normal_values(arg_keys[3], (C, 3 * C), C ** -0.5, 0.5)
    proj_weight = normal_values(arg_keys[4], (C, C), C ** -0.5, 0.5)
    up_weight = normal_values(arg_keys[5], (C, FFH), C ** -0.5, 0.5)
    down_weight = normal_values(arg_keys[6], (FFH, C), FFH ** -0.5, 0.25)
    conv_weight = normal_values(arg_keys[7], (9, C, C), (9 * C) ** -0.5, 0.1875)
    gain_one = jnp.clip(1.0 + 0.18 * jax.random.normal(arg_keys[8], (C,), jnp.float32), 0.1, 1.9)
    gain_two = jnp.clip(1.0 + 0.18 * jax.random.normal(arg_keys[9], (C,), jnp.float32), 0.1, 1.9)
    position_bias = draw_position_bias(jax.random.fold_in(arg_keys[11], 71), 0)
    return dict(tokens=tokens, grad_out=grad_out, window_ids=window_ids, qkv_weight=qkv_weight, proj_weight=proj_weight, up_weight=up_weight, down_weight=down_weight, conv_weight=conv_weight, gain_one=gain_one, gain_two=gain_two, position_bias=position_bias)


epsilon = 1e-05

def layer_norm(values, gain_vec):
    average = lax.optimization_barrier(jnp.mean(values, axis=-1, keepdims=True))
    centred = values - average
    variance = lax.optimization_barrier(jnp.mean(centred * centred, axis=-1, keepdims=True))
    inverse = lax.rsqrt(variance + epsilon)
    normed = centred * inverse
    return ((normed * gain_vec).astype(jnp.bfloat16), normed, inverse)

def layer_norm_back(grad_in, normed, inverse, gain_vec):
    scaled = grad_in * gain_vec
    first_mean = lax.optimization_barrier(jnp.mean(scaled, axis=-1, keepdims=True))
    second = lax.optimization_barrier(jnp.mean(scaled * normed, axis=-1, keepdims=True))
    return inverse * (scaled - first_mean - normed * second)

def gelu_slope(pre_act):
    cumulative = 0.5 * (1.0 + jax.scipy.special.erf(pre_act * 0.7071067811865476))
    density = jnp.exp(-0.5 * pre_act * pre_act) * 0.3989422804014327
    return cumulative + pre_act * density

def rounded(values):
    return lax.optimization_barrier(values.astype(jnp.bfloat16)).astype(jnp.float32)

def offsets_onehot():
    places = jnp.arange(WIN, dtype=jnp.int32)
    distance = places[:, None] - places[None, :] + WIN - 1
    return (distance[:, :, None] == jnp.arange(SPAN, dtype=jnp.int32)[None, None, :]).astype(jnp.float32)

def bias_matrix(position_bias):
    onehot = offsets_onehot()
    spread = jnp.einsum('hmn,acm,bdn->habcd', position_bias, onehot, onehot, precision=lax.Precision.HIGHEST)
    return spread.reshape(HEADS, WIN * WIN, WIN * WIN)

def to_windows(values_grid):
    row_count, col_count = (values_grid.shape[0], values_grid.shape[1])
    trailing = values_grid.shape[2:]
    reshaped = values_grid.reshape((row_count // WIN, WIN, col_count // WIN, WIN) + trailing)
    permute = (0, 2, 1, 3) + tuple(range(4, 4 + len(trailing)))
    return reshaped.transpose(permute).reshape((row_count // WIN * (col_count // WIN), WIN * WIN) + trailing)

def from_windows(blocks, row_count, col_count):
    trailing = blocks.shape[2:]
    reshaped = blocks.reshape((row_count // WIN, col_count // WIN, WIN, WIN) + trailing)
    permute = (0, 2, 1, 3) + tuple(range(4, 4 + len(trailing)))
    return reshaped.transpose(permute).reshape((row_count, col_count) + trailing)

def attend(windows, labels_win, qkv_weight, biases):
    window_count = windows.shape[0]
    qkv_all = jnp.dot(windows, qkv_weight, preferred_element_type=jnp.float32).astype(jnp.bfloat16)
    split_heads = qkv_all.reshape(window_count, WIN * WIN, 3, HEADS, HEAD_DIM).astype(jnp.float32)
    query_heads, key_heads, value_heads = (split_heads[:, :, 0], split_heads[:, :, 1], split_heads[:, :, 2])
    score_scale = HEAD_DIM ** (-0.5)
    scores = jnp.einsum('nihe,njhe->nhij', query_heads, key_heads) * score_scale + biases[None]
    allowed = labels_win[:, None, :, None] == labels_win[:, None, None, :]
    scores = jnp.where(allowed, scores, -jnp.inf)
    probabilities = jax.nn.softmax(scores, axis=-1)
    weights = rounded(probabilities)
    mixed_win = jnp.einsum('nhij,njhe->nihe', weights, value_heads).astype(jnp.bfloat16)
    return (mixed_win.reshape(window_count, WIN * WIN, C), qkv_all, probabilities)

def attend_back(grad_mixed, qkv_all, probabilities):
    window_count = qkv_all.shape[0]
    split_heads = qkv_all.reshape(window_count, WIN * WIN, 3, HEADS, HEAD_DIM).astype(jnp.float32)
    query_heads, key_heads, value_heads = (split_heads[:, :, 0], split_heads[:, :, 1], split_heads[:, :, 2])
    grad_heads = grad_mixed.reshape(window_count, WIN * WIN, HEADS, HEAD_DIM).astype(jnp.float32)
    weights = rounded(probabilities)
    grad_probs = jnp.einsum('nihe,njhe->nhij', grad_heads, value_heads)
    grad_value = jnp.einsum('nhij,nihe->njhe', weights, grad_heads)
    grad_scores = probabilities * (grad_probs - lax.optimization_barrier(jnp.sum(probabilities * grad_probs, axis=-1, keepdims=True)))
    bias_part = lax.optimization_barrier(jnp.sum(grad_scores, axis=0))
    grad_scores_b = rounded(grad_scores)
    score_scale = HEAD_DIM ** (-0.5)
    grad_query = jnp.einsum('nhij,njhe->nihe', grad_scores_b, key_heads) * score_scale
    grad_key = jnp.einsum('nhij,nihe->njhe', grad_scores_b, query_heads) * score_scale
    stacked = jnp.stack([grad_query, grad_key, grad_value], axis=2)
    return (stacked.reshape(window_count, WIN * WIN, 3 * C).astype(jnp.bfloat16), bias_part)

def pad_grid(values_grid):
    wrapped = jnp.concatenate([values_grid[-1:], values_grid, values_grid[:1]], axis=0)
    return jnp.pad(wrapped, ((0, 0), (1, 1), (0, 0)))

def conv_forward(padded, conv_weight):
    row_count = padded.shape[0] - 2
    col_count = padded.shape[1] - 2
    summed = jnp.zeros((row_count, col_count, conv_weight.shape[2]), jnp.float32)
    for tap_row in range(3):
        for tap_col in range(3):
            window_part = padded[tap_row:tap_row + row_count, tap_col:tap_col + col_count]
            summed = summed + jnp.dot(window_part, conv_weight[3 * tap_row + tap_col], preferred_element_type=jnp.float32)
    return summed

def conv_weight_sum(padded, grad_field):
    row_count = padded.shape[0] - 2
    col_count = padded.shape[1] - 2
    flat_grad = grad_field.reshape(-1, grad_field.shape[-1])
    pieces = []
    for tap_row in range(3):
        for tap_col in range(3):
            window_part = padded[tap_row:tap_row + row_count, tap_col:tap_col + col_count].reshape(-1, padded.shape[-1])
            pieces.append(jnp.dot(window_part.T, flat_grad, preferred_element_type=jnp.float32))
    return jnp.stack(pieces)

def conv_input_grad(grad_padded, conv_weight):
    row_count = grad_padded.shape[0] - 2
    col_count = grad_padded.shape[1] - 2
    summed = jnp.zeros((row_count, col_count, conv_weight.shape[1]), jnp.float32)
    for tap_row in range(3):
        for tap_col in range(3):
            start_row = 2 - tap_row
            start_col = 2 - tap_col
            window_part = grad_padded[start_row:start_row + row_count, start_col:start_col + col_count]
            summed = summed + jnp.dot(window_part, conv_weight[3 * tap_row + tap_col].T, preferred_element_type=jnp.float32)
    return summed

def reference(tokens, grad_out, window_ids, qkv_weight, proj_weight, up_weight, down_weight, conv_weight, gain_one, gain_two, position_bias):
    biases = bias_matrix(position_bias)
    lat_places = jnp.arange(NLAT, dtype=jnp.int32)
    seam_flag = (lat_places >= NLAT - SHIFT).astype(jnp.int32)
    labels = window_ids * 2 + seam_flag[None, :]
    label_blocks = to_windows(labels).reshape(NLON // WIN, NLAT // WIN, WIN * WIN)
    source = tokens.astype(jnp.float32)
    ln_one, normed_one, inverse_one = layer_norm(source, gain_one)
    shifted = jnp.roll(ln_one, (-SHIFT, -SHIFT), axis=(0, 1))
    blocks = to_windows(shifted).reshape(NLON // WIN, NLAT // WIN, WIN * WIN, C)

    def forward_block(inputs):
        mixed_win, qkv_all, probabilities = attend(inputs[0], inputs[1], qkv_weight, biases)
        return mixed_win
    mixed_blocks = lax.map(forward_block, (blocks, label_blocks))
    mixed_grid = from_windows(mixed_blocks.reshape(-1, WIN * WIN, C), NLON, NLAT)
    projected = jnp.dot(mixed_grid, proj_weight, preferred_element_type=jnp.float32).astype(jnp.bfloat16)
    attention = jnp.roll(projected, (SHIFT, SHIFT), axis=(0, 1))
    middle = source + attention.astype(jnp.float32)
    ln_two, normed_two, inverse_two = layer_norm(middle, gain_two)
    pre_act = jnp.dot(ln_two, up_weight, preferred_element_type=jnp.float32)
    hidden = jax.nn.gelu(pre_act, approximate=False).astype(jnp.bfloat16)
    block_out = (middle + jnp.dot(hidden, down_weight, preferred_element_type=jnp.float32)).astype(jnp.bfloat16)
    padded = pad_grid(block_out)
    downscaled = conv_forward(padded, conv_weight).astype(jnp.bfloat16)
    conv_sum = conv_weight_sum(padded, grad_out)
    grad_block = conv_input_grad(pad_grid(grad_out), conv_weight)
    grad_block_b = grad_block.astype(jnp.bfloat16)
    down_sum = jnp.dot(hidden.reshape(-1, FFH).T, grad_block_b.reshape(-1, C), preferred_element_type=jnp.float32)
    grad_hidden = jnp.dot(grad_block_b, down_weight.T, preferred_element_type=jnp.float32)
    grad_pre = (grad_hidden * gelu_slope(pre_act)).astype(jnp.bfloat16)
    up_sum = jnp.dot(ln_two.reshape(-1, C).T, grad_pre.reshape(-1, FFH), preferred_element_type=jnp.float32)
    grad_ln_two = jnp.dot(grad_pre, up_weight.T, preferred_element_type=jnp.float32)
    gain_two_sum = lax.optimization_barrier(jnp.sum(grad_ln_two * normed_two, axis=(0, 1)))
    grad_middle = grad_block + layer_norm_back(grad_ln_two, normed_two, inverse_two, gain_two)
    grad_att = jnp.roll(grad_middle.astype(jnp.bfloat16), (-SHIFT, -SHIFT), axis=(0, 1))
    proj_sum = jnp.dot(mixed_grid.reshape(-1, C).T, grad_att.reshape(-1, C), preferred_element_type=jnp.float32)
    grad_mixed = jnp.dot(grad_att, proj_weight.T, preferred_element_type=jnp.float32).astype(jnp.bfloat16)
    grad_blocks = to_windows(grad_mixed).reshape(NLON // WIN, NLAT // WIN, WIN * WIN, C)

    def backward_block(carry, inputs):
        mixed_win, qkv_all, probabilities = attend(inputs[0], inputs[1], qkv_weight, biases)
        grad_qkv_win, bias_part = attend_back(inputs[2], qkv_all, probabilities)
        return (carry + bias_part, grad_qkv_win)
    bias_sum, grad_qkv_blocks = lax.scan(backward_block, jnp.zeros((HEADS, WIN * WIN, WIN * WIN), jnp.float32), (blocks, label_blocks, grad_blocks))
    grad_qkv_all = from_windows(grad_qkv_blocks.reshape(-1, WIN * WIN, 3 * C), NLON, NLAT)
    qkv_sum = jnp.dot(shifted.reshape(-1, C).T, grad_qkv_all.reshape(-1, 3 * C), preferred_element_type=jnp.float32)
    grad_shifted = jnp.dot(grad_qkv_all, qkv_weight.T, preferred_element_type=jnp.float32)
    grad_ln_one = jnp.roll(grad_shifted, (SHIFT, SHIFT), axis=(0, 1))
    gain_one_sum = lax.optimization_barrier(jnp.sum(grad_ln_one * normed_one, axis=(0, 1)))
    grad_tokens = (grad_middle + layer_norm_back(grad_ln_one, normed_one, inverse_one, gain_one)).astype(jnp.bfloat16)
    onehot = offsets_onehot()
    table_sum = jnp.einsum('habcd,acm,bdn->hmn', bias_sum.reshape(HEADS, WIN, WIN, WIN, WIN), onehot, onehot, precision=lax.Precision.HIGHEST)
    grad_scale = 1.0 / math.sqrt(TOKENS)
    return (downscaled, grad_tokens, qkv_sum * grad_scale, proj_sum * grad_scale, up_sum * grad_scale, down_sum * grad_scale, conv_sum * grad_scale, gain_one_sum * grad_scale, gain_two_sum * grad_scale, table_sum * grad_scale)
```

```python
import math

import jax
import jax.numpy as jnp
from jax import lax
from jax.sharding import Mesh
from jax.sharding import PartitionSpec as P

HEADS = 4
WIN = 8
SHIFT = 4
SPAN = 15
HEAD_DIM = 32
TOKEN_RIM = 4
GRAD_RIM = 5
LABEL_RIM = 8

LON = ("zl", "x", "c")
LAT = ("zh", "y")
NEAR = ("x", "c")
FAR = ("y", "zl", "zh")

epsilon = 1e-05


def swapped(value, axes, first):
    count = lax.axis_size(axes)
    pairs = []
    for source in range(count):
        up = (source % 2 == 0) == first
        pairs.append((source, (source + 1) % count if up else (source - 1) % count))
    return lax.ppermute(value, axes, pairs)


def traded(to_next, to_prev, axes):
    even = lax.axis_index(axes) % 2 == 0
    later = swapped(jnp.where(even, to_prev, to_next), axes, False)
    near = swapped(jnp.where(even, to_next, to_prev), axes, True)
    return jnp.where(even, later, near), jnp.where(even, near, later)


def lon_halo(tokens, grad_out, ids):
    row_count, col_count, width = tokens.shape
    id_rows = jnp.pad(ids[row_count - LABEL_RIM :].T, ((0, 0), (0, width - LABEL_RIM)))[None]
    to_next = jnp.concatenate([tokens[-TOKEN_RIM:], grad_out[-GRAD_RIM:], id_rows])
    to_prev = jnp.concatenate([tokens[:TOKEN_RIM], grad_out[:GRAD_RIM], jnp.zeros_like(id_rows)])
    before, after = traded(to_next, to_prev, LON)
    split = TOKEN_RIM + GRAD_RIM
    tokens = jnp.concatenate([before[:TOKEN_RIM], tokens, after[:TOKEN_RIM]])
    grad_out = jnp.concatenate([before[TOKEN_RIM:split], grad_out, after[TOKEN_RIM:split]])
    ids = jnp.concatenate([before[split, :, :LABEL_RIM].T, ids])
    return tokens, grad_out, ids


def lat_halo(tokens, grad_out, ids):
    token_rows, col_count, width = tokens.shape
    grad_rows = grad_out.shape[0]
    token_size, grad_size = token_rows * TOKEN_RIM, grad_rows * GRAD_RIM
    id_cols = jnp.pad(ids[:, col_count - LABEL_RIM :], ((0, 0), (0, width - LABEL_RIM)))

    def packed(token_part, grad_part, id_part):
        return jnp.concatenate(
            [token_part.reshape(token_size, width), grad_part.reshape(grad_size, width), id_part]
        )

    def unpacked(message):
        return (
            message[:token_size].reshape(token_rows, TOKEN_RIM, width),
            message[token_size : token_size + grad_size].reshape(grad_rows, GRAD_RIM, width),
            message[token_size + grad_size :, :LABEL_RIM],
        )

    to_next = packed(tokens[:, -TOKEN_RIM:], grad_out[:, -GRAD_RIM:], id_cols)
    to_prev = packed(tokens[:, :TOKEN_RIM], grad_out[:, :GRAD_RIM], jnp.zeros_like(id_cols))
    before, after = traded(to_next, to_prev, LAT)
    tokens_before, grad_before, ids_before = unpacked(before)
    tokens_after, grad_after, _ = unpacked(after)
    return (
        jnp.concatenate([tokens_before, tokens, tokens_after], axis=1),
        jnp.concatenate([grad_before, grad_out, grad_after], axis=1),
        jnp.concatenate([ids_before, ids], axis=1),
    )


def scattered_sum(partial, axes):
    count = lax.axis_size(axes)
    chunks = partial.reshape(count, partial.shape[0] // count, partial.shape[1])
    received = lax.all_to_all(chunks, axes, 0, 0, tiled=True)
    return jnp.sum(received.astype(jnp.float32), axis=0)


def gathered(chunk, axes):
    count = lax.axis_size(axes)
    copies = jnp.broadcast_to(chunk[None], (count,) + chunk.shape)
    return lax.all_to_all(copies, axes, 0, 0, tiled=True).reshape(-1, chunk.shape[1])


def total_over_devices(rows, grad_scale):
    count = lax.axis_size(NEAR) * lax.axis_size(FAR)
    total_rows = rows.shape[0]
    rows = jnp.pad(rows, ((0, -total_rows % count), (0, 0))).astype(jnp.bfloat16)
    near = scattered_sum(rows, NEAR).astype(jnp.bfloat16)
    own = (scattered_sum(near, FAR) * grad_scale).astype(jnp.bfloat16)
    for axes in GATHERS:
        own = gathered(own, axes)
    return own[:total_rows].astype(jnp.float32)


GATHERS = (("zl", "zh"), ("y",), ("x", "c"))


def blocks_of(matrix):
    height, width = matrix.shape
    return matrix.reshape(height, width // 128, 128).transpose(1, 0, 2).reshape(-1, 128)


def from_blocks(rows, width):
    count = width // 128
    return rows.reshape(count, -1, 128).transpose(1, 0, 2).reshape(-1, width)


def layer_norm(values, gain_vec):
    average = jnp.mean(values, axis=-1, keepdims=True)
    centred = values - average
    variance = jnp.mean(centred * centred, axis=-1, keepdims=True)
    inverse = lax.rsqrt(variance + epsilon)
    normed = centred * inverse
    return ((normed * gain_vec).astype(jnp.bfloat16), normed, inverse)


def layer_norm_back(grad_in, normed, inverse, gain_vec):
    scaled = grad_in * gain_vec
    first_mean = jnp.mean(scaled, axis=-1, keepdims=True)
    second = jnp.mean(scaled * normed, axis=-1, keepdims=True)
    return inverse * (scaled - first_mean - normed * second)


def gelu_slope(pre_act):
    cumulative = 0.5 * (1.0 + jax.scipy.special.erf(pre_act * 0.7071067811865476))
    density = jnp.exp(-0.5 * pre_act * pre_act) * 0.3989422804014327
    return cumulative + pre_act * density


def offsets_onehot():
    places = jnp.arange(WIN, dtype=jnp.int32)
    distance = places[:, None] - places[None, :] + WIN - 1
    return (distance[:, :, None] == jnp.arange(SPAN, dtype=jnp.int32)[None, None, :]).astype(
        jnp.float32
    )


def bias_matrix(position_bias):
    onehot = offsets_onehot()
    spread = jnp.einsum(
        "hmn,acm,bdn->habcd", position_bias, onehot, onehot, precision=lax.Precision.HIGHEST
    )
    return spread.reshape(HEADS, WIN * WIN, WIN * WIN)


def to_windows(values_grid):
    row_count, col_count = (values_grid.shape[0], values_grid.shape[1])
    trailing = values_grid.shape[2:]
    reshaped = values_grid.reshape((row_count // WIN, WIN, col_count // WIN, WIN) + trailing)
    permute = (0, 2, 1, 3) + tuple(range(4, 4 + len(trailing)))
    return reshaped.transpose(permute).reshape(
        (row_count // WIN * (col_count // WIN), WIN * WIN) + trailing
    )


def from_windows(blocks, row_count, col_count):
    trailing = blocks.shape[2:]
    reshaped = blocks.reshape((row_count // WIN, col_count // WIN, WIN, WIN) + trailing)
    permute = (0, 2, 1, 3) + tuple(range(4, 4 + len(trailing)))
    return reshaped.transpose(permute).reshape((row_count, col_count) + trailing)


def attend(windows, labels_win, qkv_weight, biases):
    window_count, length, width = windows.shape
    qkv_all = jnp.dot(windows, qkv_weight, preferred_element_type=jnp.float32).astype(jnp.bfloat16)
    split_heads = qkv_all.reshape(window_count, length, 3, HEADS, HEAD_DIM)
    query_heads, key_heads, value_heads = (
        split_heads[:, :, 0],
        split_heads[:, :, 1],
        split_heads[:, :, 2],
    )
    score_scale = HEAD_DIM ** (-0.5)
    scores = (
        jnp.einsum("nihe,njhe->nhij", query_heads, key_heads, preferred_element_type=jnp.float32)
        * score_scale
        + biases[None]
    )
    allowed = labels_win[:, None, :, None] == labels_win[:, None, None, :]
    scores = jnp.where(allowed, scores, -jnp.inf)
    probabilities = jax.nn.softmax(scores, axis=-1)
    weights = probabilities.astype(jnp.bfloat16)
    mixed_win = jnp.einsum(
        "nhij,njhe->nihe", weights, value_heads, preferred_element_type=jnp.float32
    ).astype(jnp.bfloat16)
    return (mixed_win.reshape(window_count, length, width), qkv_all, probabilities, weights)


def attend_back(grad_mixed, qkv_all, probabilities, weights):
    window_count, length, width = grad_mixed.shape
    split_heads = qkv_all.reshape(window_count, length, 3, HEADS, HEAD_DIM)
    query_heads, key_heads, value_heads = (
        split_heads[:, :, 0],
        split_heads[:, :, 1],
        split_heads[:, :, 2],
    )
    grad_heads = grad_mixed.reshape(window_count, length, HEADS, HEAD_DIM)
    grad_probs = jnp.einsum(
        "nihe,njhe->nhij", grad_heads, value_heads, preferred_element_type=jnp.float32
    )
    grad_value = jnp.einsum(
        "nhij,nihe->njhe", weights, grad_heads, preferred_element_type=jnp.float32
    )
    grad_scores = probabilities * (
        grad_probs - jnp.sum(probabilities * grad_probs, axis=-1, keepdims=True)
    )
    grad_scores_b = grad_scores.astype(jnp.bfloat16)
    score_scale = HEAD_DIM ** (-0.5)
    grad_query = (
        jnp.einsum("nhij,njhe->nihe", grad_scores_b, key_heads, preferred_element_type=jnp.float32)
        * score_scale
    )
    grad_key = (
        jnp.einsum(
            "nhij,nihe->njhe", grad_scores_b, query_heads, preferred_element_type=jnp.float32
        )
        * score_scale
    )
    stacked = jnp.stack([grad_query, grad_key, grad_value], axis=2)
    return (stacked.reshape(window_count, length, 3 * width).astype(jnp.bfloat16), grad_scores)


def conv_forward(padded, conv_weight, keep):
    row_count = padded.shape[0] - 2
    col_count = padded.shape[1] - 2
    summed = jnp.zeros((row_count, col_count, conv_weight.shape[2]), jnp.float32)
    for tap_row in range(3):
        for tap_col in range(3):
            window_part = padded[tap_row : tap_row + row_count, tap_col : tap_col + col_count]
            product = jnp.dot(
                window_part, conv_weight[3 * tap_row + tap_col], preferred_element_type=jnp.float32
            )
            summed = summed + product * keep[tap_col][None, :, None]
    return summed


def conv_weight_sum(padded, grad_field, keep):
    row_count = padded.shape[0] - 2
    col_count = padded.shape[1] - 2
    pieces = []
    for tap_row in range(3):
        for tap_col in range(3):
            window_part = padded[tap_row : tap_row + row_count, tap_col : tap_col + col_count]
            masked = grad_field * keep[tap_col][None, :, None]
            pieces.append(
                jnp.einsum("lwc,lwd->cd", window_part, masked, preferred_element_type=jnp.float32)
            )
    return jnp.stack(pieces)


def conv_input_grad(grad_padded, conv_weight, keep):
    row_count = grad_padded.shape[0] - 2
    col_count = grad_padded.shape[1] - 2
    summed = jnp.zeros((row_count, col_count, conv_weight.shape[1]), jnp.float32)
    for tap_row in range(3):
        for tap_col in range(3):
            start_row = 2 - tap_row
            start_col = 2 - tap_col
            window_part = grad_padded[
                start_row : start_row + row_count, start_col : start_col + col_count
            ]
            window_part = (
                window_part * keep[start_col][None, :, None]
            )
            summed = summed + jnp.einsum(
                "lwd,cd->lwc",
                window_part,
                conv_weight[3 * tap_row + tap_col],
                preferred_element_type=jnp.float32,
            )
    return summed


def local_work(
    tokens_ext,
    grad_ext,
    labels,
    positions,
    lat_total,
    qkv_weight,
    proj_weight,
    up_weight,
    down_weight,
    conv_weight,
    gain_one,
    gain_two,
    position_bias,
):
    row_count, col_count, width = tokens_ext.shape
    own_rows, own_cols = row_count - 2 * TOKEN_RIM, col_count - 2 * TOKEN_RIM
    keep = jnp.stack(
        [positions != 0, jnp.ones_like(positions, jnp.bool_), positions != lat_total - 1]
    ).astype(jnp.bfloat16)
    keep_own = keep[:, TOKEN_RIM:-TOKEN_RIM]
    owned = lambda grid: grid[WIN:, WIN:]
    source = tokens_ext.astype(jnp.float32)
    biases = bias_matrix(position_bias)
    ln_one, normed_one, inverse_one = layer_norm(source, gain_one)
    mixed_win, qkv_all, probabilities, weights = attend(
        to_windows(ln_one), to_windows(labels), qkv_weight, biases
    )
    mixed_grid = from_windows(mixed_win, row_count, col_count)
    projected = jnp.dot(mixed_grid, proj_weight, preferred_element_type=jnp.float32).astype(
        jnp.bfloat16
    )
    middle = source + projected.astype(jnp.float32)
    ln_two, normed_two, inverse_two = layer_norm(middle, gain_two)
    pre_act = jnp.dot(ln_two, up_weight, preferred_element_type=jnp.float32)
    hidden = jax.nn.gelu(pre_act, approximate=False).astype(jnp.bfloat16)
    block_out = (middle + jnp.dot(hidden, down_weight, preferred_element_type=jnp.float32)).astype(
        jnp.bfloat16
    )
    rim = TOKEN_RIM - 1
    padded = block_out[rim:-rim, rim:-rim]
    downscaled = conv_forward(padded, conv_weight, keep_own).astype(jnp.bfloat16)
    conv_sum = conv_weight_sum(
        padded, grad_ext[GRAD_RIM:-GRAD_RIM, GRAD_RIM:-GRAD_RIM], keep_own
    )
    grad_block = conv_input_grad(grad_ext, conv_weight, keep)
    grad_block_b = grad_block.astype(jnp.bfloat16)
    down_sum = jnp.einsum(
        "lwf,lwc->fc", owned(hidden), owned(grad_block_b), preferred_element_type=jnp.float32
    )
    grad_hidden = jnp.einsum(
        "lwc,fc->lwf", grad_block_b, down_weight, preferred_element_type=jnp.float32
    )
    grad_pre = (grad_hidden * gelu_slope(pre_act)).astype(jnp.bfloat16)
    up_sum = jnp.einsum(
        "lwc,lwf->cf", owned(ln_two), owned(grad_pre), preferred_element_type=jnp.float32
    )
    grad_ln_two = jnp.einsum("lwf,cf->lwc", grad_pre, up_weight, preferred_element_type=jnp.float32)
    gain_two_sum = jnp.sum(owned(grad_ln_two * normed_two), axis=(0, 1))
    grad_middle = grad_block + layer_norm_back(grad_ln_two, normed_two, inverse_two, gain_two)
    grad_att = grad_middle.astype(jnp.bfloat16)
    proj_sum = jnp.einsum(
        "lwc,lwd->cd", owned(mixed_grid), owned(grad_att), preferred_element_type=jnp.float32
    )
    grad_mixed = jnp.einsum(
        "lwd,cd->lwc", grad_att, proj_weight, preferred_element_type=jnp.float32
    ).astype(jnp.bfloat16)
    grad_qkv_win, grad_scores = attend_back(
        to_windows(grad_mixed), qkv_all, probabilities, weights
    )
    length = WIN * WIN
    by_place = grad_scores.reshape(row_count // WIN, col_count // WIN, HEADS, length, length)
    bias_sum = jnp.sum(by_place[1:, 1:], axis=(0, 1))
    grad_qkv_all = from_windows(grad_qkv_win, row_count, col_count)
    qkv_sum = jnp.einsum(
        "lwc,lwk->ck", owned(ln_one), owned(grad_qkv_all), preferred_element_type=jnp.float32
    )
    grad_ln_one = jnp.einsum(
        "lwk,ck->lwc", grad_qkv_all, qkv_weight, preferred_element_type=jnp.float32
    )
    gain_one_sum = jnp.sum(owned(grad_ln_one * normed_one), axis=(0, 1))
    grad_tokens = (
        grad_middle + layer_norm_back(grad_ln_one, normed_one, inverse_one, gain_one)
    ).astype(jnp.bfloat16)[TOKEN_RIM:-TOKEN_RIM, TOKEN_RIM:-TOKEN_RIM]
    onehot = offsets_onehot()
    table_sum = jnp.einsum(
        "habcd,acm,bdn->hmn",
        bias_sum.reshape(HEADS, WIN, WIN, WIN, WIN),
        onehot,
        onehot,
        precision=lax.Precision.HIGHEST,
    )
    rows = jnp.concatenate(
        [
            conv_sum.reshape(-1, 128),
            blocks_of(qkv_sum),
            proj_sum,
            blocks_of(up_sum),
            down_sum,
            gain_one_sum[None],
            gain_two_sum[None],
            jnp.pad(table_sum.reshape(-1), (0, 124)).reshape(8, 128),
        ]
    )
    return downscaled, grad_tokens, rows


def per_device(
    tokens,
    grad_out,
    window_ids,
    qkv_weight,
    proj_weight,
    up_weight,
    down_weight,
    conv_weight,
    gain_one,
    gain_two,
    position_bias,
):
    row_count, col_count, width = tokens.shape
    lat_total = col_count * lax.axis_size(LAT)
    tokens_all = row_count * lat_total * lax.axis_size(LON)
    ids = window_ids.astype(jnp.bfloat16)
    tokens_ext, grad_ext, ids_ext = lat_halo(*lon_halo(tokens, grad_out, ids))
    first_col = lax.axis_index(LAT) * col_count
    steps = jnp.arange(col_count + 2 * TOKEN_RIM, dtype=jnp.int32)
    positions = jnp.remainder(first_col + steps - TOKEN_RIM, lat_total)
    shifted_cols = jnp.remainder(first_col + steps - LABEL_RIM, lat_total)
    seam_flag = (shifted_cols >= lat_total - SHIFT).astype(jnp.int32)
    labels = ids_ext.astype(jnp.int32) * 2 + seam_flag[None, :]
    downscaled, grad_tokens, rows = local_work(
        tokens_ext,
        grad_ext,
        labels,
        positions,
        lat_total,
        qkv_weight,
        proj_weight,
        up_weight,
        down_weight,
        conv_weight,
        gain_one,
        gain_two,
        position_bias,
    )
    totals = total_over_devices(rows, 1.0 / math.sqrt(tokens_all))
    sizes = (9 * width, 3 * width, width, 4 * width, 4 * width, 1, 1, 8)
    pieces = []
    offset = 0
    for size in sizes:
        pieces.append(totals[offset : offset + size])
        offset = offset + size
    return (
        downscaled,
        grad_tokens,
        from_blocks(pieces[1], 3 * width),
        pieces[2],
        from_blocks(pieces[3], 4 * width),
        pieces[4],
        pieces[0].reshape(9, width, width),
        pieces[5][0],
        pieces[6][0],
        pieces[7].reshape(-1)[: HEADS * SPAN * SPAN].reshape(HEADS, SPAN, SPAN),
    )


def solution(mesh):
    lon_count, lat_count = mesh.devices.shape
    near = math.gcd(lon_count, 8)
    parts = (lon_count // near, near // 2, 2, 2, lat_count // 2)
    fine = Mesh(mesh.devices.reshape(parts), ("zl", "x", "c", "zh", "y"))
    grid = P(LON, LAT, None)
    return jax.shard_map(
        per_device,
        mesh=fine,
        in_specs=(grid, grid, P(LON, LAT)) + (P(),) * 8,
        out_specs=(grid, grid) + (P(),) * 8,
        check_vma=False,
    )
```

```python
import math

import jax
import jax.numpy as jnp
from jax import lax
from jax.experimental import pallas as pl
from jax.experimental.pallas import tpu as pltpu
from jax.sharding import Mesh
from jax.sharding import PartitionSpec as P

HEADS = 4
WIN = 8
SHIFT = 4
SPAN = 15
HEAD_DIM = 32
AREA = WIN * WIN
WIN_ROWS = 3
WIN_COLS = 5
PAD_COLS = 48
ROWS = 3072
TOKEN_RIM = 4
GRAD_RIM = 5
LABEL_RIM = 8

LON = ("zl", "x", "c")
LAT = ("zh", "y")
NEAR = ("x", "c")
DEEP = ("zl", "zh")

epsilon = 1e-05


def swapped(value, axes, first):
    count = lax.axis_size(axes)
    pairs = []
    for source in range(count):
        up = (source % 2 == 0) == first
        pairs.append((source, (source + 1) % count if up else (source - 1) % count))
    return lax.ppermute(value, axes, pairs)


def traded(to_next, to_prev, axes):
    even = lax.axis_index(axes) % 2 == 0
    later = swapped(jnp.where(even, to_prev, to_next), axes, False)
    near = swapped(jnp.where(even, to_next, to_prev), axes, True)
    return jnp.where(even, later, near), jnp.where(even, near, later)


def lon_halo(tokens, grad_out, ids):
    row_count, col_count, width = tokens.shape
    id_rows = jnp.pad(ids[row_count - LABEL_RIM :].T, ((0, 0), (0, width - LABEL_RIM)))[None]
    to_next = jnp.concatenate([tokens[-TOKEN_RIM:], grad_out[-GRAD_RIM:], id_rows])
    to_prev = jnp.concatenate([tokens[:TOKEN_RIM], grad_out[:GRAD_RIM], jnp.zeros_like(id_rows)])
    before, after = traded(to_next, to_prev, LON)
    split = TOKEN_RIM + GRAD_RIM
    tokens = jnp.concatenate([before[:TOKEN_RIM], tokens, after[:TOKEN_RIM]])
    grad_out = jnp.concatenate([before[TOKEN_RIM:split], grad_out, after[TOKEN_RIM:split]])
    ids = jnp.concatenate([before[split, :, :LABEL_RIM].T, ids])
    return tokens, grad_out, ids


def lat_halo(tokens, grad_out, ids):
    token_rows, col_count, width = tokens.shape
    grad_rows = grad_out.shape[0]
    token_size, grad_size = token_rows * TOKEN_RIM, grad_rows * GRAD_RIM
    id_cols = jnp.pad(ids[:, col_count - LABEL_RIM :], ((0, 0), (0, width - LABEL_RIM)))

    def packed(token_part, grad_part, id_part):
        return jnp.concatenate(
            [token_part.reshape(token_size, width), grad_part.reshape(grad_size, width), id_part]
        )

    def unpacked(message):
        return (
            message[:token_size].reshape(token_rows, TOKEN_RIM, width),
            message[token_size : token_size + grad_size].reshape(grad_rows, GRAD_RIM, width),
            message[token_size + grad_size :, :LABEL_RIM],
        )

    to_next = packed(tokens[:, -TOKEN_RIM:], grad_out[:, -GRAD_RIM:], id_cols)
    to_prev = packed(tokens[:, :TOKEN_RIM], grad_out[:, :GRAD_RIM], jnp.zeros_like(id_cols))
    before, after = traded(to_next, to_prev, LAT)
    tokens_before, grad_before, ids_before = unpacked(before)
    tokens_after, grad_after, _ = unpacked(after)
    return (
        jnp.concatenate([tokens_before, tokens, tokens_after], axis=1),
        jnp.concatenate([grad_before, grad_out, grad_after], axis=1),
        jnp.concatenate([ids_before, ids], axis=1),
    )


def scattered_sum(partial, axes):
    count = lax.axis_size(axes)
    chunks = partial.reshape(count, partial.shape[0] // count, partial.shape[1])
    received = lax.all_to_all(chunks, axes, 0, 0, tiled=True)
    return jnp.sum(received.astype(jnp.float32), axis=0)


def gathered(chunk, axes):
    count = lax.axis_size(axes)
    copies = jnp.broadcast_to(chunk[None], (count,) + chunk.shape)
    return lax.all_to_all(copies, axes, 0, 0, tiled=True).reshape(-1, chunk.shape[1])


def total_over_devices(rows, grad_scale):
    own = scattered_sum(rows, NEAR).astype(jnp.bfloat16)
    own = scattered_sum(own, ("y",)).astype(jnp.bfloat16)
    count = lax.axis_size(DEEP)
    copies = jnp.broadcast_to(own[None], (count,) + own.shape)
    parts = lax.all_to_all(copies, DEEP, 0, 0, tiled=True)
    own = (jnp.sum(parts.astype(jnp.float32), axis=0) * grad_scale).astype(jnp.bfloat16)
    own = gathered(own, ("y",))
    return gathered(own, NEAR).astype(jnp.float32)


def from_blocks(rows, width):
    count = width // 128
    return rows.reshape(count, -1, 128).transpose(1, 0, 2).reshape(-1, width)


def lane_mean(values):
    return jnp.sum(values, axis=-1, keepdims=True) * (1.0 / 128.0)


def layer_norm(values, gain):
    centred = values - lane_mean(values)
    inverse = lax.rsqrt(lane_mean(centred * centred) + epsilon)
    normed = centred * inverse
    return (normed * gain).astype(jnp.bfloat16), normed, inverse


def layer_norm_back(grad_in, normed, inverse, gain):
    scaled = grad_in * gain
    return inverse * (scaled - lane_mean(scaled) - normed * lane_mean(scaled * normed))


def matmul(left, right):
    return jnp.dot(left, right, preferred_element_type=jnp.float32)


def matmul_nt(left, right):
    return lax.dot_general(left, right, (((1,), (1,)), ((), ())), preferred_element_type=jnp.float32)


def matmul_tn(left, right):
    return lax.dot_general(left, right, (((0,), (0,)), ((), ())), preferred_element_type=jnp.float32)


def by_heads(rows, head_masks):
    return jnp.concatenate([rows * mask for mask in head_masks], axis=0)


def own_heads(stacked, head_lanes):
    total = jnp.zeros((AREA, 128), jnp.float32)
    for head in range(HEADS):
        part = stacked[head * AREA : (head + 1) * AREA]
        total = total + jnp.where(head_lanes[head], part, 0.0)
    return total


def table_rows(bias_sum):
    lane = lax.broadcasted_iota(jnp.int32, (WIN, 128), 1)
    pieces = []
    for head in range(HEADS):
        half = head % 2
        tile = bias_sum[:, (head // 2) * 128 : (head // 2 + 1) * 128]
        tile_sum = jnp.zeros((WIN, 128), jnp.float32)
        for row in range(WIN):
            part = jnp.where(lane // AREA == half, tile[row * WIN : (row + 1) * WIN], 0.0)
            steps = (WIN * (WIN - 1 - row) - AREA * half) % 128
            tile_sum = tile_sum + (pltpu.roll(part, steps, 1) if steps else part)
        pieces.append(tile_sum)
    stacked = jnp.concatenate(pieces, axis=0)
    source = lax.broadcasted_iota(jnp.int32, (128, 256), 0)
    target = lax.broadcasted_iota(jnp.int32, (128, 256), 1)
    hit = jnp.logical_and(source // WIN == target // 16, source % WIN == target % 16)
    spread_to = jnp.where(hit, 1.0, 0.0).astype(jnp.bfloat16)
    spread = jnp.zeros((HEADS * WIN, 256), jnp.float32)
    rest = stacked
    for _ in range(3):
        part = rest.astype(jnp.bfloat16)
        spread = spread + matmul(part, spread_to)
        rest = rest - part.astype(jnp.float32)
    place = lax.broadcasted_iota(jnp.int32, (HEADS * WIN, 256), 0) % WIN
    table = jnp.zeros((HEADS * WIN, 256), jnp.float32)
    for row in range(WIN):
        part = jnp.where(place == row, spread, 0.0)
        table = table + (pltpu.roll(part, WIN - 1 - row, 1) if row < WIN - 1 else part)
    rows = []
    for head in range(HEADS):
        head_sum = jnp.sum(table[head * WIN : (head + 1) * WIN], axis=0, keepdims=True)
        rows.extend([head_sum[:, :128], head_sum[:, 128:]])
    return rows


def block_kernel(
    tokens_ref,
    gcat_ref,
    grad_own_ref,
    label_col_ref,
    label_row_ref,
    keep_ref,
    bias_ref,
    qkv_ref,
    proj_ref,
    up_ref,
    down_ref,
    conv_ref,
    conv_back_ref,
    gain_one_ref,
    gain_two_ref,
    down_out_ref,
    grad_tokens_ref,
    rows_ref,
    block_out_s,
    grad_tokens_s,
    ln_one_s,
    ln_two_s,
    hidden_s,
    grad_pre_s,
    grad_block_s,
    mixed_s,
    grad_att_s,
    grad_qkv_s,
):
    gain_one, gain_two = gain_one_ref[...], gain_two_ref[...]
    lane = lax.broadcasted_iota(jnp.int32, (AREA, 128), 1)
    head_lanes = [lane // HEAD_DIM == head for head in range(HEADS)]
    head_masks = [jnp.where(hit, 1.0, 0.0).astype(jnp.bfloat16) for hit in head_lanes]
    biases = bias_ref[...]
    score_scale = HEAD_DIM ** (-0.5)
    length = WIN_COLS * AREA
    bias_sum = jnp.zeros((AREA, HEADS * AREA), jnp.float32)
    gain_one_sum = jnp.zeros((1, 128), jnp.float32)
    gain_two_sum = jnp.zeros((1, 128), jnp.float32)
    for chunk in range(WIN_ROWS):
        start = chunk * length
        source = tokens_ref[start : start + length, :].astype(jnp.float32)
        ln_one, normed_one, inverse_one = layer_norm(source, gain_one)
        qkv_all = matmul(ln_one, qkv_ref[...]).astype(jnp.bfloat16)
        saved, mixed_parts = [], []
        for win in range(WIN_COLS):
            part = qkv_all[win * AREA : (win + 1) * AREA]
            query, key, value = part[:, :128], part[:, 128:256], part[:, 256:]
            query_heads = by_heads(query, head_masks)
            place = (chunk * WIN_COLS + win) * AREA
            column = label_col_ref[place : place + AREA, :].astype(jnp.float32)
            allowed = jnp.concatenate([column, column], axis=1) == label_row_ref[chunk * WIN_COLS + win]
            scores = matmul_nt(key, query_heads) * score_scale + biases
            scores = jnp.where(allowed, scores, -1e30)
            raised = jnp.exp(scores - jnp.max(scores, axis=0, keepdims=True))
            probabilities = raised * (1.0 / jnp.sum(raised, axis=0, keepdims=True))
            weights = probabilities.astype(jnp.bfloat16)
            mixed_parts.append(own_heads(matmul_tn(weights, value), head_lanes).astype(jnp.bfloat16))
            saved.append((query_heads, key, value, probabilities, weights))
        mixed = jnp.concatenate(mixed_parts, axis=0)
        projected = matmul(mixed, proj_ref[...]).astype(jnp.bfloat16)
        middle = source + projected.astype(jnp.float32)
        ln_two, normed_two, inverse_two = layer_norm(middle, gain_two)
        pre_act = matmul(ln_two, up_ref[...])
        cumulative = 0.5 * (1.0 + lax.erf(pre_act * 0.7071067811865476))
        hidden = (pre_act * cumulative).astype(jnp.bfloat16)
        slope = cumulative + pre_act * (jnp.exp(-0.5 * pre_act * pre_act) * 0.3989422804014327)
        block_out = (middle + matmul(hidden, down_ref[...])).astype(jnp.bfloat16).astype(jnp.float32)
        top = chunk * WIN
        for win in range(WIN_COLS):
            piece = block_out[win * AREA : (win + 1) * AREA].reshape(WIN, WIN, 128)
            block_out_s[top : top + WIN, win * WIN : (win + 1) * WIN, :] = piece

        grad_grid = jnp.zeros((WIN * PAD_COLS, 128), jnp.float32)
        for tap in range(3):
            first = (top + 2 - tap) * PAD_COLS
            grad_grid = grad_grid + matmul(
                gcat_ref[first : first + WIN * PAD_COLS, :], conv_back_ref[tap]
            )
        grad_grid = grad_grid.reshape(WIN, PAD_COLS, 128)
        grad_block = jnp.concatenate(
            [
                grad_grid[:, win * WIN : (win + 1) * WIN, :].reshape(AREA, 128)
                for win in range(WIN_COLS)
            ],
            axis=0,
        )
        grad_block_b = grad_block.astype(jnp.bfloat16)
        grad_hidden = matmul_nt(grad_block_b, down_ref[...])
        grad_pre = (grad_hidden * slope).astype(jnp.bfloat16)
        grad_ln_two = matmul_nt(grad_pre, up_ref[...])
        grad_middle = grad_block + layer_norm_back(grad_ln_two, normed_two, inverse_two, gain_two)
        grad_att = grad_middle.astype(jnp.bfloat16)
        grad_mixed = matmul_nt(grad_att, proj_ref[...]).astype(jnp.bfloat16)
        grad_parts = []
        for win in range(WIN_COLS):
            query_heads, key, value, probabilities, weights = saved[win]
            grad_heads = by_heads(grad_mixed[win * AREA : (win + 1) * AREA], head_masks)
            grad_probs = matmul_nt(value, grad_heads)
            grad_value = matmul(weights, grad_heads)
            centre = jnp.sum(probabilities * grad_probs, axis=0, keepdims=True)
            grad_scores = probabilities * (grad_probs - centre)
            if chunk and win:
                bias_sum = bias_sum + grad_scores
            grad_scores_b = grad_scores.astype(jnp.bfloat16)
            grad_key = matmul(grad_scores_b, query_heads) * score_scale
            grad_query = own_heads(matmul_tn(grad_scores_b, key), head_lanes) * score_scale
            grad_parts.append(
                jnp.concatenate([grad_query, grad_key, grad_value], axis=1).astype(jnp.bfloat16)
            )
        grad_qkv = jnp.concatenate(grad_parts, axis=0)
        grad_ln_one = matmul_nt(grad_qkv, qkv_ref[...])
        grad_tokens = grad_middle + layer_norm_back(grad_ln_one, normed_one, inverse_one, gain_one)
        for win in range(WIN_COLS):
            piece = grad_tokens[win * AREA : (win + 1) * AREA].reshape(WIN, WIN, 128)
            grad_tokens_s[top : top + WIN, win * WIN : (win + 1) * WIN, :] = piece
        if chunk:
            gain_one_sum = gain_one_sum + jnp.sum(
                (grad_ln_one * normed_one)[AREA:], axis=0, keepdims=True
            )
            gain_two_sum = gain_two_sum + jnp.sum(
                (grad_ln_two * normed_two)[AREA:], axis=0, keepdims=True
            )
            kept = slice((chunk - 1) * (length - AREA), chunk * (length - AREA))
            ln_one_s[kept, :] = ln_one[AREA:]
            ln_two_s[kept, :] = ln_two[AREA:]
            hidden_s[kept, :] = hidden[AREA:]
            grad_pre_s[kept, :] = grad_pre[AREA:]
            grad_block_s[kept, :] = grad_block_b[AREA:]
            mixed_s[kept, :] = mixed[AREA:]
            grad_att_s[kept, :] = grad_att[AREA:]
            grad_qkv_s[kept, :] = grad_qkv[AREA:]

    own_rows, own_cols = 16, 32
    shifted = []
    for tap in range(3):
        piece = block_out_s[3 : own_rows + 5, 3 + tap : 3 + tap + own_cols, :]
        if tap != 1:
            piece = piece * keep_ref[tap // 2][None]
        shifted.append(piece.reshape((own_rows + 2) * own_cols, 128).astype(jnp.bfloat16))
    patches = jnp.concatenate(shifted, axis=1)
    count = own_rows * own_cols
    downscaled = jnp.zeros((count, 128), jnp.float32)
    grad_own = grad_own_ref[...]
    for tap in range(3):
        rows = patches[tap * own_cols : tap * own_cols + count]
        downscaled = downscaled + matmul(rows, conv_ref[tap])
        rows_ref[tap * 384 : (tap + 1) * 384, :] = matmul_tn(rows, grad_own).astype(jnp.bfloat16)
    down_out_ref[...] = downscaled.astype(jnp.bfloat16)
    grad_tokens_ref[...] = (
        grad_tokens_s[4 : own_rows + 4, 4 : own_cols + 4, :].reshape(count, 128).astype(jnp.bfloat16)
    )
    place = 1152
    for left, right, flipped in (
        (ln_one_s, grad_qkv_s, False),
        (mixed_s, grad_att_s, False),
        (ln_two_s, grad_pre_s, False),
        (hidden_s, grad_block_s, True),
    ):
        product = matmul_tn(left[...], right[...]).astype(jnp.bfloat16)
        if flipped:
            rows_ref[place : place + product.shape[0], :] = product
            place = place + product.shape[0]
        else:
            for tile in range(product.shape[1] // 128):
                rows_ref[place : place + 128, :] = product[:, tile * 128 : (tile + 1) * 128]
                place = place + 128
    small = [gain_one_sum, gain_two_sum] + table_rows(bias_sum)
    small.append(jnp.zeros((16 - len(small), 128), jnp.float32))
    rows_ref[place : place + 16, :] = jnp.concatenate(small, axis=0).astype(jnp.bfloat16)
    place = place + 16
    rows_ref[place:, :] = jnp.zeros((ROWS - place, 128), jnp.bfloat16)


def bias_matrix(position_bias):
    places = jnp.arange(WIN, dtype=jnp.int32)
    distance = places[:, None] - places[None, :] + WIN - 1
    onehot = (distance[:, :, None] == jnp.arange(SPAN, dtype=jnp.int32)).astype(jnp.float32)
    spread = jnp.einsum(
        "hmn,acm,bdn->cdhab", position_bias, onehot, onehot, precision=lax.Precision.HIGHEST
    )
    return spread.reshape(AREA, HEADS * AREA)


def to_windows(grid):
    height, width = grid.shape[0] // WIN, grid.shape[1] // WIN
    split = grid.reshape((height, WIN, width, WIN) + grid.shape[2:])
    return split.swapaxes(1, 2).reshape((height * width, AREA) + grid.shape[2:])


def local_work(
    tokens_ext,
    grad_ext,
    grad_out,
    labels,
    positions,
    lat_total,
    qkv_weight,
    proj_weight,
    up_weight,
    down_weight,
    conv_weight,
    gain_one,
    gain_two,
    position_bias,
):
    row_count, col_count, width = tokens_ext.shape
    keep_before = (positions != 0).astype(jnp.float32)
    keep_after = (positions != lat_total - 1).astype(jnp.float32)
    own = slice(TOKEN_RIM, col_count - TOKEN_RIM)
    keep = jnp.stack([keep_before[own], keep_after[own]])
    keep = jnp.broadcast_to(keep[:, :, None], keep.shape + (width,))
    after = grad_ext[:, 2:] * keep_after.astype(jnp.bfloat16)[None, :, None]
    before = grad_ext[:, :-2] * keep_before.astype(jnp.bfloat16)[None, :, None]
    gcat = jnp.concatenate([after, grad_ext[:, 1:-1], before], axis=2)
    gcat = jnp.pad(gcat, ((0, 0), (0, PAD_COLS - col_count), (0, 0))).reshape(-1, 3 * width)
    tokens_win = to_windows(tokens_ext).reshape(-1, width)
    label_win = to_windows(labels)
    label_row = jnp.tile(label_win, (1, HEADS))[:, None, :]
    label_col = jnp.broadcast_to(
        label_win.astype(jnp.bfloat16).reshape(-1, 1), (row_count * col_count, width)
    )
    conv_fwd = conv_weight.reshape(3, 3 * width, width)
    conv_back = conv_weight.reshape(3, 3, width, width).swapaxes(2, 3).reshape(3, 3 * width, width)
    count = grad_out.shape[0] * grad_out.shape[1]
    kept = WIN * WIN * (WIN_ROWS - 1) * (WIN_COLS - 1)
    bf16 = lambda *shape: pltpu.VMEM(shape, jnp.bfloat16)
    grid_shape = (row_count, col_count, width)
    downscaled, grad_tokens, rows = pl.pallas_call(
        block_kernel,
        out_shape=(
            jax.ShapeDtypeStruct((count, width), jnp.bfloat16),
            jax.ShapeDtypeStruct((count, width), jnp.bfloat16),
            jax.ShapeDtypeStruct((ROWS, width), jnp.bfloat16),
        ),
        in_specs=[pl.BlockSpec(memory_space=pltpu.VMEM)] * 15,
        out_specs=[pl.BlockSpec(memory_space=pltpu.VMEM)] * 3,
        scratch_shapes=[
            pltpu.VMEM(grid_shape, jnp.float32),
            pltpu.VMEM(grid_shape, jnp.float32),
            bf16(kept, width),
            bf16(kept, width),
            bf16(kept, 4 * width),
            bf16(kept, 4 * width),
            bf16(kept, width),
            bf16(kept, width),
            bf16(kept, width),
            bf16(kept, 3 * width),
        ],
        compiler_params=pltpu.CompilerParams(vmem_limit_bytes=48 * 1024 * 1024),
        cost_estimate=pl.CostEstimate(
            flops=3_000_000_000, bytes_accessed=8_000_000, transcendentals=2_000_000
        ),
    )(
        tokens_win,
        gcat,
        grad_out.reshape(count, width),
        label_col,
        label_row,
        keep,
        bias_matrix(position_bias),
        qkv_weight,
        proj_weight,
        up_weight,
        down_weight,
        conv_fwd,
        conv_back,
        gain_one[None],
        gain_two[None],
    )
    return downscaled.reshape(grad_out.shape), grad_tokens.reshape(grad_out.shape), rows


def per_device(
    tokens,
    grad_out,
    window_ids,
    qkv_weight,
    proj_weight,
    up_weight,
    down_weight,
    conv_weight,
    gain_one,
    gain_two,
    position_bias,
):
    row_count, col_count, width = tokens.shape
    lat_total = col_count * lax.axis_size(LAT)
    tokens_all = row_count * lat_total * lax.axis_size(LON)
    ids = window_ids.astype(jnp.bfloat16)
    tokens_ext, grad_ext, ids_ext = lat_halo(*lon_halo(tokens, grad_out, ids))
    first_col = lax.axis_index(LAT) * col_count
    steps = jnp.arange(col_count + 2 * TOKEN_RIM, dtype=jnp.int32)
    positions = jnp.remainder(first_col + steps - TOKEN_RIM, lat_total)
    shifted_cols = jnp.remainder(first_col + steps - LABEL_RIM, lat_total)
    seam_flag = (shifted_cols >= lat_total - SHIFT).astype(jnp.float32)
    labels = ids_ext.astype(jnp.float32) * 2.0 + seam_flag[None, :]
    downscaled, grad_tokens, rows = local_work(
        tokens_ext,
        grad_ext,
        grad_out,
        labels,
        positions,
        lat_total,
        qkv_weight,
        proj_weight,
        up_weight,
        down_weight,
        conv_weight,
        gain_one,
        gain_two,
        position_bias,
    )
    totals = total_over_devices(rows, 1.0 / math.sqrt(tokens_all))
    sizes = (9 * width, 3 * width, width, 4 * width, 4 * width, 1, 1, 8)
    pieces = []
    offset = 0
    for size in sizes:
        pieces.append(totals[offset : offset + size])
        offset = offset + size
    return (
        downscaled,
        grad_tokens,
        from_blocks(pieces[1], 3 * width),
        pieces[2],
        from_blocks(pieces[3], 4 * width),
        pieces[4],
        pieces[0].reshape(9, width, width),
        pieces[5][0],
        pieces[6][0],
        pieces[7].reshape(HEADS, 16, 16)[:, :SPAN, :SPAN],
    )


def solution(mesh):
    lon_count, lat_count = mesh.devices.shape
    near = math.gcd(lon_count, 8)
    parts = (lon_count // near, near // 2, 2, 2, lat_count // 2)
    fine = Mesh(mesh.devices.reshape(parts), ("zl", "x", "c", "zh", "y"))
    grid = P(LON, LAT, None)
    return jax.shard_map(
        per_device,
        mesh=fine,
        in_specs=(grid, grid, P(LON, LAT)) + (P(),) * 8,
        out_specs=(grid, grid) + (P(),) * 8,
        check_vma=False,
    )
```

```python
import functools
import math

import jax
import jax.numpy as jnp
from jax import lax
from jax.experimental import pallas as pl
from jax.experimental.pallas import tpu as pltpu
from jax.sharding import Mesh
from jax.sharding import PartitionSpec as P

HEADS = 4
WIN = 8
SHIFT = 4
SPAN = 15
HEAD_DIM = 32
AREA = WIN * WIN
WIN_ROWS = 3
WIN_COLS = 5
PAD_COLS = 48
ROWS = 3072
TOKEN_RIM = 4
GRAD_RIM = 5
LABEL_RIM = 8

LON = ("zl", "x", "c")
LAT = ("zh", "y")
DEEP = ("zl", "zh")
TOKEN_ROWS = 24
GRAD_ROWS = 26
MESSAGE = (TOKEN_ROWS + GRAD_ROWS) * WIN + 32

epsilon = 1e-05


def swapped(value, axes, first):
    count = lax.axis_size(axes)
    pairs = []
    for source in range(count):
        up = (source % 2 == 0) == first
        pairs.append((source, (source + 1) % count if up else (source - 1) % count))
    return lax.ppermute(value, axes, pairs)


def place_along(axes):
    place = 0
    for axis in axes:
        place = place * lax.axis_size(axis) + lax.axis_index(axis)
    return place


def either(choice, first, second):
    return jnp.where(choice, jnp.int32(first), jnp.int32(second))


def lon_pack_kernel(tokens_ref, grad_ref, ids_ref, far_ref, near_ref, ids_s):
    even = place_along(LON) % 2 == 0
    rows = tokens_ref.shape[0]
    ids_s[...] = jnp.zeros_like(ids_s)
    ids_s[0:LABEL_RIM, 0 : ids_ref.shape[1]] = ids_ref[rows - LABEL_RIM :, :].astype(jnp.float32)
    ids = ids_s[...].astype(jnp.bfloat16)
    for ref, upper in ((near_ref, even), (far_ref, jnp.logical_not(even))):
        ref[0:TOKEN_RIM] = tokens_ref[pl.ds(either(upper, rows - TOKEN_RIM, 0), TOKEN_RIM)]
        ref[TOKEN_RIM : TOKEN_RIM + GRAD_RIM] = grad_ref[
            pl.ds(either(upper, rows - GRAD_RIM, 0), GRAD_RIM)
        ]
        ref[TOKEN_RIM + GRAD_RIM] = ids


def lon_labels(ids_ref, lon_near_ref, lon_far_ref, even, ids_s):
    row = TOKEN_RIM + GRAD_RIM
    before = jnp.where(
        even, lon_far_ref[row].astype(jnp.float32), lon_near_ref[row].astype(jnp.float32)
    )
    ids_s[...] = jnp.zeros_like(ids_s)
    ids_s[0:LABEL_RIM, :] = before[0:LABEL_RIM]
    ids_s[LABEL_RIM : LABEL_RIM + ids_ref.shape[0], 0 : ids_ref.shape[1]] = ids_ref[...].astype(
        jnp.float32
    )


def lat_pack_kernel(
    tokens_ref,
    grad_ref,
    ids_ref,
    lon_near_ref,
    lon_far_ref,
    far_ref,
    near_ref,
    tokens_s,
    grad_s,
    ids_s,
):
    lon_even = place_along(LON) % 2 == 0
    lat_even = place_along(LAT) % 2 == 0
    cols = tokens_ref.shape[1]

    def edges(scratch, row, values):
        values = values.astype(jnp.float32)
        count = values.shape[0]
        scratch[0, pl.ds(row, count)] = values[:, 0:WIN]
        scratch[1, pl.ds(row, count)] = values[:, cols - WIN :]

    edges(tokens_s, TOKEN_RIM, tokens_ref[...])
    edges(grad_s, GRAD_RIM, grad_ref[...])
    split = TOKEN_RIM + GRAD_RIM
    for ref, below in ((lon_near_ref, lon_even), (lon_far_ref, jnp.logical_not(lon_even))):
        edges(tokens_s, either(below, TOKEN_ROWS - TOKEN_RIM, 0), ref[0:TOKEN_RIM])
        edges(grad_s, either(below, GRAD_ROWS - GRAD_RIM, 0), ref[TOKEN_RIM:split])
    lon_labels(ids_ref, lon_near_ref, lon_far_ref, lon_even, ids_s)
    ids = ids_s[...].astype(jnp.bfloat16)
    first, second = TOKEN_ROWS * WIN, (TOKEN_ROWS + GRAD_ROWS) * WIN
    for ref, side in ((near_ref, either(lat_even, 1, 0)), (far_ref, either(lat_even, 0, 1))):
        ref[0:first, :] = tokens_s[side].reshape(first, 128).astype(jnp.bfloat16)
        ref[first:second, :] = grad_s[side].reshape(second - first, 128).astype(jnp.bfloat16)
        ref[second:, :] = ids


def assembled(
    tokens_ref,
    grad_ref,
    ids_ref,
    lon_near_ref,
    lon_far_ref,
    lat_near_ref,
    lat_far_ref,
    tokens_s,
    grad_s,
    ids_s,
    first_col,
    lat_total,
):
    lon_even = place_along(LON) % 2 == 0
    lat_even = place_along(LAT) % 2 == 0
    rows, cols = tokens_ref.shape[0], tokens_ref.shape[1]
    middle = slice(WIN, WIN + cols)
    tokens_s[TOKEN_RIM : TOKEN_RIM + rows, middle, :] = tokens_ref[...].astype(jnp.float32)
    grad_s[GRAD_RIM : GRAD_RIM + rows, middle, :] = grad_ref[...].astype(jnp.float32)
    split = TOKEN_RIM + GRAD_RIM
    for ref, below in ((lon_near_ref, lon_even), (lon_far_ref, jnp.logical_not(lon_even))):
        row = either(below, TOKEN_ROWS - TOKEN_RIM, 0)
        tokens_s[pl.ds(row, TOKEN_RIM), middle, :] = ref[0:TOKEN_RIM].astype(jnp.float32)
        row = either(below, GRAD_ROWS - GRAD_RIM, 0)
        grad_s[pl.ds(row, GRAD_RIM), middle, :] = ref[TOKEN_RIM:split].astype(jnp.float32)
    first, second = TOKEN_ROWS * WIN, (TOKEN_ROWS + GRAD_ROWS) * WIN
    for ref, below in ((lat_near_ref, lat_even), (lat_far_ref, jnp.logical_not(lat_even))):
        side = pl.ds(pl.multiple_of(either(below, WIN + cols, 0), WIN), WIN)
        tokens_s[:, side, :] = ref[0:first].astype(jnp.float32).reshape(TOKEN_ROWS, WIN, 128)
        grad_s[:, side, :] = ref[first:second].astype(jnp.float32).reshape(GRAD_ROWS, WIN, 128)
    lon_labels(ids_ref, lon_near_ref, lon_far_ref, lon_even, ids_s)
    before = jnp.where(
        lat_even, lat_far_ref[second:].astype(jnp.float32), lat_near_ref[second:].astype(jnp.float32)
    )
    lane = lax.broadcasted_iota(jnp.int32, ids_s.shape, 1)
    own = pltpu.roll(ids_s[...], LABEL_RIM, 1)
    ids = jnp.where(lane < LABEL_RIM, pltpu.roll(before, 128 - (cols - LABEL_RIM), 1), own)
    shifted = first_col + lane - LABEL_RIM
    shifted = jnp.where(shifted < 0, shifted + lat_total, shifted)
    return ids * 2.0 + jnp.where(shifted >= lat_total - SHIFT, 1.0, 0.0)


def bias_rows(table_ref):
    lane = lax.broadcasted_iota(jnp.int32, (WIN, 128), 1)
    source = lax.broadcasted_iota(jnp.int32, (256, 128), 0)
    target = lax.broadcasted_iota(jnp.int32, (256, 128), 1)
    hit = jnp.logical_and(source // 16 == target // WIN, source % 16 == target % WIN)
    narrow = jnp.where(hit, 1.0, 0.0).astype(jnp.bfloat16)
    pieces = []
    for head in range(HEADS):
        table = jnp.broadcast_to(table_ref[head : head + 1, :], (WIN, 256))
        place = lax.broadcasted_iota(jnp.int32, (WIN, 256), 0)
        moved = jnp.zeros((WIN, 256), jnp.float32)
        for row in range(WIN):
            steps = (256 - (WIN - 1 - row)) % 256
            part = pltpu.roll(table, steps, 1) if steps else table
            moved = jnp.where(place == row, part, moved)
        pieces.append(moved)
    rest = jnp.concatenate(pieces, axis=0)
    packed = jnp.zeros((HEADS * WIN, 128), jnp.float32)
    for _ in range(3):
        part = rest.astype(jnp.bfloat16)
        packed = packed + matmul(part, narrow)
        rest = rest - part.astype(jnp.float32)
    rows = []
    for row in range(WIN):
        tiles = []
        for pair in range(HEADS // 2):
            halves = []
            for half in range(2):
                head = 2 * pair + half
                steps = (AREA * half - WIN * (WIN - 1 - row)) % 128
                part = packed[head * WIN : (head + 1) * WIN]
                halves.append(pltpu.roll(part, steps, 1) if steps else part)
            tiles.append(jnp.where(lane < AREA, halves[0], halves[1]))
        rows.append(jnp.concatenate(tiles, axis=1))
    return jnp.concatenate(rows, axis=0)


def scattered_sum(partial, axes):
    count = lax.axis_size(axes)
    chunks = partial.reshape(count, partial.shape[0] // count, partial.shape[1])
    received = lax.all_to_all(chunks, axes, 0, 0, tiled=True)
    return jnp.sum(received.astype(jnp.float32), axis=0)


def spread(chunk, axes):
    count = lax.axis_size(axes)
    copies = jnp.broadcast_to(chunk[None], (count,) + chunk.shape)
    return lax.all_to_all(copies, axes, 0, 0, tiled=True)


def total_over_devices(kept, sent, grad_scale):
    cores = [(0, 1), (1, 0)]
    other = lax.ppermute(sent, "c", cores)
    own = (kept.astype(jnp.float32) + other.astype(jnp.float32)).astype(jnp.bfloat16)
    own = scattered_sum(own, ("x",)).astype(jnp.bfloat16)
    own = scattered_sum(own, ("y",)).astype(jnp.bfloat16)
    parts = spread(own, DEEP)
    own = (jnp.sum(parts.astype(jnp.float32), axis=0) * grad_scale).astype(jnp.bfloat16)
    own = spread(own, ("y",)).reshape(-1, 128)
    own = spread(own, ("x",)).reshape(-1, 128)
    return own, lax.ppermute(own, "c", cores)


def unpack_kernel(
    own_ref,
    other_ref,
    qkv_ref,
    proj_ref,
    up_ref,
    down_ref,
    conv_ref,
    gain_one_ref,
    gain_two_ref,
    table_ref,
    rows_s,
):
    core = lax.axis_index("c")
    half = ROWS // 2
    rows_s[pl.ds(pl.multiple_of(core * half, half), half), :] = own_ref[...]
    rows_s[pl.ds(pl.multiple_of((1 - core) * half, half), half), :] = other_ref[...]

    def piece(first, count):
        return rows_s[first : first + count, :].astype(jnp.float32)

    conv_ref[...] = piece(0, 1152).reshape(9, 128, 128)
    place = 1152
    for ref, tiles in ((qkv_ref, 3), (proj_ref, 1), (up_ref, 4)):
        for tile in range(tiles):
            ref[:, tile * 128 : (tile + 1) * 128] = piece(place, 128)
            place = place + 128
    down_ref[...] = piece(place, 512)
    small = piece(place + 512, 16)
    gain_one_ref[...] = small[0:1]
    gain_two_ref[...] = small[1:2]
    for low in range(WIN):
        moved = pltpu.roll(small, (128 - 16 * low) % 128, 1) if low else small
        for head in range(HEADS):
            for high in range(2):
                row = high * WIN + low
                if row < SPAN:
                    line = 2 + 2 * head + high
                    table_ref[head, row : row + 1, :] = moved[line : line + 1, :SPAN]


def lane_mean(values):
    return jnp.sum(values, axis=-1, keepdims=True) * (1.0 / 128.0)


def layer_norm(values, gain):
    centred = values - lane_mean(values)
    inverse = lax.rsqrt(lane_mean(centred * centred) + epsilon)
    normed = centred * inverse
    return (normed * gain).astype(jnp.bfloat16), normed, inverse


def layer_norm_back(grad_in, normed, inverse, gain):
    scaled = grad_in * gain
    return inverse * (scaled - lane_mean(scaled) - normed * lane_mean(scaled * normed))


def matmul(left, right):
    return jnp.dot(left, right, preferred_element_type=jnp.float32)


def matmul_nt(left, right):
    return lax.dot_general(left, right, (((1,), (1,)), ((), ())), preferred_element_type=jnp.float32)


def matmul_tn(left, right):
    return lax.dot_general(left, right, (((0,), (0,)), ((), ())), preferred_element_type=jnp.float32)


def by_heads(rows, head_masks):
    return jnp.concatenate([rows * mask for mask in head_masks], axis=0)


def own_heads(stacked, head_lanes):
    total = jnp.zeros((AREA, 128), jnp.float32)
    for head in range(HEADS):
        part = stacked[head * AREA : (head + 1) * AREA]
        total = total + jnp.where(head_lanes[head], part, 0.0)
    return total


def table_rows(bias_sum):
    lane = lax.broadcasted_iota(jnp.int32, (WIN, 128), 1)
    pieces = []
    for head in range(HEADS):
        half = head % 2
        tile = bias_sum[:, (head // 2) * 128 : (head // 2 + 1) * 128]
        tile_sum = jnp.zeros((WIN, 128), jnp.float32)
        for row in range(WIN):
            part = jnp.where(lane // AREA == half, tile[row * WIN : (row + 1) * WIN], 0.0)
            steps = (WIN * (WIN - 1 - row) - AREA * half) % 128
            tile_sum = tile_sum + (pltpu.roll(part, steps, 1) if steps else part)
        pieces.append(tile_sum)
    stacked = jnp.concatenate(pieces, axis=0)
    source = lax.broadcasted_iota(jnp.int32, (128, 256), 0)
    target = lax.broadcasted_iota(jnp.int32, (128, 256), 1)
    hit = jnp.logical_and(source // WIN == target // 16, source % WIN == target % 16)
    spread_to = jnp.where(hit, 1.0, 0.0).astype(jnp.bfloat16)
    spread = jnp.zeros((HEADS * WIN, 256), jnp.float32)
    rest = stacked
    for _ in range(3):
        part = rest.astype(jnp.bfloat16)
        spread = spread + matmul(part, spread_to)
        rest = rest - part.astype(jnp.float32)
    place = lax.broadcasted_iota(jnp.int32, (HEADS * WIN, 256), 0) % WIN
    table = jnp.zeros((HEADS * WIN, 256), jnp.float32)
    for row in range(WIN):
        part = jnp.where(place == row, spread, 0.0)
        table = table + (pltpu.roll(part, WIN - 1 - row, 1) if row < WIN - 1 else part)
    rows = []
    for head in range(HEADS):
        head_sum = jnp.sum(table[head * WIN : (head + 1) * WIN], axis=0, keepdims=True)
        rows.extend([head_sum[:, :128], head_sum[:, 128:]])
    return rows


def block_kernel(
    lat_total,
    tokens_ref,
    grad_ref,
    ids_ref,
    lon_near_ref,
    lon_far_ref,
    lat_near_ref,
    lat_far_ref,
    table_ref,
    qkv_ref,
    proj_ref,
    up_ref,
    down_ref,
    conv_ref,
    gain_one_ref,
    gain_two_ref,
    down_out_ref,
    grad_tokens_ref,
    kept_ref,
    sent_ref,
    tokens_s,
    grad_s,
    ids_s,
    gcat_s,
    rows_s,
    block_out_s,
    grad_tokens_s,
    ln_one_s,
    ln_two_s,
    hidden_s,
    grad_pre_s,
    grad_block_s,
    mixed_s,
    grad_att_s,
    grad_qkv_s,
):
    own_rows, own_cols = tokens_ref.shape[0], tokens_ref.shape[1]
    first_col = place_along(LAT) * own_cols
    labels = assembled(
        tokens_ref,
        grad_ref,
        ids_ref,
        lon_near_ref,
        lon_far_ref,
        lat_near_ref,
        lat_far_ref,
        tokens_s,
        grad_s,
        ids_s,
        first_col,
        lat_total,
    )
    ids_s[...] = labels
    position = first_col - TOKEN_RIM + lax.broadcasted_iota(jnp.int32, (PAD_COLS, 128), 0)
    position = jnp.where(position < 0, position + lat_total, position)
    position = jnp.where(position >= lat_total, position - lat_total, position)
    keep_after = jnp.where(position != lat_total - 1, 1.0, 0.0)
    keep_before = jnp.where(position != 0, 1.0, 0.0)
    for tap, keep in ((0, keep_after), (1, None), (2, keep_before)):
        piece = grad_s[:, 5 - tap : 5 - tap + PAD_COLS, :]
        if keep is not None:
            piece = piece * keep[None]
        gcat_s[:, tap * 128 : (tap + 1) * 128] = piece.reshape(GRAD_ROWS * PAD_COLS, 128).astype(
            jnp.bfloat16
        )
    lane_row = lax.broadcasted_iota(jnp.int32, (AREA, 128), 0)
    diagonal = (
        lax.broadcasted_iota(jnp.int32, (AREA, HEADS * AREA), 1) % AREA
        == lax.broadcasted_iota(jnp.int32, (AREA, HEADS * AREA), 0)
    )
    gain_one, gain_two = gain_one_ref[...], gain_two_ref[...]
    lane = lax.broadcasted_iota(jnp.int32, (AREA, 128), 1)
    head_lanes = [lane // HEAD_DIM == head for head in range(HEADS)]
    head_masks = [jnp.where(hit, 1.0, 0.0).astype(jnp.bfloat16) for hit in head_lanes]
    biases = bias_rows(table_ref)
    score_scale = HEAD_DIM ** (-0.5)
    length = WIN_COLS * AREA
    bias_sum = jnp.zeros((AREA, HEADS * AREA), jnp.float32)
    gain_one_sum = jnp.zeros((1, 128), jnp.float32)
    gain_two_sum = jnp.zeros((1, 128), jnp.float32)
    for chunk in range(WIN_ROWS):
        top = chunk * WIN
        source = jnp.concatenate(
            [
                tokens_s[top : top + WIN, 4 + win * WIN : 12 + win * WIN, :].reshape(AREA, 128)
                for win in range(WIN_COLS)
            ],
            axis=0,
        )
        label_rows = jnp.concatenate(
            [
                jnp.broadcast_to(ids_s[top + row : top + row + 1, :], (WIN, 128))
                for row in range(WIN)
            ],
            axis=0,
        )
        ln_one, normed_one, inverse_one = layer_norm(source, gain_one)
        qkv_all = matmul(ln_one, qkv_ref[...]).astype(jnp.bfloat16)
        saved, mixed_parts = [], []
        for win in range(WIN_COLS):
            part = qkv_all[win * AREA : (win + 1) * AREA]
            query, key, value = part[:, :128], part[:, 128:256], part[:, 256:]
            query_heads = by_heads(query, head_masks)
            picked = jnp.where(lane == win * WIN + lane_row % WIN, label_rows, 0.0)
            column = jnp.broadcast_to(
                jnp.sum(picked, axis=1, keepdims=True), (AREA, HEADS * AREA)
            )
            across = jnp.sum(jnp.where(diagonal, column, 0.0), axis=0, keepdims=True)
            allowed = column == across
            scores = matmul_nt(key, query_heads) * score_scale + biases
            scores = jnp.where(allowed, scores, -1e30)
            raised = jnp.exp(scores - jnp.max(scores, axis=0, keepdims=True))
            probabilities = raised * (1.0 / jnp.sum(raised, axis=0, keepdims=True))
            weights = probabilities.astype(jnp.bfloat16)
            mixed_parts.append(own_heads(matmul_tn(weights, value), head_lanes).astype(jnp.bfloat16))
            saved.append((query_heads, key, value, probabilities, weights))
        mixed = jnp.concatenate(mixed_parts, axis=0)
        projected = matmul(mixed, proj_ref[...]).astype(jnp.bfloat16)
        middle = source + projected.astype(jnp.float32)
        ln_two, normed_two, inverse_two = layer_norm(middle, gain_two)
        pre_act = matmul(ln_two, up_ref[...])
        cumulative = 0.5 * (1.0 + lax.erf(pre_act * 0.7071067811865476))
        hidden = (pre_act * cumulative).astype(jnp.bfloat16)
        slope = cumulative + pre_act * (jnp.exp(-0.5 * pre_act * pre_act) * 0.3989422804014327)
        block_out = (middle + matmul(hidden, down_ref[...])).astype(jnp.bfloat16).astype(jnp.float32)
        for win in range(WIN_COLS):
            piece = block_out[win * AREA : (win + 1) * AREA].reshape(WIN, WIN, 128)
            block_out_s[top : top + WIN, win * WIN : (win + 1) * WIN, :] = piece

        grad_grid = jnp.zeros((WIN * PAD_COLS, 128), jnp.float32)
        for tap in range(3):
            first = (top + 2 - tap) * PAD_COLS
            taps = jnp.concatenate([conv_ref[3 * tap + side] for side in range(3)], axis=1)
            grad_grid = grad_grid + matmul_nt(gcat_s[first : first + WIN * PAD_COLS, :], taps)
        grad_grid = grad_grid.reshape(WIN, PAD_COLS, 128)
        grad_block = jnp.concatenate(
            [
                grad_grid[:, win * WIN : (win + 1) * WIN, :].reshape(AREA, 128)
                for win in range(WIN_COLS)
            ],
            axis=0,
        )
        grad_block_b = grad_block.astype(jnp.bfloat16)
        grad_hidden = matmul_nt(grad_block_b, down_ref[...])
        grad_pre = (grad_hidden * slope).astype(jnp.bfloat16)
        grad_ln_two = matmul_nt(grad_pre, up_ref[...])
        grad_middle = grad_block + layer_norm_back(grad_ln_two, normed_two, inverse_two, gain_two)
        grad_att = grad_middle.astype(jnp.bfloat16)
        grad_mixed = matmul_nt(grad_att, proj_ref[...]).astype(jnp.bfloat16)
        grad_parts = []
        for win in range(WIN_COLS):
            query_heads, key, value, probabilities, weights = saved[win]
            grad_heads = by_heads(grad_mixed[win * AREA : (win + 1) * AREA], head_masks)
            grad_probs = matmul_nt(value, grad_heads)
            grad_value = matmul(weights, grad_heads)
            centre = jnp.sum(probabilities * grad_probs, axis=0, keepdims=True)
            grad_scores = probabilities * (grad_probs - centre)
            if chunk and win:
                bias_sum = bias_sum + grad_scores
            grad_scores_b = grad_scores.astype(jnp.bfloat16)
            grad_key = matmul(grad_scores_b, query_heads) * score_scale
            grad_query = own_heads(matmul_tn(grad_scores_b, key), head_lanes) * score_scale
            grad_parts.append(
                jnp.concatenate([grad_query, grad_key, grad_value], axis=1).astype(jnp.bfloat16)
            )
        grad_qkv = jnp.concatenate(grad_parts, axis=0)
        grad_ln_one = matmul_nt(grad_qkv, qkv_ref[...])
        grad_tokens = grad_middle + layer_norm_back(grad_ln_one, normed_one, inverse_one, gain_one)
        for win in range(WIN_COLS):
            piece = grad_tokens[win * AREA : (win + 1) * AREA].reshape(WIN, WIN, 128)
            grad_tokens_s[top : top + WIN, win * WIN : (win + 1) * WIN, :] = piece
        if chunk:
            gain_one_sum = gain_one_sum + jnp.sum(
                (grad_ln_one * normed_one)[AREA:], axis=0, keepdims=True
            )
            gain_two_sum = gain_two_sum + jnp.sum(
                (grad_ln_two * normed_two)[AREA:], axis=0, keepdims=True
            )
            kept = slice((chunk - 1) * (length - AREA), chunk * (length - AREA))
            ln_one_s[kept, :] = ln_one[AREA:]
            ln_two_s[kept, :] = ln_two[AREA:]
            hidden_s[kept, :] = hidden[AREA:]
            grad_pre_s[kept, :] = grad_pre[AREA:]
            grad_block_s[kept, :] = grad_block_b[AREA:]
            mixed_s[kept, :] = mixed[AREA:]
            grad_att_s[kept, :] = grad_att[AREA:]
            grad_qkv_s[kept, :] = grad_qkv[AREA:]

    col = first_col + lax.broadcasted_iota(jnp.int32, (own_cols, 128), 0)
    keeps = (col != 0, None, col != lat_total - 1)
    shifted = []
    for tap in range(3):
        piece = block_out_s[3 : own_rows + 5, 3 + tap : 3 + tap + own_cols, :]
        if keeps[tap] is not None:
            piece = piece * jnp.where(keeps[tap], 1.0, 0.0)[None]
        shifted.append(piece.reshape((own_rows + 2) * own_cols, 128).astype(jnp.bfloat16))
    patches = jnp.concatenate(shifted, axis=1)
    count = own_rows * own_cols
    downscaled = jnp.zeros((count, 128), jnp.float32)
    grad_own = grad_ref[...].reshape(count, 128)
    for tap in range(3):
        rows = patches[tap * own_cols : tap * own_cols + count]
        downscaled = downscaled + matmul(rows, conv_ref[3 * tap : 3 * tap + 3].reshape(384, 128))
        rows_s[tap * 384 : (tap + 1) * 384, :] = matmul_tn(rows, grad_own).astype(jnp.bfloat16)
    down_out_ref[...] = downscaled.astype(jnp.bfloat16).reshape(own_rows, own_cols, 128)
    grad_tokens_ref[...] = (
        grad_tokens_s[4 : own_rows + 4, 4 : own_cols + 4, :].astype(jnp.bfloat16)
    )
    place = 1152
    for left, right, flipped in (
        (ln_one_s, grad_qkv_s, False),
        (mixed_s, grad_att_s, False),
        (ln_two_s, grad_pre_s, False),
        (hidden_s, grad_block_s, True),
    ):
        product = matmul_tn(left[...], right[...]).astype(jnp.bfloat16)
        if flipped:
            rows_s[place : place + product.shape[0], :] = product
            place = place + product.shape[0]
        else:
            for tile in range(product.shape[1] // 128):
                rows_s[place : place + 128, :] = product[:, tile * 128 : (tile + 1) * 128]
                place = place + 128
    small = [gain_one_sum, gain_two_sum] + table_rows(bias_sum)
    small.append(jnp.zeros((16 - len(small), 128), jnp.float32))
    rows_s[place : place + 16, :] = jnp.concatenate(small, axis=0).astype(jnp.bfloat16)
    place = place + 16
    rows_s[place:, :] = jnp.zeros((ROWS - place, 128), jnp.bfloat16)
    core = lax.axis_index("c")
    half = ROWS // 2
    kept_ref[...] = rows_s[pl.ds(pl.multiple_of(core * half, half), half), :]
    sent_ref[...] = rows_s[pl.ds(pl.multiple_of((1 - core) * half, half), half), :]


def per_device(
    tokens,
    grad_out,
    window_ids,
    qkv_weight,
    proj_weight,
    up_weight,
    down_weight,
    conv_weight,
    gain_one,
    gain_two,
    position_bias,
):
    row_count, col_count, width = tokens.shape
    lat_total = col_count * lax.axis_size(LAT)
    tokens_all = row_count * lat_total * lax.axis_size(LON)
    vmem = pl.BlockSpec(memory_space=pltpu.VMEM)
    params = pltpu.CompilerParams(vmem_limit_bytes=48 * 1024 * 1024)
    bf16 = lambda *shape: jax.ShapeDtypeStruct(shape, jnp.bfloat16)
    f32 = lambda *shape: jax.ShapeDtypeStruct(shape, jnp.float32)
    held = lambda *shape: pltpu.VMEM(shape, jnp.bfloat16)
    wide = lambda *shape: pltpu.VMEM(shape, jnp.float32)
    table = jnp.pad(position_bias, ((0, 0), (0, 1), (0, 1))).reshape(HEADS, 256)
    slabs = TOKEN_RIM + GRAD_RIM + 1
    far, near = pl.pallas_call(
        lon_pack_kernel,
        out_shape=(bf16(slabs, col_count, width),) * 2,
        in_specs=[vmem] * 3,
        out_specs=(vmem,) * 2,
        scratch_shapes=[wide(col_count, width)],
        compiler_params=params,
    )(tokens, grad_out, window_ids)
    lon_far = swapped(far, LON, False)
    lon_near = swapped(near, LON, True)
    far, near = pl.pallas_call(
        lat_pack_kernel,
        out_shape=(bf16(MESSAGE, width),) * 2,
        in_specs=[vmem] * 5,
        out_specs=(vmem,) * 2,
        scratch_shapes=[
            wide(2, TOKEN_ROWS, WIN, width),
            wide(2, GRAD_ROWS, WIN, width),
            wide(32, width),
        ],
        compiler_params=params,
    )(tokens, grad_out, window_ids, lon_near, lon_far)
    lat_far = swapped(far, LAT, False)
    lat_near = swapped(near, LAT, True)
    count = AREA * (WIN_ROWS - 1) * (WIN_COLS - 1)
    downscaled, grad_tokens, kept, sent = pl.pallas_call(
        functools.partial(block_kernel, lat_total),
        out_shape=(
            bf16(*tokens.shape),
            bf16(*tokens.shape),
            bf16(ROWS // 2, width),
            bf16(ROWS // 2, width),
        ),
        in_specs=[vmem] * 15,
        out_specs=(vmem,) * 4,
        scratch_shapes=[
            wide(TOKEN_ROWS, 48, width),
            wide(GRAD_ROWS, 56, width),
            wide(32, width),
            held(GRAD_ROWS * PAD_COLS, 3 * width),
            held(ROWS, width),
            wide(TOKEN_ROWS, 40, width),
            wide(TOKEN_ROWS, 40, width),
            held(count, width),
            held(count, width),
            held(count, 4 * width),
            held(count, 4 * width),
            held(count, width),
            held(count, width),
            held(count, width),
            held(count, 3 * width),
        ],
        compiler_params=params,
        cost_estimate=pl.CostEstimate(
            flops=3_000_000_000, bytes_accessed=8_000_000, transcendentals=2_000_000
        ),
    )(
        tokens,
        grad_out,
        window_ids,
        lon_near,
        lon_far,
        lat_near,
        lat_far,
        table,
        qkv_weight,
        proj_weight,
        up_weight,
        down_weight,
        conv_weight,
        gain_one[None],
        gain_two[None],
    )
    own, other = total_over_devices(kept, sent, 1.0 / math.sqrt(tokens_all))
    results = pl.pallas_call(
        unpack_kernel,
        out_shape=(
            f32(width, 3 * width),
            f32(width, width),
            f32(width, 4 * width),
            f32(4 * width, width),
            f32(9, width, width),
            f32(1, width),
            f32(1, width),
            f32(HEADS, SPAN, SPAN),
        ),
        in_specs=[vmem] * 2,
        out_specs=(vmem,) * 8,
        scratch_shapes=[held(ROWS, width)],
        compiler_params=params,
    )(own, other)
    return (downscaled, grad_tokens) + results[:5] + (results[5][0], results[6][0], results[7])


def solution(mesh):
    lon_count, lat_count = mesh.devices.shape
    near = math.gcd(lon_count, 8)
    parts = (lon_count // near, near // 2, 2, 2, lat_count // 2)
    fine = Mesh(mesh.devices.reshape(parts), ("zl", "x", "c", "zh", "y"))
    grid = P(LON, LAT, None)
    return jax.shard_map(
        per_device,
        mesh=fine,
        in_specs=(grid, grid, P(LON, LAT)) + (P(),) * 8,
        out_specs=(grid, grid) + (P(),) * 8,
        check_vma=False,
    )
```

```python
import functools
import math

import jax
import jax.numpy as jnp
from jax import lax
from jax.experimental import pallas as pl
from jax.experimental.pallas import tpu as pltpu
from jax.sharding import Mesh
from jax.sharding import PartitionSpec as P

HEADS = 4
WIN = 8
SHIFT = 4
SPAN = 15
HEAD_DIM = 32
AREA = WIN * WIN
WIN_ROWS = 3
WIN_COLS = 5
PAD_COLS = 48
ROWS = 3072
TOKEN_RIM = 4
GRAD_RIM = 5
LABEL_RIM = 8

LON = ("zl", "x", "c")
LAT = ("zh", "y")
DEEP = ("zl", "zh")
TOKEN_ROWS = 24
GRAD_ROWS = 26
TOKEN_PART = TOKEN_ROWS * TOKEN_RIM
ID_PLACE = 232
MESSAGE = 240

epsilon = 1e-05


def swapped(value, axes, first):
    count = lax.axis_size(axes)
    pairs = []
    for source in range(count):
        up = (source % 2 == 0) == first
        pairs.append((source, (source + 1) % count if up else (source - 1) % count))
    return lax.ppermute(value, axes, pairs)


def place_along(axes):
    place = 0
    for axis in axes:
        place = place * lax.axis_size(axis) + lax.axis_index(axis)
    return place


def either(choice, first, second):
    return jnp.where(choice, jnp.int32(first), jnp.int32(second))


def fetched(pairs, sems):
    copies = [
        pltpu.make_async_copy(source, target, sems.at[place])
        for place, (source, target) in enumerate(pairs)
    ]
    for copy in copies:
        copy.start()
    return copies


def lon_pack_kernel(
    tokens_hbm, grad_hbm, ids_hbm, far_ref, near_ref, tokens_ref, grad_ref, ids_ref, ids_s, sems
):
    copies = fetched(
        ((tokens_hbm, tokens_ref), (grad_hbm, grad_ref), (ids_hbm, ids_ref)), sems
    )
    even = place_along(LON) % 2 == 0
    rows = tokens_ref.shape[0]
    ids_s[...] = jnp.zeros_like(ids_s)
    for copy in copies:
        copy.wait()
    ids_s[0:LABEL_RIM, 0 : ids_ref.shape[1]] = ids_ref[rows - LABEL_RIM :, :].astype(jnp.float32)
    ids = ids_s[...].astype(jnp.bfloat16)
    for ref, upper in ((near_ref, even), (far_ref, jnp.logical_not(even))):
        ref[0:TOKEN_RIM] = tokens_ref[pl.ds(either(upper, rows - TOKEN_RIM, 0), TOKEN_RIM)]
        ref[TOKEN_RIM : TOKEN_RIM + GRAD_RIM] = grad_ref[
            pl.ds(either(upper, rows - GRAD_RIM, 0), GRAD_RIM)
        ]
        ref[TOKEN_RIM + GRAD_RIM] = ids


def lon_labels(ids_ref, lon_near_ref, lon_far_ref, even, ids_s):
    row = TOKEN_RIM + GRAD_RIM
    before = jnp.where(
        even, lon_far_ref[row].astype(jnp.float32), lon_near_ref[row].astype(jnp.float32)
    )
    ids_s[...] = jnp.zeros_like(ids_s)
    ids_s[0:LABEL_RIM, :] = before[0:LABEL_RIM]
    ids_s[LABEL_RIM : LABEL_RIM + ids_ref.shape[0], 0 : ids_ref.shape[1]] = ids_ref[...].astype(
        jnp.float32
    )


def lat_pack_kernel(
    tokens_ref,
    grad_ref,
    ids_ref,
    lon_far_ref,
    lon_near_ref,
    far_ref,
    near_ref,
    tokens_s,
    grad_s,
    ids_s,
    message_s,
):
    lon_even = place_along(LON) % 2 == 0
    lat_even = place_along(LAT) % 2 == 0
    cols = tokens_ref.shape[1]

    def edges(scratch, row, values):
        values = values.astype(jnp.float32)
        count = values.shape[0]
        scratch[0, pl.ds(row, count)] = values[:, 0:WIN]
        scratch[1, pl.ds(row, count)] = values[:, cols - WIN :]

    edges(tokens_s, TOKEN_RIM, tokens_ref[...])
    edges(grad_s, GRAD_RIM, grad_ref[...])
    split = TOKEN_RIM + GRAD_RIM
    for ref, below in ((lon_near_ref, lon_even), (lon_far_ref, jnp.logical_not(lon_even))):
        edges(tokens_s, either(below, TOKEN_ROWS - TOKEN_RIM, 0), ref[0:TOKEN_RIM])
        edges(grad_s, either(below, GRAD_ROWS - GRAD_RIM, 0), ref[TOKEN_RIM:split])
    lon_labels(ids_ref, lon_near_ref, lon_far_ref, lon_even, ids_s)
    lane = lax.broadcasted_iota(jnp.int32, (WIN, 128), 1)
    ids = jnp.zeros((WIN, 128), jnp.float32)
    for part in range(TOKEN_ROWS // WIN):
        moved = pltpu.roll(
            ids_s[part * WIN : (part + 1) * WIN, :], (128 - (cols - WIN) + WIN * part) % 128, 1
        )
        ids = jnp.where(lane // WIN == part, moved, ids)
    for side in range(2):
        skip = side * (WIN - TOKEN_RIM)
        for row in range(TOKEN_ROWS):
            message_s[side, row * TOKEN_RIM : (row + 1) * TOKEN_RIM, :] = tokens_s[
                side, row, skip : skip + TOKEN_RIM, :
            ]
        skip = side * (WIN - GRAD_RIM)
        for row in range(GRAD_ROWS):
            first = TOKEN_PART + row * GRAD_RIM
            message_s[side, first : first + GRAD_RIM, :] = grad_s[
                side, row, skip : skip + GRAD_RIM, :
            ]
        first = TOKEN_PART + GRAD_ROWS * GRAD_RIM
        message_s[side, first:ID_PLACE, :] = jnp.zeros((ID_PLACE - first, 128), jnp.float32)
        message_s[side, ID_PLACE:, :] = ids
    near_ref[...] = message_s[either(lat_even, 1, 0)].astype(jnp.bfloat16)
    far_ref[...] = message_s[either(lat_even, 0, 1)].astype(jnp.bfloat16)


def assembled(
    tokens_ref,
    grad_ref,
    ids_ref,
    lon_near_ref,
    lon_far_ref,
    lat_near_ref,
    lat_far_ref,
    tokens_s,
    grad_s,
    ids_s,
    message_s,
    first_col,
    lat_total,
):
    lon_even = place_along(LON) % 2 == 0
    lat_even = place_along(LAT) % 2 == 0
    rows, cols = tokens_ref.shape[0], tokens_ref.shape[1]
    middle = slice(WIN, WIN + cols)
    tokens_s[TOKEN_RIM : TOKEN_RIM + rows, middle, :] = tokens_ref[...].astype(jnp.float32)
    grad_s[GRAD_RIM : GRAD_RIM + rows, middle, :] = grad_ref[...].astype(jnp.float32)
    split = TOKEN_RIM + GRAD_RIM
    for ref, below in ((lon_near_ref, lon_even), (lon_far_ref, jnp.logical_not(lon_even))):
        row = either(below, TOKEN_ROWS - TOKEN_RIM, 0)
        tokens_s[pl.ds(row, TOKEN_RIM), middle, :] = ref[0:TOKEN_RIM].astype(jnp.float32)
        row = either(below, GRAD_ROWS - GRAD_RIM, 0)
        grad_s[pl.ds(row, GRAD_RIM), middle, :] = ref[TOKEN_RIM:split].astype(jnp.float32)
    near, far = lat_near_ref[...].astype(jnp.float32), lat_far_ref[...].astype(jnp.float32)
    message_s[0] = jnp.where(lat_even, far, near)
    message_s[1] = jnp.where(lat_even, near, far)
    for side, token_col, grad_col in (
        (0, WIN - TOKEN_RIM, WIN - GRAD_RIM),
        (1, WIN + cols, WIN + cols),
    ):
        for row in range(TOKEN_ROWS):
            tokens_s[row, token_col : token_col + TOKEN_RIM, :] = message_s[
                side, row * TOKEN_RIM : (row + 1) * TOKEN_RIM, :
            ]
        for row in range(GRAD_ROWS):
            first = TOKEN_PART + row * GRAD_RIM
            grad_s[row, grad_col : grad_col + GRAD_RIM, :] = message_s[
                side, first : first + GRAD_RIM, :
            ]
    lon_labels(ids_ref, lon_near_ref, lon_far_ref, lon_even, ids_s)
    packed = message_s[0, ID_PLACE:, :]
    before = jnp.concatenate(
        [packed]
        + [pltpu.roll(packed, 128 - WIN * part, 1) for part in range(1, TOKEN_ROWS // WIN)]
        + [jnp.zeros_like(packed)],
        axis=0,
    )
    lane = lax.broadcasted_iota(jnp.int32, ids_s.shape, 1)
    own = pltpu.roll(ids_s[...], LABEL_RIM, 1)
    ids = jnp.where(lane < LABEL_RIM, before, own)
    shifted = first_col + lane - LABEL_RIM
    shifted = jnp.where(shifted < 0, shifted + lat_total, shifted)
    return ids * 2.0 + jnp.where(shifted >= lat_total - SHIFT, 1.0, 0.0)


def bias_rows(table_ref):
    lane = lax.broadcasted_iota(jnp.int32, (WIN, 128), 1)
    source = lax.broadcasted_iota(jnp.int32, (256, 128), 0)
    target = lax.broadcasted_iota(jnp.int32, (256, 128), 1)
    hit = jnp.logical_and(source // 16 == target // WIN, source % 16 == target % WIN)
    narrow = jnp.where(hit, 1.0, 0.0).astype(jnp.bfloat16)
    pieces = []
    for head in range(HEADS):
        table = jnp.broadcast_to(table_ref[head : head + 1, :], (WIN, 256))
        place = lax.broadcasted_iota(jnp.int32, (WIN, 256), 0)
        moved = jnp.zeros((WIN, 256), jnp.float32)
        for row in range(WIN):
            steps = (256 - (WIN - 1 - row)) % 256
            part = pltpu.roll(table, steps, 1) if steps else table
            moved = jnp.where(place == row, part, moved)
        pieces.append(moved)
    rest = jnp.concatenate(pieces, axis=0)
    packed = jnp.zeros((HEADS * WIN, 128), jnp.float32)
    for _ in range(3):
        part = rest.astype(jnp.bfloat16)
        packed = packed + matmul(part, narrow)
        rest = rest - part.astype(jnp.float32)
    rows = []
    for row in range(WIN):
        tiles = []
        for pair in range(HEADS // 2):
            halves = []
            for half in range(2):
                head = 2 * pair + half
                steps = (AREA * half - WIN * (WIN - 1 - row)) % 128
                part = packed[head * WIN : (head + 1) * WIN]
                halves.append(pltpu.roll(part, steps, 1) if steps else part)
            tiles.append(jnp.where(lane < AREA, halves[0], halves[1]))
        rows.append(jnp.concatenate(tiles, axis=1))
    return jnp.concatenate(rows, axis=0)


def scattered_sum(partial, axes):
    count = lax.axis_size(axes)
    chunks = partial.reshape(count, partial.shape[0] // count, partial.shape[1])
    received = lax.all_to_all(chunks, axes, 0, 0, tiled=True)
    return jnp.sum(received.astype(jnp.float32), axis=0)


def spread(chunk, axes):
    count = lax.axis_size(axes)
    copies = jnp.broadcast_to(chunk[None], (count,) + chunk.shape)
    return lax.all_to_all(copies, axes, 0, 0, tiled=True)


def total_over_devices(kept, sent, grad_scale):
    cores = [(0, 1), (1, 0)]
    other = lax.ppermute(sent, "c", cores)
    own = (kept.astype(jnp.float32) + other.astype(jnp.float32)).astype(jnp.bfloat16)
    own = scattered_sum(own, ("x",)).astype(jnp.bfloat16)
    own = scattered_sum(own, ("y",)).astype(jnp.bfloat16)
    parts = spread(own, DEEP)
    own = (jnp.sum(parts.astype(jnp.float32), axis=0) * grad_scale).astype(jnp.bfloat16)
    own = spread(own, ("y",)).reshape(-1, 128)
    own = spread(own, ("x",)).reshape(-1, 128)
    return own, lax.ppermute(own, "c", cores)


def unpack_kernel(
    own_ref,
    other_ref,
    qkv_ref,
    proj_ref,
    up_ref,
    down_ref,
    conv_ref,
    gain_one_ref,
    gain_two_ref,
    table_ref,
    rows_s,
):
    core = lax.axis_index("c")
    half = ROWS // 2
    rows_s[pl.ds(pl.multiple_of(core * half, half), half), :] = own_ref[...]
    rows_s[pl.ds(pl.multiple_of((1 - core) * half, half), half), :] = other_ref[...]

    def piece(first, count):
        return rows_s[first : first + count, :].astype(jnp.float32)

    conv_ref[...] = piece(0, 1152).reshape(9, 128, 128)
    place = 1152
    for ref, tiles in ((qkv_ref, 3), (proj_ref, 1), (up_ref, 4)):
        for tile in range(tiles):
            ref[:, tile * 128 : (tile + 1) * 128] = piece(place, 128)
            place = place + 128
    down_ref[...] = piece(place, 512)
    small = piece(place + 512, 16)
    gain_one_ref[...] = small[0:1]
    gain_two_ref[...] = small[1:2]
    for low in range(WIN):
        moved = pltpu.roll(small, (128 - 16 * low) % 128, 1) if low else small
        for head in range(HEADS):
            for high in range(2):
                row = high * WIN + low
                if row < SPAN:
                    line = 2 + 2 * head + high
                    table_ref[row, head : head + 1, :] = moved[line : line + 1, :SPAN]


def lane_mean(values):
    return jnp.sum(values, axis=-1, keepdims=True) * (1.0 / 128.0)


def layer_norm(values, gain):
    centred = values - lane_mean(values)
    inverse = lax.rsqrt(lane_mean(centred * centred) + epsilon)
    normed = centred * inverse
    return (normed * gain).astype(jnp.bfloat16), normed, inverse


def layer_norm_back(grad_in, normed, inverse, gain):
    scaled = grad_in * gain
    return inverse * (scaled - lane_mean(scaled) - normed * lane_mean(scaled * normed))


def matmul(left, right):
    return jnp.dot(left, right, preferred_element_type=jnp.float32)


def matmul_nt(left, right):
    return lax.dot_general(left, right, (((1,), (1,)), ((), ())), preferred_element_type=jnp.float32)


def matmul_tn(left, right):
    return lax.dot_general(left, right, (((0,), (0,)), ((), ())), preferred_element_type=jnp.float32)


def by_heads(rows, head_masks):
    return jnp.concatenate([rows * mask for mask in head_masks], axis=0)


def own_heads(stacked, head_lanes):
    total = jnp.zeros((AREA, 128), jnp.float32)
    for head in range(HEADS):
        part = stacked[head * AREA : (head + 1) * AREA]
        total = total + jnp.where(head_lanes[head], part, 0.0)
    return total


def table_rows(bias_sum):
    lane = lax.broadcasted_iota(jnp.int32, (WIN, 128), 1)
    pieces = []
    for head in range(HEADS):
        half = head % 2
        tile = bias_sum[:, (head // 2) * 128 : (head // 2 + 1) * 128]
        tile_sum = jnp.zeros((WIN, 128), jnp.float32)
        for row in range(WIN):
            part = jnp.where(lane // AREA == half, tile[row * WIN : (row + 1) * WIN], 0.0)
            steps = (WIN * (WIN - 1 - row) - AREA * half) % 128
            tile_sum = tile_sum + (pltpu.roll(part, steps, 1) if steps else part)
        pieces.append(tile_sum)
    stacked = jnp.concatenate(pieces, axis=0)
    source = lax.broadcasted_iota(jnp.int32, (128, 256), 0)
    target = lax.broadcasted_iota(jnp.int32, (128, 256), 1)
    hit = jnp.logical_and(source // WIN == target // 16, source % WIN == target % 16)
    spread_to = jnp.where(hit, 1.0, 0.0).astype(jnp.bfloat16)
    spread = jnp.zeros((HEADS * WIN, 256), jnp.float32)
    rest = stacked
    for _ in range(3):
        part = rest.astype(jnp.bfloat16)
        spread = spread + matmul(part, spread_to)
        rest = rest - part.astype(jnp.float32)
    place = lax.broadcasted_iota(jnp.int32, (HEADS * WIN, 256), 0) % WIN
    table = jnp.zeros((HEADS * WIN, 256), jnp.float32)
    for row in range(WIN):
        part = jnp.where(place == row, spread, 0.0)
        table = table + (pltpu.roll(part, WIN - 1 - row, 1) if row < WIN - 1 else part)
    rows = []
    for head in range(HEADS):
        head_sum = jnp.sum(table[head * WIN : (head + 1) * WIN], axis=0, keepdims=True)
        rows.extend([head_sum[:, :128], head_sum[:, 128:]])
    return rows


def block_kernel(
    lat_total,
    tokens_ref,
    grad_ref,
    ids_ref,
    lon_far_ref,
    lon_near_ref,
    lat_far_ref,
    lat_near_ref,
    table_ref,
    qkv_hbm,
    proj_hbm,
    up_hbm,
    down_hbm,
    conv_hbm,
    gain_one_hbm,
    gain_two_hbm,
    down_out_ref,
    grad_tokens_ref,
    kept_ref,
    sent_ref,
    tokens_s,
    grad_s,
    ids_s,
    gcat_s,
    rows_s,
    block_out_s,
    grad_tokens_s,
    ln_one_s,
    ln_two_s,
    hidden_s,
    grad_pre_s,
    grad_block_s,
    mixed_s,
    grad_att_s,
    grad_qkv_s,
    message_s,
    qkv_ref,
    proj_ref,
    up_ref,
    down_ref,
    conv_ref,
    gain_one_ref,
    gain_two_ref,
    sems,
):
    copies = fetched(
        (
            (qkv_hbm, qkv_ref),
            (gain_one_hbm, gain_one_ref),
            (gain_two_hbm, gain_two_ref),
            (proj_hbm, proj_ref),
            (up_hbm, up_ref),
            (down_hbm, down_ref),
            (conv_hbm, conv_ref),
        ),
        sems,
    )
    own_rows, own_cols = tokens_ref.shape[0], tokens_ref.shape[1]
    first_col = place_along(LAT) * own_cols
    labels = assembled(
        tokens_ref,
        grad_ref,
        ids_ref,
        lon_near_ref,
        lon_far_ref,
        lat_near_ref,
        lat_far_ref,
        tokens_s,
        grad_s,
        ids_s,
        message_s,
        first_col,
        lat_total,
    )
    ids_s[...] = labels
    position = first_col - TOKEN_RIM + lax.broadcasted_iota(jnp.int32, (PAD_COLS, 128), 0)
    position = jnp.where(position < 0, position + lat_total, position)
    position = jnp.where(position >= lat_total, position - lat_total, position)
    keep_after = jnp.where(position != lat_total - 1, 1.0, 0.0)
    keep_before = jnp.where(position != 0, 1.0, 0.0)
    for tap, keep in ((0, keep_after), (1, None), (2, keep_before)):
        piece = grad_s[:, 5 - tap : 5 - tap + PAD_COLS, :]
        if keep is not None:
            piece = piece * keep[None]
        gcat_s[:, tap * 128 : (tap + 1) * 128] = piece.reshape(GRAD_ROWS * PAD_COLS, 128).astype(
            jnp.bfloat16
        )
    lane_row = lax.broadcasted_iota(jnp.int32, (AREA, 128), 0)
    diagonal = (
        lax.broadcasted_iota(jnp.int32, (AREA, HEADS * AREA), 1) % AREA
        == lax.broadcasted_iota(jnp.int32, (AREA, HEADS * AREA), 0)
    )
    biases = bias_rows(table_ref)
    for copy in copies:
        copy.wait()
    gain_one, gain_two = gain_one_ref[...], gain_two_ref[...]
    lane = lax.broadcasted_iota(jnp.int32, (AREA, 128), 1)
    head_lanes = [lane // HEAD_DIM == head for head in range(HEADS)]
    head_masks = [jnp.where(hit, 1.0, 0.0).astype(jnp.bfloat16) for hit in head_lanes]
    score_scale = HEAD_DIM ** (-0.5)
    length = WIN_COLS * AREA
    bias_sum = jnp.zeros((AREA, HEADS * AREA), jnp.float32)
    gain_one_sum = jnp.zeros((1, 128), jnp.float32)
    gain_two_sum = jnp.zeros((1, 128), jnp.float32)
    for chunk in range(WIN_ROWS):
        top = chunk * WIN
        source = jnp.concatenate(
            [
                tokens_s[top : top + WIN, 4 + win * WIN : 12 + win * WIN, :].reshape(AREA, 128)
                for win in range(WIN_COLS)
            ],
            axis=0,
        )
        label_rows = jnp.concatenate(
            [
                jnp.broadcast_to(ids_s[top + row : top + row + 1, :], (WIN, 128))
                for row in range(WIN)
            ],
            axis=0,
        )
        ln_one, normed_one, inverse_one = layer_norm(source, gain_one)
        qkv_all = matmul(ln_one, qkv_ref[...]).astype(jnp.bfloat16)
        saved, mixed_parts = [], []
        for win in range(WIN_COLS):
            part = qkv_all[win * AREA : (win + 1) * AREA]
            query, key, value = part[:, :128], part[:, 128:256], part[:, 256:]
            query_heads = by_heads(query, head_masks)
            picked = jnp.where(lane == win * WIN + lane_row % WIN, label_rows, 0.0)
            column = jnp.broadcast_to(
                jnp.sum(picked, axis=1, keepdims=True), (AREA, HEADS * AREA)
            )
            across = jnp.sum(jnp.where(diagonal, column, 0.0), axis=0, keepdims=True)
            allowed = column == across
            scores = matmul_nt(key, query_heads) * score_scale + biases
            scores = jnp.where(allowed, scores, -1e30)
            raised = jnp.exp(scores - jnp.max(scores, axis=0, keepdims=True))
            probabilities = raised * (1.0 / jnp.sum(raised, axis=0, keepdims=True))
            weights = probabilities.astype(jnp.bfloat16)
            mixed_parts.append(own_heads(matmul_tn(weights, value), head_lanes).astype(jnp.bfloat16))
            saved.append((query_heads, key, value, probabilities, weights))
        mixed = jnp.concatenate(mixed_parts, axis=0)
        projected = matmul(mixed, proj_ref[...]).astype(jnp.bfloat16)
        middle = source + projected.astype(jnp.float32)
        ln_two, normed_two, inverse_two = layer_norm(middle, gain_two)
        pre_act = matmul(ln_two, up_ref[...])
        cumulative = 0.5 * (1.0 + lax.erf(pre_act * 0.7071067811865476))
        hidden = (pre_act * cumulative).astype(jnp.bfloat16)
        slope = cumulative + pre_act * (jnp.exp(-0.5 * pre_act * pre_act) * 0.3989422804014327)
        block_out = (middle + matmul(hidden, down_ref[...])).astype(jnp.bfloat16).astype(jnp.float32)
        for win in range(WIN_COLS):
            piece = block_out[win * AREA : (win + 1) * AREA].reshape(WIN, WIN, 128)
            block_out_s[top : top + WIN, win * WIN : (win + 1) * WIN, :] = piece

        grad_grid = jnp.zeros((WIN * PAD_COLS, 128), jnp.float32)
        for tap in range(3):
            first = (top + 2 - tap) * PAD_COLS
            taps = jnp.concatenate([conv_ref[3 * tap + side] for side in range(3)], axis=1)
            grad_grid = grad_grid + matmul_nt(gcat_s[first : first + WIN * PAD_COLS, :], taps)
        grad_grid = grad_grid.reshape(WIN, PAD_COLS, 128)
        grad_block = jnp.concatenate(
            [
                grad_grid[:, win * WIN : (win + 1) * WIN, :].reshape(AREA, 128)
                for win in range(WIN_COLS)
            ],
            axis=0,
        )
        grad_block_b = grad_block.astype(jnp.bfloat16)
        grad_hidden = matmul_nt(grad_block_b, down_ref[...])
        grad_pre = (grad_hidden * slope).astype(jnp.bfloat16)
        grad_ln_two = matmul_nt(grad_pre, up_ref[...])
        grad_middle = grad_block + layer_norm_back(grad_ln_two, normed_two, inverse_two, gain_two)
        grad_att = grad_middle.astype(jnp.bfloat16)
        grad_mixed = matmul_nt(grad_att, proj_ref[...]).astype(jnp.bfloat16)
        grad_parts = []
        for win in range(WIN_COLS):
            query_heads, key, value, probabilities, weights = saved[win]
            grad_heads = by_heads(grad_mixed[win * AREA : (win + 1) * AREA], head_masks)
            grad_probs = matmul_nt(value, grad_heads)
            grad_value = matmul(weights, grad_heads)
            centre = jnp.sum(probabilities * grad_probs, axis=0, keepdims=True)
            grad_scores = probabilities * (grad_probs - centre)
            if chunk and win:
                bias_sum = bias_sum + grad_scores
            grad_scores_b = grad_scores.astype(jnp.bfloat16)
            grad_key = matmul(grad_scores_b, query_heads) * score_scale
            grad_query = own_heads(matmul_tn(grad_scores_b, key), head_lanes) * score_scale
            grad_parts.append(
                jnp.concatenate([grad_query, grad_key, grad_value], axis=1).astype(jnp.bfloat16)
            )
        grad_qkv = jnp.concatenate(grad_parts, axis=0)
        grad_ln_one = matmul_nt(grad_qkv, qkv_ref[...])
        grad_tokens = grad_middle + layer_norm_back(grad_ln_one, normed_one, inverse_one, gain_one)
        for win in range(WIN_COLS):
            piece = grad_tokens[win * AREA : (win + 1) * AREA].reshape(WIN, WIN, 128)
            grad_tokens_s[top : top + WIN, win * WIN : (win + 1) * WIN, :] = piece
        if chunk:
            gain_one_sum = gain_one_sum + jnp.sum(
                (grad_ln_one * normed_one)[AREA:], axis=0, keepdims=True
            )
            gain_two_sum = gain_two_sum + jnp.sum(
                (grad_ln_two * normed_two)[AREA:], axis=0, keepdims=True
            )
            kept = slice((chunk - 1) * (length - AREA), chunk * (length - AREA))
            ln_one_s[kept, :] = ln_one[AREA:]
            ln_two_s[kept, :] = ln_two[AREA:]
            hidden_s[kept, :] = hidden[AREA:]
            grad_pre_s[kept, :] = grad_pre[AREA:]
            grad_block_s[kept, :] = grad_block_b[AREA:]
            mixed_s[kept, :] = mixed[AREA:]
            grad_att_s[kept, :] = grad_att[AREA:]
            grad_qkv_s[kept, :] = grad_qkv[AREA:]

    col = first_col + lax.broadcasted_iota(jnp.int32, (own_cols, 128), 0)
    keeps = (col != 0, None, col != lat_total - 1)
    shifted = []
    for tap in range(3):
        piece = block_out_s[3 : own_rows + 5, 3 + tap : 3 + tap + own_cols, :]
        if keeps[tap] is not None:
            piece = piece * jnp.where(keeps[tap], 1.0, 0.0)[None]
        shifted.append(piece.reshape((own_rows + 2) * own_cols, 128).astype(jnp.bfloat16))
    patches = jnp.concatenate(shifted, axis=1)
    count = own_rows * own_cols
    downscaled = jnp.zeros((count, 128), jnp.float32)
    grad_own = grad_ref[...].reshape(count, 128)
    for tap in range(3):
        rows = patches[tap * own_cols : tap * own_cols + count]
        downscaled = downscaled + matmul(rows, conv_ref[3 * tap : 3 * tap + 3].reshape(384, 128))
        rows_s[tap * 384 : (tap + 1) * 384, :] = matmul_tn(rows, grad_own).astype(jnp.bfloat16)
    down_out_ref[...] = downscaled.astype(jnp.bfloat16).reshape(own_rows, own_cols, 128)
    grad_tokens_ref[...] = (
        grad_tokens_s[4 : own_rows + 4, 4 : own_cols + 4, :].astype(jnp.bfloat16)
    )
    place = 1152
    for left, right, flipped in (
        (ln_one_s, grad_qkv_s, False),
        (mixed_s, grad_att_s, False),
        (ln_two_s, grad_pre_s, False),
        (hidden_s, grad_block_s, True),
    ):
        product = matmul_tn(left[...], right[...]).astype(jnp.bfloat16)
        if flipped:
            rows_s[place : place + product.shape[0], :] = product
            place = place + product.shape[0]
        else:
            for tile in range(product.shape[1] // 128):
                rows_s[place : place + 128, :] = product[:, tile * 128 : (tile + 1) * 128]
                place = place + 128
    small = [gain_one_sum, gain_two_sum] + table_rows(bias_sum)
    small.append(jnp.zeros((16 - len(small), 128), jnp.float32))
    rows_s[place : place + 16, :] = jnp.concatenate(small, axis=0).astype(jnp.bfloat16)
    place = place + 16
    rows_s[place:, :] = jnp.zeros((ROWS - place, 128), jnp.bfloat16)
    core = lax.axis_index("c")
    half = ROWS // 2
    kept_ref[...] = rows_s[pl.ds(pl.multiple_of(core * half, half), half), :]
    sent_ref[...] = rows_s[pl.ds(pl.multiple_of((1 - core) * half, half), half), :]


def per_device(
    tokens,
    grad_out,
    window_ids,
    qkv_weight,
    proj_weight,
    up_weight,
    down_weight,
    conv_weight,
    gain_one,
    gain_two,
    position_bias,
):
    row_count, col_count, width = tokens.shape
    lat_total = col_count * lax.axis_size(LAT)
    tokens_all = row_count * lat_total * lax.axis_size(LON)
    vmem = pl.BlockSpec(memory_space=pltpu.VMEM)
    params = pltpu.CompilerParams(vmem_limit_bytes=48 * 1024 * 1024)
    bf16 = lambda *shape: jax.ShapeDtypeStruct(shape, jnp.bfloat16)
    f32 = lambda *shape: jax.ShapeDtypeStruct(shape, jnp.float32)
    held = lambda *shape: pltpu.VMEM(shape, jnp.bfloat16)
    wide = lambda *shape: pltpu.VMEM(shape, jnp.float32)
    table = jnp.pad(position_bias, ((0, 0), (0, 1), (0, 1))).reshape(HEADS, 256)
    slabs = TOKEN_RIM + GRAD_RIM + 1
    anywhere = pl.BlockSpec(memory_space=pltpu.HBM)
    far, near, tokens, grad_out, window_ids = pl.pallas_call(
        lon_pack_kernel,
        out_shape=(
            bf16(slabs, col_count, width),
            bf16(slabs, col_count, width),
            bf16(*tokens.shape),
            bf16(*grad_out.shape),
            jax.ShapeDtypeStruct(window_ids.shape, jnp.int32),
        ),
        in_specs=[anywhere] * 3,
        out_specs=(vmem,) * 5,
        scratch_shapes=[wide(col_count, width), pltpu.SemaphoreType.DMA((3,))],
        compiler_params=params,
    )(tokens, grad_out, window_ids)
    lon_far = swapped(far, LON, False)
    lon_near = swapped(near, LON, True)
    far, near = pl.pallas_call(
        lat_pack_kernel,
        out_shape=(bf16(MESSAGE, width),) * 2,
        in_specs=[vmem] * 5,
        out_specs=(vmem,) * 2,
        scratch_shapes=[
            wide(2, TOKEN_ROWS, WIN, width),
            wide(2, GRAD_ROWS, WIN, width),
            wide(32, width),
            wide(2, MESSAGE, width),
        ],
        compiler_params=params,
    )(tokens, grad_out, window_ids, lon_far, lon_near)
    lat_far = swapped(far, LAT, False)
    lat_near = swapped(near, LAT, True)
    count = AREA * (WIN_ROWS - 1) * (WIN_COLS - 1)
    downscaled, grad_tokens, kept, sent = pl.pallas_call(
        functools.partial(block_kernel, lat_total),
        out_shape=(
            bf16(*tokens.shape),
            bf16(*tokens.shape),
            bf16(ROWS // 2, width),
            bf16(ROWS // 2, width),
        ),
        in_specs=[vmem] * 8 + [anywhere] * 7,
        out_specs=(vmem,) * 4,
        scratch_shapes=[
            wide(TOKEN_ROWS, 48, width),
            wide(GRAD_ROWS, 56, width),
            wide(32, width),
            held(GRAD_ROWS * PAD_COLS, 3 * width),
            held(ROWS, width),
            wide(TOKEN_ROWS, 40, width),
            wide(TOKEN_ROWS, 40, width),
            held(count, width),
            held(count, width),
            held(count, 4 * width),
            held(count, 4 * width),
            held(count, width),
            held(count, width),
            held(count, width),
            held(count, 3 * width),
            wide(2, MESSAGE, width),
            held(*qkv_weight.shape),
            held(*proj_weight.shape),
            held(*up_weight.shape),
            held(*down_weight.shape),
            held(*conv_weight.shape),
            wide(1, width),
            wide(1, width),
            pltpu.SemaphoreType.DMA((7,)),
        ],
        compiler_params=params,
        cost_estimate=pl.CostEstimate(
            flops=3_000_000_000, bytes_accessed=8_000_000, transcendentals=2_000_000
        ),
    )(
        tokens,
        grad_out,
        window_ids,
        lon_far,
        lon_near,
        lat_far,
        lat_near,
        table,
        qkv_weight,
        proj_weight,
        up_weight,
        down_weight,
        conv_weight,
        gain_one[None],
        gain_two[None],
    )
    own, other = total_over_devices(kept, sent, 1.0 / math.sqrt(tokens_all))
    results = pl.pallas_call(
        unpack_kernel,
        out_shape=(
            f32(width, 3 * width),
            f32(width, width),
            f32(width, 4 * width),
            f32(4 * width, width),
            f32(9, width, width),
            f32(1, width),
            f32(1, width),
            f32(SPAN, HEADS, SPAN),
        ),
        in_specs=[vmem] * 2,
        out_specs=(vmem,) * 8,
        scratch_shapes=[held(ROWS, width)],
        compiler_params=params,
    )(own, other)
    return (downscaled, grad_tokens) + results[:5] + (
        results[5][0],
        results[6][0],
        results[7].swapaxes(0, 1),
    )


def solution(mesh):
    lon_count, lat_count = mesh.devices.shape
    near = math.gcd(lon_count, 8)
    parts = (lon_count // near, near // 2, 2, 2, lat_count // 2)
    fine = Mesh(mesh.devices.reshape(parts), ("zl", "x", "c", "zh", "y"))
    grid = P(LON, LAT, None)
    return jax.shard_map(
        per_device,
        mesh=fine,
        in_specs=(grid, grid, P(LON, LAT)) + (P(),) * 8,
        out_specs=(grid, grid) + (P(),) * 8,
        check_vma=False,
    )
```

```python
import functools
import math

import jax
import jax.numpy as jnp
from jax import lax
from jax.experimental import pallas as pl
from jax.experimental.pallas import tpu as pltpu
from jax.sharding import Mesh
from jax.sharding import PartitionSpec as P

HEADS = 4
WIN = 8
SHIFT = 4
SPAN = 15
HEAD_DIM = 32
AREA = WIN * WIN
WIN_ROWS = 3
WIN_COLS = 5
PAD_COLS = 48
ROWS = 3072
TOKEN_RIM = 4
GRAD_RIM = 5
LABEL_RIM = 8

LON = ("zl", "x", "c")
LAT = ("zh", "y")
DEEP = ("zl", "zh")
TOKEN_ROWS = 24
GRAD_ROWS = 26
TOKEN_PART = TOKEN_ROWS * TOKEN_RIM
ID_PLACE = 232
MESSAGE = 240

epsilon = 1e-05


def swapped(value, axes, first):
    count = lax.axis_size(axes)
    pairs = []
    for source in range(count):
        up = (source % 2 == 0) == first
        pairs.append((source, (source + 1) % count if up else (source - 1) % count))
    return lax.ppermute(value, axes, pairs)


def place_along(axes):
    place = 0
    for axis in axes:
        place = place * lax.axis_size(axis) + lax.axis_index(axis)
    return place


def either(choice, first, second):
    return jnp.where(choice, jnp.int32(first), jnp.int32(second))


def fetched(pairs, sems):
    copies = [
        pltpu.make_async_copy(source, target, sems.at[place])
        for place, (source, target) in enumerate(pairs)
    ]
    for copy in copies:
        copy.start()
    return copies


def lon_pack_kernel(
    tokens_hbm, grad_hbm, ids_hbm, far_ref, near_ref, tokens_ref, grad_ref, ids_ref, ids_s, sems
):
    copies = fetched(
        ((tokens_hbm, tokens_ref), (grad_hbm, grad_ref), (ids_hbm, ids_ref)), sems
    )
    even = place_along(LON) % 2 == 0
    rows = tokens_ref.shape[0]
    ids_s[...] = jnp.zeros_like(ids_s)
    for copy in copies:
        copy.wait()
    ids_s[0:LABEL_RIM, 0 : ids_ref.shape[1]] = ids_ref[rows - LABEL_RIM :, :].astype(jnp.float32)
    ids = ids_s[...].astype(jnp.bfloat16)
    for ref, upper in ((near_ref, even), (far_ref, jnp.logical_not(even))):
        ref[0:TOKEN_RIM] = tokens_ref[pl.ds(either(upper, rows - TOKEN_RIM, 0), TOKEN_RIM)]
        ref[TOKEN_RIM : TOKEN_RIM + GRAD_RIM] = grad_ref[
            pl.ds(either(upper, rows - GRAD_RIM, 0), GRAD_RIM)
        ]
        ref[TOKEN_RIM + GRAD_RIM] = ids


def lon_labels(ids_ref, lon_near_ref, lon_far_ref, even, ids_s):
    row = TOKEN_RIM + GRAD_RIM
    before = jnp.where(
        even, lon_far_ref[row].astype(jnp.float32), lon_near_ref[row].astype(jnp.float32)
    )
    ids_s[...] = jnp.zeros_like(ids_s)
    ids_s[0:LABEL_RIM, :] = before[0:LABEL_RIM]
    ids_s[LABEL_RIM : LABEL_RIM + ids_ref.shape[0], 0 : ids_ref.shape[1]] = ids_ref[...].astype(
        jnp.float32
    )


def lat_pack_kernel(
    tokens_ref,
    grad_ref,
    ids_ref,
    lon_far_ref,
    lon_near_ref,
    far_ref,
    near_ref,
    tokens_s,
    grad_s,
    ids_s,
    message_s,
):
    lon_even = place_along(LON) % 2 == 0
    lat_even = place_along(LAT) % 2 == 0
    cols = tokens_ref.shape[1]

    def edges(scratch, row, values):
        values = values.astype(jnp.float32)
        count = values.shape[0]
        scratch[0, pl.ds(row, count)] = values[:, 0:WIN]
        scratch[1, pl.ds(row, count)] = values[:, cols - WIN :]

    edges(tokens_s, TOKEN_RIM, tokens_ref[...])
    edges(grad_s, GRAD_RIM, grad_ref[...])
    split = TOKEN_RIM + GRAD_RIM
    for ref, below in ((lon_near_ref, lon_even), (lon_far_ref, jnp.logical_not(lon_even))):
        edges(tokens_s, either(below, TOKEN_ROWS - TOKEN_RIM, 0), ref[0:TOKEN_RIM])
        edges(grad_s, either(below, GRAD_ROWS - GRAD_RIM, 0), ref[TOKEN_RIM:split])
    lon_labels(ids_ref, lon_near_ref, lon_far_ref, lon_even, ids_s)
    lane = lax.broadcasted_iota(jnp.int32, (WIN, 128), 1)
    ids = jnp.zeros((WIN, 128), jnp.float32)
    for part in range(TOKEN_ROWS // WIN):
        moved = pltpu.roll(
            ids_s[part * WIN : (part + 1) * WIN, :], (128 - (cols - WIN) + WIN * part) % 128, 1
        )
        ids = jnp.where(lane // WIN == part, moved, ids)
    for side in range(2):
        skip = side * (WIN - TOKEN_RIM)
        for row in range(TOKEN_ROWS):
            message_s[side, row * TOKEN_RIM : (row + 1) * TOKEN_RIM, :] = tokens_s[
                side, row, skip : skip + TOKEN_RIM, :
            ]
        skip = side * (WIN - GRAD_RIM)
        for row in range(GRAD_ROWS):
            first = TOKEN_PART + row * GRAD_RIM
            message_s[side, first : first + GRAD_RIM, :] = grad_s[
                side, row, skip : skip + GRAD_RIM, :
            ]
        first = TOKEN_PART + GRAD_ROWS * GRAD_RIM
        message_s[side, first:ID_PLACE, :] = jnp.zeros((ID_PLACE - first, 128), jnp.float32)
        message_s[side, ID_PLACE:, :] = ids
    near_ref[...] = message_s[either(lat_even, 1, 0)].astype(jnp.bfloat16)
    far_ref[...] = message_s[either(lat_even, 0, 1)].astype(jnp.bfloat16)


def assembled(
    tokens_ref,
    grad_ref,
    ids_ref,
    lon_near_ref,
    lon_far_ref,
    lat_near_ref,
    lat_far_ref,
    tokens_s,
    grad_s,
    ids_s,
    message_s,
    first_col,
    lat_total,
):
    lon_even = place_along(LON) % 2 == 0
    lat_even = place_along(LAT) % 2 == 0
    rows, cols = tokens_ref.shape[0], tokens_ref.shape[1]
    middle = slice(WIN, WIN + cols)
    tokens_s[TOKEN_RIM : TOKEN_RIM + rows, middle, :] = tokens_ref[...].astype(jnp.float32)
    grad_s[GRAD_RIM : GRAD_RIM + rows, middle, :] = grad_ref[...].astype(jnp.float32)
    split = TOKEN_RIM + GRAD_RIM
    for ref, below in ((lon_near_ref, lon_even), (lon_far_ref, jnp.logical_not(lon_even))):
        row = either(below, TOKEN_ROWS - TOKEN_RIM, 0)
        tokens_s[pl.ds(row, TOKEN_RIM), middle, :] = ref[0:TOKEN_RIM].astype(jnp.float32)
        row = either(below, GRAD_ROWS - GRAD_RIM, 0)
        grad_s[pl.ds(row, GRAD_RIM), middle, :] = ref[TOKEN_RIM:split].astype(jnp.float32)
    near, far = lat_near_ref[...].astype(jnp.float32), lat_far_ref[...].astype(jnp.float32)
    message_s[0] = jnp.where(lat_even, far, near)
    message_s[1] = jnp.where(lat_even, near, far)
    for side, token_col, grad_col in (
        (0, WIN - TOKEN_RIM, WIN - GRAD_RIM),
        (1, WIN + cols, WIN + cols),
    ):
        for row in range(TOKEN_ROWS):
            tokens_s[row, token_col : token_col + TOKEN_RIM, :] = message_s[
                side, row * TOKEN_RIM : (row + 1) * TOKEN_RIM, :
            ]
        for row in range(GRAD_ROWS):
            first = TOKEN_PART + row * GRAD_RIM
            grad_s[row, grad_col : grad_col + GRAD_RIM, :] = message_s[
                side, first : first + GRAD_RIM, :
            ]
    lon_labels(ids_ref, lon_near_ref, lon_far_ref, lon_even, ids_s)
    packed = message_s[0, ID_PLACE:, :]
    before = jnp.concatenate(
        [packed]
        + [pltpu.roll(packed, 128 - WIN * part, 1) for part in range(1, TOKEN_ROWS // WIN)]
        + [jnp.zeros_like(packed)],
        axis=0,
    )
    lane = lax.broadcasted_iota(jnp.int32, ids_s.shape, 1)
    own = pltpu.roll(ids_s[...], LABEL_RIM, 1)
    ids = jnp.where(lane < LABEL_RIM, before, own)
    shifted = first_col + lane - LABEL_RIM
    shifted = jnp.where(shifted < 0, shifted + lat_total, shifted)
    return ids * 2.0 + jnp.where(shifted >= lat_total - SHIFT, 1.0, 0.0)


def bias_rows(table_ref):
    lane = lax.broadcasted_iota(jnp.int32, (WIN, 128), 1)
    source = lax.broadcasted_iota(jnp.int32, (256, 128), 0)
    target = lax.broadcasted_iota(jnp.int32, (256, 128), 1)
    hit = jnp.logical_and(source // 16 == target // WIN, source % 16 == target % WIN)
    narrow = jnp.where(hit, 1.0, 0.0).astype(jnp.bfloat16)
    pieces = []
    for head in range(HEADS):
        table = jnp.broadcast_to(table_ref[head : head + 1, :], (WIN, 256))
        place = lax.broadcasted_iota(jnp.int32, (WIN, 256), 0)
        moved = jnp.zeros((WIN, 256), jnp.float32)
        for row in range(WIN):
            steps = (256 - (WIN - 1 - row)) % 256
            part = pltpu.roll(table, steps, 1) if steps else table
            moved = jnp.where(place == row, part, moved)
        pieces.append(moved)
    rest = jnp.concatenate(pieces, axis=0)
    packed = jnp.zeros((HEADS * WIN, 128), jnp.float32)
    for _ in range(3):
        part = rest.astype(jnp.bfloat16)
        packed = packed + matmul(part, narrow)
        rest = rest - part.astype(jnp.float32)
    rows = []
    for row in range(WIN):
        tiles = []
        for pair in range(HEADS // 2):
            halves = []
            for half in range(2):
                head = 2 * pair + half
                steps = (AREA * half - WIN * (WIN - 1 - row)) % 128
                part = packed[head * WIN : (head + 1) * WIN]
                halves.append(pltpu.roll(part, steps, 1) if steps else part)
            tiles.append(jnp.where(lane < AREA, halves[0], halves[1]))
        rows.append(jnp.concatenate(tiles, axis=1))
    return jnp.concatenate(rows, axis=0)


def bias_kernel(table_ref, gain_one_ref, gain_two_ref, bias_ref, gains_ref):
    bias_ref[...] = bias_rows(table_ref)
    gains_ref[...] = jnp.zeros_like(gains_ref)
    gains_ref[0:1, :] = gain_one_ref[...]
    gains_ref[1:2, :] = gain_two_ref[...]


def scattered_sum(partial, axes):
    count = lax.axis_size(axes)
    chunks = partial.reshape(count, partial.shape[0] // count, partial.shape[1])
    received = lax.all_to_all(chunks, axes, 0, 0, tiled=True)
    return jnp.sum(received.astype(jnp.float32), axis=0)


def spread(chunk, axes):
    count = lax.axis_size(axes)
    copies = jnp.broadcast_to(chunk[None], (count,) + chunk.shape)
    return lax.all_to_all(copies, axes, 0, 0, tiled=True)


def total_over_devices(kept, sent, grad_scale):
    cores = [(0, 1), (1, 0)]
    other = lax.ppermute(sent, "c", cores)
    own = (kept.astype(jnp.float32) + other.astype(jnp.float32)).astype(jnp.bfloat16)
    own = scattered_sum(own, ("x", "y")).astype(jnp.bfloat16)
    parts = spread(own, DEEP)
    own = (jnp.sum(parts.astype(jnp.float32), axis=0) * grad_scale).astype(jnp.bfloat16)
    own = spread(own, ("y",)).reshape(-1, 128)
    own = spread(own, ("x",)).reshape(-1, 128)
    return own, lax.ppermute(own, "c", cores)


def unpack_kernel(
    own_ref,
    other_ref,
    qkv_ref,
    proj_ref,
    up_ref,
    down_ref,
    conv_ref,
    gain_one_ref,
    gain_two_ref,
    table_ref,
    rows_s,
):
    core = lax.axis_index("c")
    half = ROWS // 2
    rows_s[pl.ds(pl.multiple_of(core * half, half), half), :] = own_ref[...]
    rows_s[pl.ds(pl.multiple_of((1 - core) * half, half), half), :] = other_ref[...]

    def piece(first, count):
        return rows_s[first : first + count, :].astype(jnp.float32)

    conv_ref[...] = piece(0, 1152).reshape(9, 128, 128)
    place = 1152
    for ref, tiles in ((qkv_ref, 3), (proj_ref, 1), (up_ref, 4)):
        for tile in range(tiles):
            ref[:, tile * 128 : (tile + 1) * 128] = piece(place, 128)
            place = place + 128
    down_ref[...] = piece(place, 512)
    small = piece(place + 512, 16)
    gain_one_ref[...] = small[0:1]
    gain_two_ref[...] = small[1:2]
    for low in range(WIN):
        moved = pltpu.roll(small, (128 - 16 * low) % 128, 1) if low else small
        for head in range(HEADS):
            for high in range(2):
                row = high * WIN + low
                if row < SPAN:
                    line = 2 + 2 * head + high
                    table_ref[row, head : head + 1, :] = moved[line : line + 1, :SPAN]


def lane_mean(values):
    return jnp.sum(values, axis=-1, keepdims=True) * (1.0 / 128.0)


def layer_norm(values, gain):
    centred = values - lane_mean(values)
    inverse = lax.rsqrt(lane_mean(centred * centred) + epsilon)
    normed = centred * inverse
    return (normed * gain).astype(jnp.bfloat16), normed, inverse


def layer_norm_back(grad_in, normed, inverse, gain):
    scaled = grad_in * gain
    return inverse * (scaled - lane_mean(scaled) - normed * lane_mean(scaled * normed))


def matmul(left, right):
    return jnp.dot(left, right, preferred_element_type=jnp.float32)


def matmul_nt(left, right):
    return lax.dot_general(left, right, (((1,), (1,)), ((), ())), preferred_element_type=jnp.float32)


def matmul_tn(left, right):
    return lax.dot_general(left, right, (((0,), (0,)), ((), ())), preferred_element_type=jnp.float32)


def by_heads(rows, head_masks):
    return jnp.concatenate([rows * mask for mask in head_masks], axis=0)


def own_heads(stacked, head_lanes):
    total = jnp.zeros((AREA, 128), jnp.float32)
    for head in range(HEADS):
        part = stacked[head * AREA : (head + 1) * AREA]
        total = total + jnp.where(head_lanes[head], part, 0.0)
    return total


def table_rows(bias_sum):
    lane = lax.broadcasted_iota(jnp.int32, (WIN, 128), 1)
    pieces = []
    for head in range(HEADS):
        half = head % 2
        tile = bias_sum[:, (head // 2) * 128 : (head // 2 + 1) * 128]
        tile_sum = jnp.zeros((WIN, 128), jnp.float32)
        for row in range(WIN):
            part = jnp.where(lane // AREA == half, tile[row * WIN : (row + 1) * WIN], 0.0)
            steps = (WIN * (WIN - 1 - row) - AREA * half) % 128
            tile_sum = tile_sum + (pltpu.roll(part, steps, 1) if steps else part)
        pieces.append(tile_sum)
    stacked = jnp.concatenate(pieces, axis=0)
    source = lax.broadcasted_iota(jnp.int32, (128, 256), 0)
    target = lax.broadcasted_iota(jnp.int32, (128, 256), 1)
    hit = jnp.logical_and(source // WIN == target // 16, source % WIN == target % 16)
    spread_to = jnp.where(hit, 1.0, 0.0).astype(jnp.bfloat16)
    spread = jnp.zeros((HEADS * WIN, 256), jnp.float32)
    rest = stacked
    for _ in range(3):
        part = rest.astype(jnp.bfloat16)
        spread = spread + matmul(part, spread_to)
        rest = rest - part.astype(jnp.float32)
    place = lax.broadcasted_iota(jnp.int32, (HEADS * WIN, 256), 0) % WIN
    table = jnp.zeros((HEADS * WIN, 256), jnp.float32)
    for row in range(WIN):
        part = jnp.where(place == row, spread, 0.0)
        table = table + (pltpu.roll(part, WIN - 1 - row, 1) if row < WIN - 1 else part)
    rows = []
    for head in range(HEADS):
        head_sum = jnp.sum(table[head * WIN : (head + 1) * WIN], axis=0, keepdims=True)
        rows.extend([head_sum[:, :128], head_sum[:, 128:]])
    return rows


def block_kernel(
    lat_total,
    tokens_ref,
    grad_ref,
    ids_ref,
    lon_far_ref,
    lon_near_ref,
    lat_far_ref,
    lat_near_ref,
    bias_ref,
    gains_ref,
    qkv_ref,
    proj_ref,
    up_ref,
    down_ref,
    conv_ref,
    down_out_ref,
    grad_tokens_ref,
    kept_ref,
    sent_ref,
    tokens_s,
    grad_s,
    ids_s,
    gcat_s,
    rows_s,
    block_out_s,
    grad_tokens_s,
    ln_one_s,
    ln_two_s,
    hidden_s,
    grad_pre_s,
    grad_block_s,
    mixed_s,
    grad_att_s,
    grad_qkv_s,
    message_s,
):
    own_rows, own_cols = tokens_ref.shape[0], tokens_ref.shape[1]
    first_col = place_along(LAT) * own_cols
    labels = assembled(
        tokens_ref,
        grad_ref,
        ids_ref,
        lon_near_ref,
        lon_far_ref,
        lat_near_ref,
        lat_far_ref,
        tokens_s,
        grad_s,
        ids_s,
        message_s,
        first_col,
        lat_total,
    )
    ids_s[...] = labels
    position = first_col - TOKEN_RIM + lax.broadcasted_iota(jnp.int32, (PAD_COLS, 128), 0)
    position = jnp.where(position < 0, position + lat_total, position)
    position = jnp.where(position >= lat_total, position - lat_total, position)
    keep_after = jnp.where(position != lat_total - 1, 1.0, 0.0)
    keep_before = jnp.where(position != 0, 1.0, 0.0)
    for tap, keep in ((0, keep_after), (1, None), (2, keep_before)):
        piece = grad_s[:, 5 - tap : 5 - tap + PAD_COLS, :]
        if keep is not None:
            piece = piece * keep[None]
        gcat_s[:, tap * 128 : (tap + 1) * 128] = piece.reshape(GRAD_ROWS * PAD_COLS, 128).astype(
            jnp.bfloat16
        )
    lane_row = lax.broadcasted_iota(jnp.int32, (AREA, 128), 0)
    diagonal = (
        lax.broadcasted_iota(jnp.int32, (AREA, HEADS * AREA), 1) % AREA
        == lax.broadcasted_iota(jnp.int32, (AREA, HEADS * AREA), 0)
    )
    biases = bias_ref[...]
    gain_one, gain_two = gains_ref[0:1, :], gains_ref[1:2, :]
    lane = lax.broadcasted_iota(jnp.int32, (AREA, 128), 1)
    head_lanes = [lane // HEAD_DIM == head for head in range(HEADS)]
    head_masks = [jnp.where(hit, 1.0, 0.0).astype(jnp.bfloat16) for hit in head_lanes]
    score_scale = HEAD_DIM ** (-0.5)
    length = WIN_COLS * AREA
    bias_sum = jnp.zeros((AREA, HEADS * AREA), jnp.float32)
    gain_one_sum = jnp.zeros((1, 128), jnp.float32)
    gain_two_sum = jnp.zeros((1, 128), jnp.float32)
    def chunk_steps(chunk):
        nonlocal bias_sum, gain_one_sum, gain_two_sum
        top = chunk * WIN
        source = jnp.concatenate(
            [
                tokens_s[top : top + WIN, 4 + win * WIN : 12 + win * WIN, :].reshape(AREA, 128)
                for win in range(WIN_COLS)
            ],
            axis=0,
        )
        label_rows = jnp.concatenate(
            [
                jnp.broadcast_to(ids_s[top + row : top + row + 1, :], (WIN, 128))
                for row in range(WIN)
            ],
            axis=0,
        )
        ln_one, normed_one, inverse_one = layer_norm(source, gain_one)
        yield
        qkv_all = matmul(ln_one, qkv_ref[...]).astype(jnp.bfloat16)
        yield
        grad_grid = jnp.zeros((WIN * PAD_COLS, 128), jnp.float32)
        for tap in range(3):
            first = (top + 2 - tap) * PAD_COLS
            taps = jnp.concatenate([conv_ref[3 * tap + side] for side in range(3)], axis=1)
            grad_grid = grad_grid + matmul_nt(gcat_s[first : first + WIN * PAD_COLS, :], taps)
        grad_grid = grad_grid.reshape(WIN, PAD_COLS, 128)
        grad_block = jnp.concatenate(
            [
                grad_grid[:, win * WIN : (win + 1) * WIN, :].reshape(AREA, 128)
                for win in range(WIN_COLS)
            ],
            axis=0,
        )
        saved, mixed_parts = [], []
        raw = []
        for win in range(WIN_COLS):
            part = qkv_all[win * AREA : (win + 1) * AREA]
            query, key, value = part[:, :128], part[:, 128:256], part[:, 256:]
            query_heads = by_heads(query, head_masks)
            picked = jnp.where(lane == win * WIN + lane_row % WIN, label_rows, 0.0)
            column = jnp.broadcast_to(
                jnp.sum(picked, axis=1, keepdims=True), (AREA, HEADS * AREA)
            )
            across = jnp.sum(jnp.where(diagonal, column, 0.0), axis=0, keepdims=True)
            scores = matmul_nt(key, query_heads) * score_scale + biases
            scores = jnp.where(column == across, scores, -1e30)
            raw.append((query_heads, key, value, scores))
        yield
        for query_heads, key, value, scores in raw:
            raised = jnp.exp(scores - jnp.max(scores, axis=0, keepdims=True))
            probabilities = raised * (1.0 / jnp.sum(raised, axis=0, keepdims=True))
            saved.append((query_heads, key, value, probabilities, probabilities.astype(jnp.bfloat16)))
        yield
        for query_heads, key, value, probabilities, weights in saved:
            mixed_parts.append(own_heads(matmul_tn(weights, value), head_lanes).astype(jnp.bfloat16))
        yield
        mixed = jnp.concatenate(mixed_parts, axis=0)
        projected = matmul(mixed, proj_ref[...]).astype(jnp.bfloat16)
        yield
        middle = source + projected.astype(jnp.float32)
        ln_two, normed_two, inverse_two = layer_norm(middle, gain_two)
        yield
        pre_act = matmul(ln_two, up_ref[...])
        yield
        cumulative = 0.5 * (1.0 + lax.erf(pre_act * 0.7071067811865476))
        hidden = (pre_act * cumulative).astype(jnp.bfloat16)
        slope = cumulative + pre_act * (jnp.exp(-0.5 * pre_act * pre_act) * 0.3989422804014327)
        yield
        block_out = (middle + matmul(hidden, down_ref[...])).astype(jnp.bfloat16).astype(jnp.float32)
        for win in range(WIN_COLS):
            piece = block_out[win * AREA : (win + 1) * AREA].reshape(WIN, WIN, 128)
            block_out_s[top : top + WIN, win * WIN : (win + 1) * WIN, :] = piece

        yield
        grad_block_b = grad_block.astype(jnp.bfloat16)
        grad_hidden = matmul_nt(grad_block_b, down_ref[...])
        yield
        grad_pre = (grad_hidden * slope).astype(jnp.bfloat16)
        grad_ln_two = matmul_nt(grad_pre, up_ref[...])
        yield
        grad_middle = grad_block + layer_norm_back(grad_ln_two, normed_two, inverse_two, gain_two)
        grad_att = grad_middle.astype(jnp.bfloat16)
        yield
        grad_mixed = matmul_nt(grad_att, proj_ref[...]).astype(jnp.bfloat16)
        yield
        grad_parts, steps_back = [], []
        for win in range(WIN_COLS):
            query_heads, key, value, probabilities, weights = saved[win]
            grad_heads = by_heads(grad_mixed[win * AREA : (win + 1) * AREA], head_masks)
            grad_probs = matmul_nt(value, grad_heads)
            grad_value = matmul(weights, grad_heads)
            steps_back.append((grad_probs, grad_value))
        yield
        grads = []
        for win in range(WIN_COLS):
            probabilities = saved[win][3]
            grad_probs = steps_back[win][0]
            centre = jnp.sum(probabilities * grad_probs, axis=0, keepdims=True)
            grad_scores = probabilities * (grad_probs - centre)
            if chunk and win:
                bias_sum = bias_sum + grad_scores
            grads.append(grad_scores.astype(jnp.bfloat16))
        yield
        for win in range(WIN_COLS):
            query_heads, key = saved[win][:2]
            grad_key = matmul(grads[win], query_heads) * score_scale
            grad_query = own_heads(matmul_tn(grads[win], key), head_lanes) * score_scale
            grad_parts.append(
                jnp.concatenate([grad_query, grad_key, steps_back[win][1]], axis=1).astype(
                    jnp.bfloat16
                )
            )
        yield
        grad_qkv = jnp.concatenate(grad_parts, axis=0)
        grad_ln_one = matmul_nt(grad_qkv, qkv_ref[...])
        yield
        grad_tokens = grad_middle + layer_norm_back(grad_ln_one, normed_one, inverse_one, gain_one)
        for win in range(WIN_COLS):
            piece = grad_tokens[win * AREA : (win + 1) * AREA].reshape(WIN, WIN, 128)
            grad_tokens_s[top : top + WIN, win * WIN : (win + 1) * WIN, :] = piece
        if chunk:
            gain_one_sum = gain_one_sum + jnp.sum(
                (grad_ln_one * normed_one)[AREA:], axis=0, keepdims=True
            )
            gain_two_sum = gain_two_sum + jnp.sum(
                (grad_ln_two * normed_two)[AREA:], axis=0, keepdims=True
            )
            kept = slice((chunk - 1) * (length - AREA), chunk * (length - AREA))
            ln_one_s[kept, :] = ln_one[AREA:]
            ln_two_s[kept, :] = ln_two[AREA:]
            hidden_s[kept, :] = hidden[AREA:]
            grad_pre_s[kept, :] = grad_pre[AREA:]
            grad_block_s[kept, :] = grad_block_b[AREA:]
            mixed_s[kept, :] = mixed[AREA:]
            grad_att_s[kept, :] = grad_att[AREA:]
            grad_qkv_s[kept, :] = grad_qkv[AREA:]


    running = [chunk_steps(chunk) for chunk in range(WIN_ROWS)]
    while running:
        running = [steps for steps in running if next(steps, running) is not running]

    col = first_col + lax.broadcasted_iota(jnp.int32, (own_cols, 128), 0)
    keeps = (col != 0, None, col != lat_total - 1)
    shifted = []
    for tap in range(3):
        piece = block_out_s[3 : own_rows + 5, 3 + tap : 3 + tap + own_cols, :]
        if keeps[tap] is not None:
            piece = piece * jnp.where(keeps[tap], 1.0, 0.0)[None]
        shifted.append(piece.reshape((own_rows + 2) * own_cols, 128).astype(jnp.bfloat16))
    patches = jnp.concatenate(shifted, axis=1)
    count = own_rows * own_cols
    downscaled = jnp.zeros((count, 128), jnp.float32)
    grad_own = grad_ref[...].reshape(count, 128)
    for tap in range(3):
        rows = patches[tap * own_cols : tap * own_cols + count]
        downscaled = downscaled + matmul(rows, conv_ref[3 * tap : 3 * tap + 3].reshape(384, 128))
        rows_s[tap * 384 : (tap + 1) * 384, :] = matmul_tn(rows, grad_own).astype(jnp.bfloat16)
    down_out_ref[...] = downscaled.astype(jnp.bfloat16).reshape(own_rows, own_cols, 128)
    grad_tokens_ref[...] = (
        grad_tokens_s[4 : own_rows + 4, 4 : own_cols + 4, :].astype(jnp.bfloat16)
    )
    place = 1152
    for left, right, flipped in (
        (ln_one_s, grad_qkv_s, False),
        (mixed_s, grad_att_s, False),
        (ln_two_s, grad_pre_s, False),
        (hidden_s, grad_block_s, True),
    ):
        product = matmul_tn(left[...], right[...]).astype(jnp.bfloat16)
        if flipped:
            rows_s[place : place + product.shape[0], :] = product
            place = place + product.shape[0]
        else:
            for tile in range(product.shape[1] // 128):
                rows_s[place : place + 128, :] = product[:, tile * 128 : (tile + 1) * 128]
                place = place + 128
    small = [gain_one_sum, gain_two_sum] + table_rows(bias_sum)
    small.append(jnp.zeros((16 - len(small), 128), jnp.float32))
    rows_s[place : place + 16, :] = jnp.concatenate(small, axis=0).astype(jnp.bfloat16)
    place = place + 16
    rows_s[place:, :] = jnp.zeros((ROWS - place, 128), jnp.bfloat16)
    core = lax.axis_index("c")
    half = ROWS // 2
    kept_ref[...] = rows_s[pl.ds(pl.multiple_of(core * half, half), half), :]
    sent_ref[...] = rows_s[pl.ds(pl.multiple_of((1 - core) * half, half), half), :]


def per_device(
    tokens,
    grad_out,
    window_ids,
    qkv_weight,
    proj_weight,
    up_weight,
    down_weight,
    conv_weight,
    gain_one,
    gain_two,
    position_bias,
):
    row_count, col_count, width = tokens.shape
    lat_total = col_count * lax.axis_size(LAT)
    tokens_all = row_count * lat_total * lax.axis_size(LON)
    vmem = pl.BlockSpec(memory_space=pltpu.VMEM)
    params = pltpu.CompilerParams(vmem_limit_bytes=48 * 1024 * 1024)
    bf16 = lambda *shape: jax.ShapeDtypeStruct(shape, jnp.bfloat16)
    f32 = lambda *shape: jax.ShapeDtypeStruct(shape, jnp.float32)
    held = lambda *shape: pltpu.VMEM(shape, jnp.bfloat16)
    wide = lambda *shape: pltpu.VMEM(shape, jnp.float32)
    table = jnp.pad(position_bias, ((0, 0), (0, 1), (0, 1))).reshape(HEADS, 256)
    biases, gains = pl.pallas_call(
        bias_kernel,
        out_shape=(f32(AREA, HEADS * AREA), f32(WIN, width)),
        in_specs=[vmem] * 3,
        out_specs=(vmem,) * 2,
        compiler_params=params,
        cost_estimate=pl.CostEstimate(flops=10_000_000, bytes_accessed=80_000, transcendentals=0),
    )(table, gain_one[None], gain_two[None])
    slabs = TOKEN_RIM + GRAD_RIM + 1
    anywhere = pl.BlockSpec(memory_space=pltpu.HBM)
    far, near, tokens, grad_out, window_ids = pl.pallas_call(
        lon_pack_kernel,
        out_shape=(
            bf16(slabs, col_count, width),
            bf16(slabs, col_count, width),
            bf16(*tokens.shape),
            bf16(*grad_out.shape),
            jax.ShapeDtypeStruct(window_ids.shape, jnp.int32),
        ),
        in_specs=[anywhere] * 3,
        out_specs=(vmem,) * 5,
        scratch_shapes=[wide(col_count, width), pltpu.SemaphoreType.DMA((3,))],
        compiler_params=params,
    )(tokens, grad_out, window_ids)
    lon_far = swapped(far, LON, False)
    lon_near = swapped(near, LON, True)
    far, near = pl.pallas_call(
        lat_pack_kernel,
        out_shape=(bf16(MESSAGE, width),) * 2,
        in_specs=[vmem] * 5,
        out_specs=(vmem,) * 2,
        scratch_shapes=[
            wide(2, TOKEN_ROWS, WIN, width),
            wide(2, GRAD_ROWS, WIN, width),
            wide(32, width),
            wide(2, MESSAGE, width),
        ],
        compiler_params=params,
    )(tokens, grad_out, window_ids, lon_far, lon_near)
    lat_far = swapped(far, LAT, False)
    lat_near = swapped(near, LAT, True)
    count = AREA * (WIN_ROWS - 1) * (WIN_COLS - 1)
    downscaled, grad_tokens, kept, sent = pl.pallas_call(
        functools.partial(block_kernel, lat_total),
        out_shape=(
            bf16(*tokens.shape),
            bf16(*tokens.shape),
            bf16(ROWS // 2, width),
            bf16(ROWS // 2, width),
        ),
        in_specs=[vmem] * 14,
        out_specs=(vmem,) * 4,
        scratch_shapes=[
            wide(TOKEN_ROWS, 48, width),
            wide(GRAD_ROWS, 56, width),
            wide(32, width),
            held(GRAD_ROWS * PAD_COLS, 3 * width),
            held(ROWS, width),
            wide(TOKEN_ROWS, 40, width),
            wide(TOKEN_ROWS, 40, width),
            held(count, width),
            held(count, width),
            held(count, 4 * width),
            held(count, 4 * width),
            held(count, width),
            held(count, width),
            held(count, width),
            held(count, 3 * width),
            wide(2, MESSAGE, width),
        ],
        compiler_params=params,
        cost_estimate=pl.CostEstimate(
            flops=3_000_000_000, bytes_accessed=8_000_000, transcendentals=2_000_000
        ),
    )(
        tokens,
        grad_out,
        window_ids,
        lon_far,
        lon_near,
        lat_far,
        lat_near,
        biases,
        gains,
        qkv_weight,
        proj_weight,
        up_weight,
        down_weight,
        conv_weight,
    )
    own, other = total_over_devices(kept, sent, 1.0 / math.sqrt(tokens_all))
    results = pl.pallas_call(
        unpack_kernel,
        out_shape=(
            f32(width, 3 * width),
            f32(width, width),
            f32(width, 4 * width),
            f32(4 * width, width),
            f32(9, width, width),
            f32(1, width),
            f32(1, width),
            f32(SPAN, HEADS, SPAN),
        ),
        in_specs=[vmem] * 2,
        out_specs=(vmem,) * 8,
        scratch_shapes=[held(ROWS, width)],
        compiler_params=params,
    )(own, other)
    return (downscaled, grad_tokens) + results[:5] + (
        results[5][0],
        results[6][0],
        results[7].swapaxes(0, 1),
    )


def solution(mesh):
    lon_count, lat_count = mesh.devices.shape
    near = math.gcd(lon_count, 8)
    parts = (lon_count // near, near // 2, 2, 2, lat_count // 2)
    fine = Mesh(mesh.devices.reshape(parts), ("zl", "x", "c", "zh", "y"))
    grid = P(LON, LAT, None)
    return jax.shard_map(
        per_device,
        mesh=fine,
        in_specs=(grid, grid, P(LON, LAT)) + (P(),) * 8,
        out_specs=(grid, grid) + (P(),) * 8,
        check_vma=False,
    )
```

```python
import functools
import math

import jax
import jax.numpy as jnp
from jax import lax
from jax.experimental import pallas as pl
from jax.experimental.pallas import tpu as pltpu
from jax.sharding import Mesh
from jax.sharding import PartitionSpec as P

HEADS = 4
WIN = 8
SHIFT = 4
SPAN = 15
HEAD_DIM = 32
AREA = WIN * WIN
WIN_ROWS = 3
WIN_COLS = 5
PAD_COLS = 48
ROWS = 2816
TOKEN_RIM = 4
GRAD_RIM = 5
LABEL_RIM = 8

LON = ("zl", "x", "c")
LAT = ("zh", "y")
DEEP = ("zl", "zh")
TOKEN_ROWS = 24
GRAD_ROWS = 26
TOKEN_PART = TOKEN_ROWS * TOKEN_RIM
ID_PLACE = 232
MESSAGE = 240

epsilon = 1e-05


def swapped(value, axes, first):
    count = lax.axis_size(axes)
    pairs = []
    for source in range(count):
        up = (source % 2 == 0) == first
        pairs.append((source, (source + 1) % count if up else (source - 1) % count))
    return lax.ppermute(value, axes, pairs)


def place_along(axes):
    place = 0
    for axis in axes:
        place = place * lax.axis_size(axis) + lax.axis_index(axis)
    return place


def either(choice, first, second):
    return jnp.where(choice, jnp.int32(first), jnp.int32(second))


def lon_pack_kernel(fields_ref, ids_ref, far_ref, near_ref, ids_s):
    even = place_along(LON) % 2 == 0
    rows, cols = ids_ref.shape
    ids_s[...] = jnp.zeros_like(ids_s)
    ids_s[0:LABEL_RIM, 0:cols] = ids_ref[rows - LABEL_RIM :, :].astype(jnp.float32)
    ids = ids_s[...].astype(jnp.bfloat16)
    for ref, upper in ((near_ref, even), (far_ref, jnp.logical_not(even))):
        ref[0:TOKEN_RIM] = fields_ref[0, pl.ds(either(upper, rows - TOKEN_RIM, 0), TOKEN_RIM)]
        ref[TOKEN_RIM : TOKEN_RIM + GRAD_RIM] = fields_ref[
            1, pl.ds(either(upper, rows - GRAD_RIM, 0), GRAD_RIM)
        ]
        ref[TOKEN_RIM + GRAD_RIM] = ids


def lon_labels(ids_ref, lon_near_ref, lon_far_ref, even, ids_s):
    row = TOKEN_RIM + GRAD_RIM
    before = jnp.where(
        even, lon_far_ref[row].astype(jnp.float32), lon_near_ref[row].astype(jnp.float32)
    )
    ids_s[...] = jnp.zeros_like(ids_s)
    ids_s[0:LABEL_RIM, :] = before[0:LABEL_RIM]
    ids_s[LABEL_RIM : LABEL_RIM + ids_ref.shape[0], 0 : ids_ref.shape[1]] = ids_ref[...].astype(
        jnp.float32
    )


def lat_pack_kernel(
    fields_ref,
    ids_ref,
    lon_far_ref,
    lon_near_ref,
    far_ref,
    near_ref,
    tokens_s,
    grad_s,
    ids_s,
    message_s,
):
    lon_even = place_along(LON) % 2 == 0
    lat_even = place_along(LAT) % 2 == 0
    cols = fields_ref.shape[2]

    def edges(scratch, row, values):
        values = values.astype(jnp.float32)
        count = values.shape[0]
        scratch[0, pl.ds(row, count)] = values[:, 0:WIN]
        scratch[1, pl.ds(row, count)] = values[:, cols - WIN :]

    edges(tokens_s, TOKEN_RIM, fields_ref[0])
    edges(grad_s, GRAD_RIM, fields_ref[1])
    split = TOKEN_RIM + GRAD_RIM
    for ref, below in ((lon_near_ref, lon_even), (lon_far_ref, jnp.logical_not(lon_even))):
        edges(tokens_s, either(below, TOKEN_ROWS - TOKEN_RIM, 0), ref[0:TOKEN_RIM])
        edges(grad_s, either(below, GRAD_ROWS - GRAD_RIM, 0), ref[TOKEN_RIM:split])
    lon_labels(ids_ref, lon_near_ref, lon_far_ref, lon_even, ids_s)
    lane = lax.broadcasted_iota(jnp.int32, (WIN, 128), 1)
    ids = jnp.zeros((WIN, 128), jnp.float32)
    for part in range(TOKEN_ROWS // WIN):
        moved = pltpu.roll(
            ids_s[part * WIN : (part + 1) * WIN, :], (128 - (cols - WIN) + WIN * part) % 128, 1
        )
        ids = jnp.where(lane // WIN == part, moved, ids)
    for side in range(2):
        skip = side * (WIN - TOKEN_RIM)
        for row in range(TOKEN_ROWS):
            message_s[side, row * TOKEN_RIM : (row + 1) * TOKEN_RIM, :] = tokens_s[
                side, row, skip : skip + TOKEN_RIM, :
            ]
        skip = side * (WIN - GRAD_RIM)
        for row in range(GRAD_ROWS):
            first = TOKEN_PART + row * GRAD_RIM
            message_s[side, first : first + GRAD_RIM, :] = grad_s[
                side, row, skip : skip + GRAD_RIM, :
            ]
        first = TOKEN_PART + GRAD_ROWS * GRAD_RIM
        message_s[side, first:ID_PLACE, :] = jnp.zeros((ID_PLACE - first, 128), jnp.float32)
        message_s[side, ID_PLACE:, :] = ids
    near_ref[...] = message_s[either(lat_even, 1, 0)].astype(jnp.bfloat16)
    far_ref[...] = message_s[either(lat_even, 0, 1)].astype(jnp.bfloat16)


def assembled(
    fields_ref,
    ids_ref,
    lon_near_ref,
    lon_far_ref,
    lat_near_ref,
    lat_far_ref,
    tokens_s,
    grad_s,
    ids_s,
    message_s,
    first_col,
    lat_total,
):
    lon_even = place_along(LON) % 2 == 0
    lat_even = place_along(LAT) % 2 == 0
    rows, cols = ids_ref.shape
    middle = slice(WIN, WIN + cols)
    tokens_s[TOKEN_RIM : TOKEN_RIM + rows, middle, :] = fields_ref[0].astype(jnp.float32)
    grad_s[GRAD_RIM : GRAD_RIM + rows, middle, :] = fields_ref[1].astype(jnp.float32)
    split = TOKEN_RIM + GRAD_RIM
    for ref, below in ((lon_near_ref, lon_even), (lon_far_ref, jnp.logical_not(lon_even))):
        row = either(below, TOKEN_ROWS - TOKEN_RIM, 0)
        tokens_s[pl.ds(row, TOKEN_RIM), middle, :] = ref[0:TOKEN_RIM].astype(jnp.float32)
        row = either(below, GRAD_ROWS - GRAD_RIM, 0)
        grad_s[pl.ds(row, GRAD_RIM), middle, :] = ref[TOKEN_RIM:split].astype(jnp.float32)
    near, far = lat_near_ref[...].astype(jnp.float32), lat_far_ref[...].astype(jnp.float32)
    message_s[0] = jnp.where(lat_even, far, near)
    message_s[1] = jnp.where(lat_even, near, far)
    for side, token_col, grad_col in (
        (0, WIN - TOKEN_RIM, WIN - GRAD_RIM),
        (1, WIN + cols, WIN + cols),
    ):
        for row in range(TOKEN_ROWS):
            tokens_s[row, token_col : token_col + TOKEN_RIM, :] = message_s[
                side, row * TOKEN_RIM : (row + 1) * TOKEN_RIM, :
            ]
        for row in range(GRAD_ROWS):
            first = TOKEN_PART + row * GRAD_RIM
            grad_s[row, grad_col : grad_col + GRAD_RIM, :] = message_s[
                side, first : first + GRAD_RIM, :
            ]
    lon_labels(ids_ref, lon_near_ref, lon_far_ref, lon_even, ids_s)
    packed = message_s[0, ID_PLACE:, :]
    before = jnp.concatenate(
        [packed]
        + [pltpu.roll(packed, 128 - WIN * part, 1) for part in range(1, TOKEN_ROWS // WIN)]
        + [jnp.zeros_like(packed)],
        axis=0,
    )
    lane = lax.broadcasted_iota(jnp.int32, ids_s.shape, 1)
    own = pltpu.roll(ids_s[...], LABEL_RIM, 1)
    ids = jnp.where(lane < LABEL_RIM, before, own)
    shifted = first_col + lane - LABEL_RIM
    shifted = jnp.where(shifted < 0, shifted + lat_total, shifted)
    return ids * 2.0 + jnp.where(shifted >= lat_total - SHIFT, 1.0, 0.0)


def bias_rows(table_ref):
    lane = lax.broadcasted_iota(jnp.int32, (WIN, 128), 1)
    source = lax.broadcasted_iota(jnp.int32, (256, 128), 0)
    target = lax.broadcasted_iota(jnp.int32, (256, 128), 1)
    hit = jnp.logical_and(source // 16 == target // WIN, source % 16 == target % WIN)
    narrow = jnp.where(hit, 1.0, 0.0).astype(jnp.bfloat16)
    pieces = []
    for head in range(HEADS):
        table = jnp.broadcast_to(table_ref[head : head + 1, :], (WIN, 256))
        place = lax.broadcasted_iota(jnp.int32, (WIN, 256), 0)
        moved = jnp.zeros((WIN, 256), jnp.float32)
        for row in range(WIN):
            steps = (256 - (WIN - 1 - row)) % 256
            part = pltpu.roll(table, steps, 1) if steps else table
            moved = jnp.where(place == row, part, moved)
        pieces.append(moved)
    rest = jnp.concatenate(pieces, axis=0)
    packed = jnp.zeros((HEADS * WIN, 128), jnp.float32)
    for _ in range(3):
        part = rest.astype(jnp.bfloat16)
        packed = packed + matmul(part, narrow)
        rest = rest - part.astype(jnp.float32)
    rows = []
    for row in range(WIN):
        tiles = []
        for pair in range(HEADS // 2):
            halves = []
            for half in range(2):
                head = 2 * pair + half
                steps = (AREA * half - WIN * (WIN - 1 - row)) % 128
                part = packed[head * WIN : (head + 1) * WIN]
                halves.append(pltpu.roll(part, steps, 1) if steps else part)
            tiles.append(jnp.where(lane < AREA, halves[0], halves[1]))
        rows.append(jnp.concatenate(tiles, axis=1))
    return jnp.concatenate(rows, axis=0)


def bias_kernel(table_ref, gain_one_ref, gain_two_ref, bias_ref, gains_ref):
    bias_ref[...] = bias_rows(table_ref)
    gains_ref[...] = jnp.zeros_like(gains_ref)
    gains_ref[0:1, :] = gain_one_ref[...]
    gains_ref[1:2, :] = gain_two_ref[...]


def scattered_sum(partial, axes):
    count = lax.axis_size(axes)
    chunks = partial.reshape(count, -1, 4, partial.shape[-1])
    received = lax.all_to_all(chunks, axes, 0, 0, tiled=True)
    return jnp.sum(received.astype(jnp.float32), axis=0)


def spread(chunk, axes):
    count = lax.axis_size(axes)
    copies = jnp.broadcast_to(chunk[None], (count,) + chunk.shape)
    return lax.all_to_all(copies, axes, 0, 0, tiled=True)


def total_over_devices(kept, sent, grad_scale):
    cores = [(0, 1), (1, 0)]
    other = lax.ppermute(sent, "c", cores)
    own = (kept.astype(jnp.float32) + other.astype(jnp.float32)).astype(jnp.bfloat16)
    own = scattered_sum(own, ("x", "y")).astype(jnp.bfloat16)
    parts = spread(own, DEEP)
    own = (jnp.sum(parts.astype(jnp.float32), axis=0) * grad_scale).astype(jnp.bfloat16)
    own = spread(own, ("x", "y")).reshape(-1, 128)
    return own, lax.ppermute(own, "c", cores)


def unpack_kernel(
    own_ref,
    other_ref,
    qkv_ref,
    proj_ref,
    up_ref,
    down_ref,
    conv_ref,
    gain_one_ref,
    gain_two_ref,
    table_ref,
    rows_s,
):
    core = lax.axis_index("c")
    half = ROWS // 2
    rows_s[pl.ds(pl.multiple_of(core * half, half), half), :] = own_ref[...]
    rows_s[pl.ds(pl.multiple_of((1 - core) * half, half), half), :] = other_ref[...]

    def piece(first, count):
        return rows_s[first : first + count, :].astype(jnp.float32)

    conv_ref[...] = piece(0, 1152).reshape(9, 128, 128)
    place = 1152
    for ref, tiles in ((qkv_ref, 3), (proj_ref, 1), (up_ref, 4)):
        for tile in range(tiles):
            ref[:, tile * 128 : (tile + 1) * 128] = piece(place, 128)
            place = place + 128
    down_ref[...] = piece(place, 512)
    small = piece(place + 512, 16)
    gain_one_ref[...] = small[0:1]
    gain_two_ref[...] = small[1:2]
    for low in range(WIN):
        moved = pltpu.roll(small, (128 - 16 * low) % 128, 1) if low else small
        for head in range(HEADS):
            for high in range(2):
                row = high * WIN + low
                if row < SPAN:
                    line = 2 + 2 * head + high
                    table_ref[row, head : head + 1, :] = moved[line : line + 1, :SPAN]


def lane_mean(values):
    return jnp.sum(values, axis=-1, keepdims=True) * (1.0 / 128.0)


def layer_norm(values, gain):
    centred = values - lane_mean(values)
    inverse = lax.rsqrt(lane_mean(centred * centred) + epsilon)
    normed = centred * inverse
    return (normed * gain).astype(jnp.bfloat16), normed, inverse


def layer_norm_back(grad_in, normed, inverse, gain):
    scaled = grad_in * gain
    return inverse * (scaled - lane_mean(scaled) - normed * lane_mean(scaled * normed))


def matmul(left, right):
    return jnp.dot(left, right, preferred_element_type=jnp.float32)


def matmul_nt(left, right):
    return lax.dot_general(left, right, (((1,), (1,)), ((), ())), preferred_element_type=jnp.float32)


def matmul_tn(left, right):
    return lax.dot_general(left, right, (((0,), (0,)), ((), ())), preferred_element_type=jnp.float32)


def by_heads(rows, head_masks):
    return jnp.concatenate([rows * mask for mask in head_masks], axis=0)


def own_heads(stacked, head_lanes):
    total = jnp.zeros((AREA, 128), jnp.float32)
    for head in range(HEADS):
        part = stacked[head * AREA : (head + 1) * AREA]
        total = total + jnp.where(head_lanes[head], part, 0.0)
    return total


def table_rows(bias_sum):
    lane = lax.broadcasted_iota(jnp.int32, (WIN, 128), 1)
    pieces = []
    for head in range(HEADS):
        half = head % 2
        tile = bias_sum[:, (head // 2) * 128 : (head // 2 + 1) * 128]
        tile_sum = jnp.zeros((WIN, 128), jnp.float32)
        for row in range(WIN):
            part = jnp.where(lane // AREA == half, tile[row * WIN : (row + 1) * WIN], 0.0)
            steps = (WIN * (WIN - 1 - row) - AREA * half) % 128
            tile_sum = tile_sum + (pltpu.roll(part, steps, 1) if steps else part)
        pieces.append(tile_sum)
    stacked = jnp.concatenate(pieces, axis=0)
    source = lax.broadcasted_iota(jnp.int32, (128, 256), 0)
    target = lax.broadcasted_iota(jnp.int32, (128, 256), 1)
    hit = jnp.logical_and(source // WIN == target // 16, source % WIN == target % 16)
    spread_to = jnp.where(hit, 1.0, 0.0).astype(jnp.bfloat16)
    spread = jnp.zeros((HEADS * WIN, 256), jnp.float32)
    rest = stacked
    for _ in range(3):
        part = rest.astype(jnp.bfloat16)
        spread = spread + matmul(part, spread_to)
        rest = rest - part.astype(jnp.float32)
    place = lax.broadcasted_iota(jnp.int32, (HEADS * WIN, 256), 0) % WIN
    table = jnp.zeros((HEADS * WIN, 256), jnp.float32)
    for row in range(WIN):
        part = jnp.where(place == row, spread, 0.0)
        table = table + (pltpu.roll(part, WIN - 1 - row, 1) if row < WIN - 1 else part)
    rows = []
    for head in range(HEADS):
        head_sum = jnp.sum(table[head * WIN : (head + 1) * WIN], axis=0, keepdims=True)
        rows.extend([head_sum[:, :128], head_sum[:, 128:]])
    return rows


def block_kernel(
    lat_total,
    fields_ref,
    ids_ref,
    lon_far_ref,
    lon_near_ref,
    lat_far_ref,
    lat_near_ref,
    bias_ref,
    gains_ref,
    qkv_ref,
    proj_ref,
    up_ref,
    down_ref,
    conv_ref,
    down_out_ref,
    grad_tokens_ref,
    kept_ref,
    sent_ref,
    tokens_s,
    grad_s,
    ids_s,
    gcat_s,
    rows_s,
    block_out_s,
    grad_tokens_s,
    ln_one_s,
    ln_two_s,
    hidden_s,
    grad_pre_s,
    grad_block_s,
    mixed_s,
    grad_att_s,
    grad_qkv_s,
    message_s,
):
    own_rows, own_cols = ids_ref.shape
    first_col = place_along(LAT) * own_cols
    labels = assembled(
        fields_ref,
        ids_ref,
        lon_near_ref,
        lon_far_ref,
        lat_near_ref,
        lat_far_ref,
        tokens_s,
        grad_s,
        ids_s,
        message_s,
        first_col,
        lat_total,
    )
    ids_s[...] = labels
    position = first_col - TOKEN_RIM + lax.broadcasted_iota(jnp.int32, (PAD_COLS, 128), 0)
    position = jnp.where(position < 0, position + lat_total, position)
    position = jnp.where(position >= lat_total, position - lat_total, position)
    keep_after = jnp.where(position != lat_total - 1, 1.0, 0.0)
    keep_before = jnp.where(position != 0, 1.0, 0.0)
    for tap, keep in ((0, keep_after), (1, None), (2, keep_before)):
        piece = grad_s[:, 5 - tap : 5 - tap + PAD_COLS, :]
        if keep is not None:
            piece = piece * keep[None]
        gcat_s[:, tap * 128 : (tap + 1) * 128] = piece.reshape(GRAD_ROWS * PAD_COLS, 128).astype(
            jnp.bfloat16
        )
    lane_row = lax.broadcasted_iota(jnp.int32, (AREA, 128), 0)
    diagonal = (
        lax.broadcasted_iota(jnp.int32, (AREA, HEADS * AREA), 1) % AREA
        == lax.broadcasted_iota(jnp.int32, (AREA, HEADS * AREA), 0)
    )
    biases = bias_ref[...]
    gain_one, gain_two = gains_ref[0:1, :], gains_ref[1:2, :]
    lane = lax.broadcasted_iota(jnp.int32, (AREA, 128), 1)
    head_lanes = [lane // HEAD_DIM == head for head in range(HEADS)]
    head_masks = [jnp.where(hit, 1.0, 0.0).astype(jnp.bfloat16) for hit in head_lanes]
    score_scale = HEAD_DIM ** (-0.5)
    length = WIN_COLS * AREA
    bias_sum = jnp.zeros((AREA, HEADS * AREA), jnp.float32)
    gain_one_sum = jnp.zeros((1, 128), jnp.float32)
    gain_two_sum = jnp.zeros((1, 128), jnp.float32)
    def chunk_steps(chunk):
        nonlocal bias_sum, gain_one_sum, gain_two_sum
        top = chunk * WIN
        source = jnp.concatenate(
            [
                tokens_s[top : top + WIN, 4 + win * WIN : 12 + win * WIN, :].reshape(AREA, 128)
                for win in range(WIN_COLS)
            ],
            axis=0,
        )
        label_rows = jnp.concatenate(
            [
                jnp.broadcast_to(ids_s[top + row : top + row + 1, :], (WIN, 128))
                for row in range(WIN)
            ],
            axis=0,
        )
        ln_one, normed_one, inverse_one = layer_norm(source, gain_one)
        yield
        qkv_all = matmul(ln_one, qkv_ref[...]).astype(jnp.bfloat16)
        yield
        grad_grid = jnp.zeros((WIN * PAD_COLS, 128), jnp.float32)
        for tap in range(3):
            first = (top + 2 - tap) * PAD_COLS
            taps = jnp.concatenate([conv_ref[3 * tap + side] for side in range(3)], axis=1)
            grad_grid = grad_grid + matmul_nt(gcat_s[first : first + WIN * PAD_COLS, :], taps)
        grad_grid = grad_grid.reshape(WIN, PAD_COLS, 128)
        grad_block = jnp.concatenate(
            [
                grad_grid[:, win * WIN : (win + 1) * WIN, :].reshape(AREA, 128)
                for win in range(WIN_COLS)
            ],
            axis=0,
        )
        saved, mixed_parts = [], []
        raw = []
        for win in range(WIN_COLS):
            part = qkv_all[win * AREA : (win + 1) * AREA]
            query, key, value = part[:, :128], part[:, 128:256], part[:, 256:]
            query_heads = by_heads(query, head_masks)
            picked = jnp.where(lane == win * WIN + lane_row % WIN, label_rows, 0.0)
            column = jnp.broadcast_to(
                jnp.sum(picked, axis=1, keepdims=True), (AREA, HEADS * AREA)
            )
            across = jnp.sum(jnp.where(diagonal, column, 0.0), axis=0, keepdims=True)
            scores = matmul_nt(key, query_heads) * score_scale + biases
            scores = jnp.where(column == across, scores, -1e30)
            raw.append((query_heads, key, value, scores))
        yield
        for query_heads, key, value, scores in raw:
            raised = jnp.exp(scores - jnp.max(scores, axis=0, keepdims=True))
            probabilities = raised * (1.0 / jnp.sum(raised, axis=0, keepdims=True))
            saved.append((query_heads, key, value, probabilities, probabilities.astype(jnp.bfloat16)))
        yield
        for query_heads, key, value, probabilities, weights in saved:
            mixed_parts.append(own_heads(matmul_tn(weights, value), head_lanes).astype(jnp.bfloat16))
        yield
        mixed = jnp.concatenate(mixed_parts, axis=0)
        projected = matmul(mixed, proj_ref[...]).astype(jnp.bfloat16)
        yield
        middle = source + projected.astype(jnp.float32)
        ln_two, normed_two, inverse_two = layer_norm(middle, gain_two)
        yield
        pre_act = matmul(ln_two, up_ref[...])
        yield
        cumulative = 0.5 * (1.0 + lax.erf(pre_act * 0.7071067811865476))
        hidden = (pre_act * cumulative).astype(jnp.bfloat16)
        slope = cumulative + pre_act * (jnp.exp(-0.5 * pre_act * pre_act) * 0.3989422804014327)
        yield
        block_out = (middle + matmul(hidden, down_ref[...])).astype(jnp.bfloat16).astype(jnp.float32)
        for win in range(WIN_COLS):
            piece = block_out[win * AREA : (win + 1) * AREA].reshape(WIN, WIN, 128)
            block_out_s[top : top + WIN, win * WIN : (win + 1) * WIN, :] = piece

        yield
        grad_block_b = grad_block.astype(jnp.bfloat16)
        grad_hidden = matmul_nt(grad_block_b, down_ref[...])
        yield
        grad_pre = (grad_hidden * slope).astype(jnp.bfloat16)
        grad_ln_two = matmul_nt(grad_pre, up_ref[...])
        yield
        grad_middle = grad_block + layer_norm_back(grad_ln_two, normed_two, inverse_two, gain_two)
        grad_att = grad_middle.astype(jnp.bfloat16)
        yield
        grad_mixed = matmul_nt(grad_att, proj_ref[...]).astype(jnp.bfloat16)
        yield
        grad_parts, steps_back = [], []
        for win in range(WIN_COLS):
            query_heads, key, value, probabilities, weights = saved[win]
            grad_heads = by_heads(grad_mixed[win * AREA : (win + 1) * AREA], head_masks)
            grad_probs = matmul_nt(value, grad_heads)
            grad_value = matmul(weights, grad_heads)
            steps_back.append((grad_probs, grad_value))
        yield
        grads = []
        for win in range(WIN_COLS):
            probabilities = saved[win][3]
            grad_probs = steps_back[win][0]
            centre = jnp.sum(probabilities * grad_probs, axis=0, keepdims=True)
            grad_scores = probabilities * (grad_probs - centre)
            if chunk and win:
                bias_sum = bias_sum + grad_scores
            grads.append(grad_scores.astype(jnp.bfloat16))
        yield
        for win in range(WIN_COLS):
            query_heads, key = saved[win][:2]
            grad_key = matmul(grads[win], query_heads) * score_scale
            grad_query = own_heads(matmul_tn(grads[win], key), head_lanes) * score_scale
            grad_parts.append(
                jnp.concatenate([grad_query, grad_key, steps_back[win][1]], axis=1).astype(
                    jnp.bfloat16
                )
            )
        yield
        grad_qkv = jnp.concatenate(grad_parts, axis=0)
        grad_ln_one = matmul_nt(grad_qkv, qkv_ref[...])
        yield
        grad_tokens = grad_middle + layer_norm_back(grad_ln_one, normed_one, inverse_one, gain_one)
        for win in range(WIN_COLS):
            piece = grad_tokens[win * AREA : (win + 1) * AREA].reshape(WIN, WIN, 128)
            grad_tokens_s[top : top + WIN, win * WIN : (win + 1) * WIN, :] = piece
        if chunk:
            gain_one_sum = gain_one_sum + jnp.sum(
                (grad_ln_one * normed_one)[AREA:], axis=0, keepdims=True
            )
            gain_two_sum = gain_two_sum + jnp.sum(
                (grad_ln_two * normed_two)[AREA:], axis=0, keepdims=True
            )
            kept = slice((chunk - 1) * (length - AREA), chunk * (length - AREA))
            ln_one_s[kept, :] = ln_one[AREA:]
            ln_two_s[kept, :] = ln_two[AREA:]
            hidden_s[kept, :] = hidden[AREA:]
            grad_pre_s[kept, :] = grad_pre[AREA:]
            grad_block_s[kept, :] = grad_block_b[AREA:]
            mixed_s[kept, :] = mixed[AREA:]
            grad_att_s[kept, :] = grad_att[AREA:]
            grad_qkv_s[kept, :] = grad_qkv[AREA:]


    running = [chunk_steps(chunk) for chunk in range(WIN_ROWS)]
    while running:
        running = [steps for steps in running if next(steps, running) is not running]

    col = first_col + lax.broadcasted_iota(jnp.int32, (own_cols, 128), 0)
    keeps = (col != 0, None, col != lat_total - 1)
    shifted = []
    for tap in range(3):
        piece = block_out_s[3 : own_rows + 5, 3 + tap : 3 + tap + own_cols, :]
        if keeps[tap] is not None:
            piece = piece * jnp.where(keeps[tap], 1.0, 0.0)[None]
        shifted.append(piece.reshape((own_rows + 2) * own_cols, 128).astype(jnp.bfloat16))
    patches = jnp.concatenate(shifted, axis=1)
    count = own_rows * own_cols
    downscaled = jnp.zeros((count, 128), jnp.float32)
    grad_own = fields_ref[1].reshape(count, 128)
    for tap in range(3):
        rows = patches[tap * own_cols : tap * own_cols + count]
        downscaled = downscaled + matmul(rows, conv_ref[3 * tap : 3 * tap + 3].reshape(384, 128))
        rows_s[tap * 384 : (tap + 1) * 384, :] = matmul_tn(rows, grad_own).astype(jnp.bfloat16)
    down_out_ref[...] = downscaled.astype(jnp.bfloat16).reshape(own_rows, own_cols, 128)
    grad_tokens_ref[...] = (
        grad_tokens_s[4 : own_rows + 4, 4 : own_cols + 4, :].astype(jnp.bfloat16)
    )
    place = 1152
    for left, right, flipped in (
        (ln_one_s, grad_qkv_s, False),
        (mixed_s, grad_att_s, False),
        (ln_two_s, grad_pre_s, False),
        (hidden_s, grad_block_s, True),
    ):
        product = matmul_tn(left[...], right[...]).astype(jnp.bfloat16)
        if flipped:
            rows_s[place : place + product.shape[0], :] = product
            place = place + product.shape[0]
        else:
            for tile in range(product.shape[1] // 128):
                rows_s[place : place + 128, :] = product[:, tile * 128 : (tile + 1) * 128]
                place = place + 128
    small = [gain_one_sum, gain_two_sum] + table_rows(bias_sum)
    small.append(jnp.zeros((16 - len(small), 128), jnp.float32))
    rows_s[place : place + 16, :] = jnp.concatenate(small, axis=0).astype(jnp.bfloat16)
    place = place + 16
    rows_s[place:, :] = jnp.zeros((ROWS - place, 128), jnp.bfloat16)
    core = lax.axis_index("c")
    half = ROWS // 2
    kept_ref[...] = rows_s[pl.ds(pl.multiple_of(core * half, half), half), :]
    sent_ref[...] = rows_s[pl.ds(pl.multiple_of((1 - core) * half, half), half), :]


def per_device(
    tokens,
    grad_out,
    window_ids,
    qkv_weight,
    proj_weight,
    up_weight,
    down_weight,
    conv_weight,
    gain_one,
    gain_two,
    position_bias,
):
    row_count, col_count, width = tokens.shape
    lat_total = col_count * lax.axis_size(LAT)
    tokens_all = row_count * lat_total * lax.axis_size(LON)
    vmem = pl.BlockSpec(memory_space=pltpu.VMEM)
    params = pltpu.CompilerParams(vmem_limit_bytes=48 * 1024 * 1024)
    bf16 = lambda *shape: jax.ShapeDtypeStruct(shape, jnp.bfloat16)
    f32 = lambda *shape: jax.ShapeDtypeStruct(shape, jnp.float32)
    held = lambda *shape: pltpu.VMEM(shape, jnp.bfloat16)
    wide = lambda *shape: pltpu.VMEM(shape, jnp.float32)
    table = jnp.pad(position_bias, ((0, 0), (0, 1), (0, 1))).reshape(HEADS, 256)
    biases, gains = pl.pallas_call(
        bias_kernel,
        out_shape=(f32(AREA, HEADS * AREA), f32(WIN, width)),
        in_specs=[vmem] * 3,
        out_specs=(vmem,) * 2,
        compiler_params=params,
        cost_estimate=pl.CostEstimate(flops=10_000_000, bytes_accessed=80_000, transcendentals=0),
    )(table, gain_one[None], gain_two[None])
    slabs = TOKEN_RIM + GRAD_RIM + 1
    fields = jnp.stack([tokens, grad_out])
    far, near = pl.pallas_call(
        lon_pack_kernel,
        out_shape=(bf16(slabs, col_count, width),) * 2,
        in_specs=[vmem] * 2,
        out_specs=(vmem,) * 2,
        scratch_shapes=[wide(col_count, width)],
        compiler_params=params,
    )(fields, window_ids)
    lon_far = swapped(far, LON, False)
    lon_near = swapped(near, LON, True)
    far, near = pl.pallas_call(
        lat_pack_kernel,
        out_shape=(bf16(MESSAGE, width),) * 2,
        in_specs=[vmem] * 4,
        out_specs=(vmem,) * 2,
        scratch_shapes=[
            wide(2, TOKEN_ROWS, WIN, width),
            wide(2, GRAD_ROWS, WIN, width),
            wide(32, width),
            wide(2, MESSAGE, width),
        ],
        compiler_params=params,
    )(fields, window_ids, lon_far, lon_near)
    lat_far = swapped(far, LAT, False)
    lat_near = swapped(near, LAT, True)
    count = AREA * (WIN_ROWS - 1) * (WIN_COLS - 1)
    downscaled, grad_tokens, kept, sent = pl.pallas_call(
        functools.partial(block_kernel, lat_total),
        out_shape=(
            bf16(*tokens.shape),
            bf16(*tokens.shape),
            bf16(ROWS // 2, width),
            bf16(ROWS // 2, width),
        ),
        in_specs=[vmem] * 13,
        out_specs=(vmem,) * 4,
        scratch_shapes=[
            wide(TOKEN_ROWS, 48, width),
            wide(GRAD_ROWS, 56, width),
            wide(32, width),
            held(GRAD_ROWS * PAD_COLS, 3 * width),
            held(ROWS, width),
            wide(TOKEN_ROWS, 40, width),
            wide(TOKEN_ROWS, 40, width),
            held(count, width),
            held(count, width),
            held(count, 4 * width),
            held(count, 4 * width),
            held(count, width),
            held(count, width),
            held(count, width),
            held(count, 3 * width),
            wide(2, MESSAGE, width),
        ],
        compiler_params=params,
        cost_estimate=pl.CostEstimate(
            flops=3_000_000_000, bytes_accessed=8_000_000, transcendentals=2_000_000
        ),
    )(
        fields,
        window_ids,
        lon_far,
        lon_near,
        lat_far,
        lat_near,
        biases,
        gains,
        qkv_weight,
        proj_weight,
        up_weight,
        down_weight,
        conv_weight,
    )
    own, other = total_over_devices(kept, sent, 1.0 / math.sqrt(tokens_all))
    results = pl.pallas_call(
        unpack_kernel,
        out_shape=(
            f32(width, 3 * width),
            f32(width, width),
            f32(width, 4 * width),
            f32(4 * width, width),
            f32(9, width, width),
            f32(1, width),
            f32(1, width),
            f32(SPAN, HEADS, SPAN),
        ),
        in_specs=[vmem] * 2,
        out_specs=(vmem,) * 8,
        scratch_shapes=[held(ROWS, width)],
        compiler_params=params,
    )(own, other)
    return (downscaled, grad_tokens) + results[:5] + (
        results[5][0],
        results[6][0],
        results[7].swapaxes(0, 1),
    )


def solution(mesh):
    lon_count, lat_count = mesh.devices.shape
    near = math.gcd(lon_count, 8)
    parts = (lon_count // near, near // 2, 2, 2, lat_count // 2)
    fine = Mesh(mesh.devices.reshape(parts), ("zl", "x", "c", "zh", "y"))
    grid = P(LON, LAT, None)
    return jax.shard_map(
        per_device,
        mesh=fine,
        in_specs=(grid, grid, P(LON, LAT)) + (P(),) * 8,
        out_specs=(grid, grid) + (P(),) * 8,
        check_vma=False,
    )
```

```python
import functools
import math

import jax
import jax.numpy as jnp
from jax import lax
from jax.experimental import pallas as pl
from jax.experimental.pallas import tpu as pltpu
from jax.sharding import Mesh
from jax.sharding import PartitionSpec as P

HEADS = 4
WIN = 8
SHIFT = 4
SPAN = 15
HEAD_DIM = 32
AREA = WIN * WIN
WIN_ROWS = 3
WIN_COLS = 5
PAD_COLS = 48
ROWS = 2816
TOKEN_RIM = 4
GRAD_RIM = 5
LABEL_RIM = 8

LON = ("zl", "x", "c")
LAT = ("zh", "y")
DEEP = ("zl", "zh")
TOKEN_ROWS = 24
GRAD_ROWS = 26
TOKEN_PART = TOKEN_ROWS * TOKEN_RIM
ID_PLACE = 232
MESSAGE = 240

epsilon = 1e-05


def swapped(value, axes, first):
    count = lax.axis_size(axes)
    pairs = []
    for source in range(count):
        up = (source % 2 == 0) == first
        pairs.append((source, (source + 1) % count if up else (source - 1) % count))
    return lax.ppermute(value, axes, pairs)


def place_along(axes):
    place = 0
    for axis in axes:
        place = place * lax.axis_size(axis) + lax.axis_index(axis)
    return place


def either(choice, first, second):
    return jnp.where(choice, jnp.int32(first), jnp.int32(second))


def lon_pack_kernel(fields_ref, ids_ref, far_ref, near_ref, ids_s):
    even = place_along(LON) % 2 == 0
    rows, cols = ids_ref.shape
    ids_s[...] = jnp.zeros_like(ids_s)
    ids_s[0:LABEL_RIM, 0:cols] = ids_ref[rows - LABEL_RIM :, :].astype(jnp.float32)
    ids = ids_s[...].astype(jnp.bfloat16)
    for ref, upper in ((near_ref, even), (far_ref, jnp.logical_not(even))):
        ref[0:TOKEN_RIM] = fields_ref[0, pl.ds(either(upper, rows - TOKEN_RIM, 0), TOKEN_RIM)]
        ref[TOKEN_RIM : TOKEN_RIM + GRAD_RIM] = fields_ref[
            1, pl.ds(either(upper, rows - GRAD_RIM, 0), GRAD_RIM)
        ]
        ref[TOKEN_RIM + GRAD_RIM] = ids


def lon_labels(ids_ref, lon_near_ref, lon_far_ref, even, ids_s):
    row = TOKEN_RIM + GRAD_RIM
    before = jnp.where(
        even, lon_far_ref[row].astype(jnp.float32), lon_near_ref[row].astype(jnp.float32)
    )
    ids_s[...] = jnp.zeros_like(ids_s)
    ids_s[0:LABEL_RIM, :] = before[0:LABEL_RIM]
    ids_s[LABEL_RIM : LABEL_RIM + ids_ref.shape[0], 0 : ids_ref.shape[1]] = ids_ref[...].astype(
        jnp.float32
    )


def lat_pack_kernel(
    fields_ref,
    ids_ref,
    lon_far_ref,
    lon_near_ref,
    far_ref,
    near_ref,
    tokens_s,
    grad_s,
    ids_s,
    message_s,
):
    lon_even = place_along(LON) % 2 == 0
    lat_even = place_along(LAT) % 2 == 0
    cols = fields_ref.shape[2]

    def edges(scratch, row, values):
        values = values.astype(jnp.float32)
        count = values.shape[0]
        scratch[0, pl.ds(row, count)] = values[:, 0:WIN]
        scratch[1, pl.ds(row, count)] = values[:, cols - WIN :]

    edges(tokens_s, TOKEN_RIM, fields_ref[0])
    edges(grad_s, GRAD_RIM, fields_ref[1])
    split = TOKEN_RIM + GRAD_RIM
    for ref, below in ((lon_near_ref, lon_even), (lon_far_ref, jnp.logical_not(lon_even))):
        edges(tokens_s, either(below, TOKEN_ROWS - TOKEN_RIM, 0), ref[0:TOKEN_RIM])
        edges(grad_s, either(below, GRAD_ROWS - GRAD_RIM, 0), ref[TOKEN_RIM:split])
    lon_labels(ids_ref, lon_near_ref, lon_far_ref, lon_even, ids_s)
    lane = lax.broadcasted_iota(jnp.int32, (WIN, 128), 1)
    ids = jnp.zeros((WIN, 128), jnp.float32)
    for part in range(TOKEN_ROWS // WIN):
        moved = pltpu.roll(
            ids_s[part * WIN : (part + 1) * WIN, :], (128 - (cols - WIN) + WIN * part) % 128, 1
        )
        ids = jnp.where(lane // WIN == part, moved, ids)
    for side in range(2):
        skip = side * (WIN - TOKEN_RIM)
        for row in range(TOKEN_ROWS):
            message_s[side, row * TOKEN_RIM : (row + 1) * TOKEN_RIM, :] = tokens_s[
                side, row, skip : skip + TOKEN_RIM, :
            ]
        skip = side * (WIN - GRAD_RIM)
        for row in range(GRAD_ROWS):
            first = TOKEN_PART + row * GRAD_RIM
            message_s[side, first : first + GRAD_RIM, :] = grad_s[
                side, row, skip : skip + GRAD_RIM, :
            ]
        first = TOKEN_PART + GRAD_ROWS * GRAD_RIM
        message_s[side, first:ID_PLACE, :] = jnp.zeros((ID_PLACE - first, 128), jnp.float32)
        message_s[side, ID_PLACE:, :] = ids
    near_ref[...] = message_s[either(lat_even, 1, 0)].astype(jnp.bfloat16)
    far_ref[...] = message_s[either(lat_even, 0, 1)].astype(jnp.bfloat16)


def assembled(
    fields_ref,
    ids_ref,
    lon_near_ref,
    lon_far_ref,
    lat_near_ref,
    lat_far_ref,
    tokens_s,
    grad_s,
    ids_s,
    message_s,
    first_col,
    lat_total,
):
    lon_even = place_along(LON) % 2 == 0
    lat_even = place_along(LAT) % 2 == 0
    rows, cols = ids_ref.shape
    middle = slice(WIN, WIN + cols)
    tokens_s[TOKEN_RIM : TOKEN_RIM + rows, middle, :] = fields_ref[0].astype(jnp.float32)
    grad_s[GRAD_RIM : GRAD_RIM + rows, middle, :] = fields_ref[1].astype(jnp.float32)
    split = TOKEN_RIM + GRAD_RIM
    for ref, below in ((lon_near_ref, lon_even), (lon_far_ref, jnp.logical_not(lon_even))):
        row = either(below, TOKEN_ROWS - TOKEN_RIM, 0)
        tokens_s[pl.ds(row, TOKEN_RIM), middle, :] = ref[0:TOKEN_RIM].astype(jnp.float32)
        row = either(below, GRAD_ROWS - GRAD_RIM, 0)
        grad_s[pl.ds(row, GRAD_RIM), middle, :] = ref[TOKEN_RIM:split].astype(jnp.float32)
    near, far = lat_near_ref[...].astype(jnp.float32), lat_far_ref[...].astype(jnp.float32)
    message_s[0] = jnp.where(lat_even, far, near)
    message_s[1] = jnp.where(lat_even, near, far)
    for side, token_col, grad_col in (
        (0, WIN - TOKEN_RIM, WIN - GRAD_RIM),
        (1, WIN + cols, WIN + cols),
    ):
        for row in range(TOKEN_ROWS):
            tokens_s[row, token_col : token_col + TOKEN_RIM, :] = message_s[
                side, row * TOKEN_RIM : (row + 1) * TOKEN_RIM, :
            ]
        for row in range(GRAD_ROWS):
            first = TOKEN_PART + row * GRAD_RIM
            grad_s[row, grad_col : grad_col + GRAD_RIM, :] = message_s[
                side, first : first + GRAD_RIM, :
            ]
    lon_labels(ids_ref, lon_near_ref, lon_far_ref, lon_even, ids_s)
    packed = message_s[0, ID_PLACE:, :]
    before = jnp.concatenate(
        [packed]
        + [pltpu.roll(packed, 128 - WIN * part, 1) for part in range(1, TOKEN_ROWS // WIN)]
        + [jnp.zeros_like(packed)],
        axis=0,
    )
    lane = lax.broadcasted_iota(jnp.int32, ids_s.shape, 1)
    own = pltpu.roll(ids_s[...], LABEL_RIM, 1)
    ids = jnp.where(lane < LABEL_RIM, before, own)
    shifted = first_col + lane - LABEL_RIM
    shifted = jnp.where(shifted < 0, shifted + lat_total, shifted)
    return ids * 2.0 + jnp.where(shifted >= lat_total - SHIFT, 1.0, 0.0)


def bias_rows(table_ref):
    lane = lax.broadcasted_iota(jnp.int32, (WIN, 128), 1)
    source = lax.broadcasted_iota(jnp.int32, (256, 128), 0)
    target = lax.broadcasted_iota(jnp.int32, (256, 128), 1)
    hit = jnp.logical_and(source // 16 == target // WIN, source % 16 == target % WIN)
    narrow = jnp.where(hit, 1.0, 0.0).astype(jnp.bfloat16)
    pieces = []
    for head in range(HEADS):
        table = jnp.broadcast_to(table_ref[head : head + 1, :], (WIN, 256))
        place = lax.broadcasted_iota(jnp.int32, (WIN, 256), 0)
        moved = jnp.zeros((WIN, 256), jnp.float32)
        for row in range(WIN):
            steps = (256 - (WIN - 1 - row)) % 256
            part = pltpu.roll(table, steps, 1) if steps else table
            moved = jnp.where(place == row, part, moved)
        pieces.append(moved)
    rest = jnp.concatenate(pieces, axis=0)
    packed = jnp.zeros((HEADS * WIN, 128), jnp.float32)
    for _ in range(3):
        part = rest.astype(jnp.bfloat16)
        packed = packed + matmul(part, narrow)
        rest = rest - part.astype(jnp.float32)
    rows = []
    for row in range(WIN):
        tiles = []
        for pair in range(HEADS // 2):
            halves = []
            for half in range(2):
                head = 2 * pair + half
                steps = (AREA * half - WIN * (WIN - 1 - row)) % 128
                part = packed[head * WIN : (head + 1) * WIN]
                halves.append(pltpu.roll(part, steps, 1) if steps else part)
            tiles.append(jnp.where(lane < AREA, halves[0], halves[1]))
        rows.append(jnp.concatenate(tiles, axis=1))
    return jnp.concatenate(rows, axis=0)


def bias_kernel(table_ref, gain_one_ref, gain_two_ref, bias_ref, gains_ref):
    bias_ref[...] = bias_rows(table_ref)
    gains_ref[...] = jnp.zeros_like(gains_ref)
    gains_ref[0:1, :] = gain_one_ref[...]
    gains_ref[1:2, :] = gain_two_ref[...]


def scattered_sum(partial, axes):
    count = lax.axis_size(axes)
    chunks = partial.reshape(count, -1, 4, partial.shape[-1])
    received = lax.all_to_all(chunks, axes, 0, 0, tiled=True)
    return jnp.sum(received.astype(jnp.float32), axis=0)


def spread(chunk, axes):
    count = lax.axis_size(axes)
    copies = jnp.broadcast_to(chunk[None], (count,) + chunk.shape)
    return lax.all_to_all(copies, axes, 0, 0, tiled=True)


def total_over_devices(kept, sent, grad_scale):
    cores = [(0, 1), (1, 0)]
    other = lax.ppermute(sent, "c", cores)
    own = (kept.astype(jnp.float32) + other.astype(jnp.float32)).astype(jnp.bfloat16)
    own = scattered_sum(own, ("x", "y")).astype(jnp.bfloat16)
    parts = spread(own, DEEP)
    own = (jnp.sum(parts.astype(jnp.float32), axis=0) * grad_scale).astype(jnp.bfloat16)
    own = spread(own, ("x", "y")).reshape(-1, 128)
    return own, lax.ppermute(own, "c", cores)


def unpack_kernel(
    own_ref,
    other_ref,
    qkv_ref,
    proj_ref,
    up_ref,
    down_ref,
    conv_ref,
    gain_one_ref,
    gain_two_ref,
    table_ref,
    rows_s,
):
    core = lax.axis_index("c")
    half = ROWS // 2
    rows_s[pl.ds(pl.multiple_of(core * half, half), half), :] = own_ref[...]
    rows_s[pl.ds(pl.multiple_of((1 - core) * half, half), half), :] = other_ref[...]

    def piece(first, count):
        return rows_s[first : first + count, :].astype(jnp.float32)

    conv_ref[...] = piece(0, 1152).reshape(9, 128, 128)
    place = 1152
    for ref, tiles in ((qkv_ref, 3), (proj_ref, 1), (up_ref, 4)):
        for tile in range(tiles):
            ref[:, tile * 128 : (tile + 1) * 128] = piece(place, 128)
            place = place + 128
    down_ref[...] = piece(place, 512)
    small = piece(place + 512, 16)
    gain_one_ref[...] = small[0:1]
    gain_two_ref[...] = small[1:2]
    for low in range(WIN):
        moved = pltpu.roll(small, (128 - 16 * low) % 128, 1) if low else small
        for head in range(HEADS):
            for high in range(2):
                row = high * WIN + low
                if row < SPAN:
                    line = 2 + 2 * head + high
                    table_ref[row, head : head + 1, :] = moved[line : line + 1, :SPAN]


def lane_mean(values):
    return jnp.sum(values, axis=-1, keepdims=True) * (1.0 / 128.0)


def layer_norm(values, gain):
    centred = values - lane_mean(values)
    inverse = lax.rsqrt(lane_mean(centred * centred) + epsilon)
    normed = centred * inverse
    return (normed * gain).astype(jnp.bfloat16), normed, inverse


def layer_norm_back(grad_in, normed, inverse, gain):
    scaled = grad_in * gain
    return inverse * (scaled - lane_mean(scaled) - normed * lane_mean(scaled * normed))


def matmul(left, right):
    return jnp.dot(left, right, preferred_element_type=jnp.float32)


def matmul_nt(left, right):
    return lax.dot_general(left, right, (((1,), (1,)), ((), ())), preferred_element_type=jnp.float32)


def matmul_tn(left, right):
    return lax.dot_general(left, right, (((0,), (0,)), ((), ())), preferred_element_type=jnp.float32)


def by_heads(rows, head_masks):
    return jnp.concatenate([rows * mask for mask in head_masks], axis=0)


def own_heads(stacked, head_lanes):
    total = jnp.zeros((AREA, 128), jnp.float32)
    for head in range(HEADS):
        part = stacked[head * AREA : (head + 1) * AREA]
        total = total + jnp.where(head_lanes[head], part, 0.0)
    return total


def table_rows(bias_sum):
    lane = lax.broadcasted_iota(jnp.int32, (WIN, 128), 1)
    pieces = []
    for head in range(HEADS):
        half = head % 2
        tile = bias_sum[:, (head // 2) * 128 : (head // 2 + 1) * 128]
        tile_sum = jnp.zeros((WIN, 128), jnp.float32)
        for row in range(WIN):
            part = jnp.where(lane // AREA == half, tile[row * WIN : (row + 1) * WIN], 0.0)
            steps = (WIN * (WIN - 1 - row) - AREA * half) % 128
            tile_sum = tile_sum + (pltpu.roll(part, steps, 1) if steps else part)
        pieces.append(tile_sum)
    stacked = jnp.concatenate(pieces, axis=0)
    source = lax.broadcasted_iota(jnp.int32, (128, 256), 0)
    target = lax.broadcasted_iota(jnp.int32, (128, 256), 1)
    hit = jnp.logical_and(source // WIN == target // 16, source % WIN == target % 16)
    spread_to = jnp.where(hit, 1.0, 0.0).astype(jnp.bfloat16)
    spread = jnp.zeros((HEADS * WIN, 256), jnp.float32)
    rest = stacked
    for _ in range(3):
        part = rest.astype(jnp.bfloat16)
        spread = spread + matmul(part, spread_to)
        rest = rest - part.astype(jnp.float32)
    place = lax.broadcasted_iota(jnp.int32, (HEADS * WIN, 256), 0) % WIN
    table = jnp.zeros((HEADS * WIN, 256), jnp.float32)
    for row in range(WIN):
        part = jnp.where(place == row, spread, 0.0)
        table = table + (pltpu.roll(part, WIN - 1 - row, 1) if row < WIN - 1 else part)
    rows = []
    for head in range(HEADS):
        head_sum = jnp.sum(table[head * WIN : (head + 1) * WIN], axis=0, keepdims=True)
        rows.extend([head_sum[:, :128], head_sum[:, 128:]])
    return rows


def shifted_columns(grid_ref, first_col, lat_total, own_rows, own_cols):
    col = first_col + lax.broadcasted_iota(jnp.int32, (own_cols, 128), 0)
    keeps = (col != 0, None, col != lat_total - 1)
    shifted = []
    for tap in range(3):
        piece = grid_ref[3 : own_rows + 5, 3 + tap : 3 + tap + own_cols, :]
        if keeps[tap] is not None:
            piece = piece * jnp.where(keeps[tap], 1.0, 0.0)[None]
        shifted.append(piece.reshape((own_rows + 2) * own_cols, 128).astype(jnp.bfloat16))
    return jnp.concatenate(shifted, axis=1)


def finish_kernel(lat_total, block_out_ref, grad_grid_ref, conv_ref, down_out_ref, grad_tokens_ref):
    own_rows, own_cols = down_out_ref.shape[0], down_out_ref.shape[1]
    first_col = place_along(LAT) * own_cols
    patches = shifted_columns(block_out_ref, first_col, lat_total, own_rows, own_cols)
    count = own_rows * own_cols
    downscaled = jnp.zeros((count, 128), jnp.float32)
    for tap in range(3):
        rows = patches[tap * own_cols : tap * own_cols + count]
        downscaled = downscaled + matmul(rows, conv_ref[3 * tap : 3 * tap + 3].reshape(384, 128))
    down_out_ref[...] = downscaled.astype(jnp.bfloat16).reshape(own_rows, own_cols, 128)
    grad_tokens_ref[...] = grad_grid_ref[4 : own_rows + 4, 4 : own_cols + 4, :].astype(jnp.bfloat16)


def block_kernel(
    lat_total,
    fields_ref,
    ids_ref,
    lon_far_ref,
    lon_near_ref,
    lat_far_ref,
    lat_near_ref,
    bias_ref,
    gains_ref,
    qkv_ref,
    proj_ref,
    up_ref,
    down_ref,
    conv_ref,
    block_out_s,
    grad_tokens_s,
    kept_ref,
    sent_ref,
    tokens_s,
    grad_s,
    ids_s,
    gcat_s,
    rows_s,
    ln_one_s,
    ln_two_s,
    hidden_s,
    grad_pre_s,
    grad_block_s,
    mixed_s,
    grad_att_s,
    grad_qkv_s,
    message_s,
):
    own_rows, own_cols = ids_ref.shape
    first_col = place_along(LAT) * own_cols
    labels = assembled(
        fields_ref,
        ids_ref,
        lon_near_ref,
        lon_far_ref,
        lat_near_ref,
        lat_far_ref,
        tokens_s,
        grad_s,
        ids_s,
        message_s,
        first_col,
        lat_total,
    )
    ids_s[...] = labels
    position = first_col - TOKEN_RIM + lax.broadcasted_iota(jnp.int32, (PAD_COLS, 128), 0)
    position = jnp.where(position < 0, position + lat_total, position)
    position = jnp.where(position >= lat_total, position - lat_total, position)
    keep_after = jnp.where(position != lat_total - 1, 1.0, 0.0)
    keep_before = jnp.where(position != 0, 1.0, 0.0)
    for tap, keep in ((0, keep_after), (1, None), (2, keep_before)):
        piece = grad_s[:, 5 - tap : 5 - tap + PAD_COLS, :]
        if keep is not None:
            piece = piece * keep[None]
        gcat_s[:, tap * 128 : (tap + 1) * 128] = piece.reshape(GRAD_ROWS * PAD_COLS, 128).astype(
            jnp.bfloat16
        )
    lane_row = lax.broadcasted_iota(jnp.int32, (AREA, 128), 0)
    diagonal = (
        lax.broadcasted_iota(jnp.int32, (AREA, HEADS * AREA), 1) % AREA
        == lax.broadcasted_iota(jnp.int32, (AREA, HEADS * AREA), 0)
    )
    biases = bias_ref[...]
    gain_one, gain_two = gains_ref[0:1, :], gains_ref[1:2, :]
    lane = lax.broadcasted_iota(jnp.int32, (AREA, 128), 1)
    head_lanes = [lane // HEAD_DIM == head for head in range(HEADS)]
    head_masks = [jnp.where(hit, 1.0, 0.0).astype(jnp.bfloat16) for hit in head_lanes]
    score_scale = HEAD_DIM ** (-0.5)
    length = WIN_COLS * AREA
    bias_sum = jnp.zeros((AREA, HEADS * AREA), jnp.float32)
    gain_one_sum = jnp.zeros((1, 128), jnp.float32)
    gain_two_sum = jnp.zeros((1, 128), jnp.float32)
    def chunk_steps(chunk):
        nonlocal bias_sum, gain_one_sum, gain_two_sum
        top = chunk * WIN
        source = jnp.concatenate(
            [
                tokens_s[top : top + WIN, 4 + win * WIN : 12 + win * WIN, :].reshape(AREA, 128)
                for win in range(WIN_COLS)
            ],
            axis=0,
        )
        label_rows = jnp.concatenate(
            [
                jnp.broadcast_to(ids_s[top + row : top + row + 1, :], (WIN, 128))
                for row in range(WIN)
            ],
            axis=0,
        )
        ln_one, normed_one, inverse_one = layer_norm(source, gain_one)
        yield
        qkv_all = matmul(ln_one, qkv_ref[...]).astype(jnp.bfloat16)
        yield
        grad_grid = jnp.zeros((WIN * PAD_COLS, 128), jnp.float32)
        for tap in range(3):
            first = (top + 2 - tap) * PAD_COLS
            taps = jnp.concatenate([conv_ref[3 * tap + side] for side in range(3)], axis=1)
            grad_grid = grad_grid + matmul_nt(gcat_s[first : first + WIN * PAD_COLS, :], taps)
        grad_grid = grad_grid.reshape(WIN, PAD_COLS, 128)
        grad_block = jnp.concatenate(
            [
                grad_grid[:, win * WIN : (win + 1) * WIN, :].reshape(AREA, 128)
                for win in range(WIN_COLS)
            ],
            axis=0,
        )
        saved, mixed_parts = [], []
        raw = []
        for win in range(WIN_COLS):
            part = qkv_all[win * AREA : (win + 1) * AREA]
            query, key, value = part[:, :128], part[:, 128:256], part[:, 256:]
            query_heads = by_heads(query, head_masks)
            picked = jnp.where(lane == win * WIN + lane_row % WIN, label_rows, 0.0)
            column = jnp.broadcast_to(
                jnp.sum(picked, axis=1, keepdims=True), (AREA, HEADS * AREA)
            )
            across = jnp.sum(jnp.where(diagonal, column, 0.0), axis=0, keepdims=True)
            scores = matmul_nt(key, query_heads) * score_scale + biases
            scores = jnp.where(column == across, scores, -1e30)
            raw.append((query_heads, key, value, scores))
        yield
        for query_heads, key, value, scores in raw:
            raised = jnp.exp(scores - jnp.max(scores, axis=0, keepdims=True))
            probabilities = raised * (1.0 / jnp.sum(raised, axis=0, keepdims=True))
            saved.append((query_heads, key, value, probabilities, probabilities.astype(jnp.bfloat16)))
        yield
        for query_heads, key, value, probabilities, weights in saved:
            mixed_parts.append(own_heads(matmul_tn(weights, value), head_lanes).astype(jnp.bfloat16))
        yield
        mixed = jnp.concatenate(mixed_parts, axis=0)
        projected = matmul(mixed, proj_ref[...]).astype(jnp.bfloat16)
        yield
        middle = source + projected.astype(jnp.float32)
        ln_two, normed_two, inverse_two = layer_norm(middle, gain_two)
        yield
        pre_act = matmul(ln_two, up_ref[...])
        yield
        cumulative = 0.5 * (1.0 + lax.erf(pre_act * 0.7071067811865476))
        hidden = (pre_act * cumulative).astype(jnp.bfloat16)
        slope = cumulative + pre_act * (jnp.exp(-0.5 * pre_act * pre_act) * 0.3989422804014327)
        yield
        block_out = (middle + matmul(hidden, down_ref[...])).astype(jnp.bfloat16).astype(jnp.float32)
        for win in range(WIN_COLS):
            piece = block_out[win * AREA : (win + 1) * AREA].reshape(WIN, WIN, 128)
            block_out_s[top : top + WIN, win * WIN : (win + 1) * WIN, :] = piece

        yield
        grad_block_b = grad_block.astype(jnp.bfloat16)
        grad_hidden = matmul_nt(grad_block_b, down_ref[...])
        yield
        grad_pre = (grad_hidden * slope).astype(jnp.bfloat16)
        grad_ln_two = matmul_nt(grad_pre, up_ref[...])
        yield
        grad_middle = grad_block + layer_norm_back(grad_ln_two, normed_two, inverse_two, gain_two)
        grad_att = grad_middle.astype(jnp.bfloat16)
        yield
        grad_mixed = matmul_nt(grad_att, proj_ref[...]).astype(jnp.bfloat16)
        yield
        grad_parts, steps_back = [], []
        for win in range(WIN_COLS):
            query_heads, key, value, probabilities, weights = saved[win]
            grad_heads = by_heads(grad_mixed[win * AREA : (win + 1) * AREA], head_masks)
            grad_probs = matmul_nt(value, grad_heads)
            grad_value = matmul(weights, grad_heads)
            steps_back.append((grad_probs, grad_value))
        yield
        grads = []
        for win in range(WIN_COLS):
            probabilities = saved[win][3]
            grad_probs = steps_back[win][0]
            centre = jnp.sum(probabilities * grad_probs, axis=0, keepdims=True)
            grad_scores = probabilities * (grad_probs - centre)
            if chunk and win:
                bias_sum = bias_sum + grad_scores
            grads.append(grad_scores.astype(jnp.bfloat16))
        yield
        for win in range(WIN_COLS):
            query_heads, key = saved[win][:2]
            grad_key = matmul(grads[win], query_heads) * score_scale
            grad_query = own_heads(matmul_tn(grads[win], key), head_lanes) * score_scale
            grad_parts.append(
                jnp.concatenate([grad_query, grad_key, steps_back[win][1]], axis=1).astype(
                    jnp.bfloat16
                )
            )
        yield
        grad_qkv = jnp.concatenate(grad_parts, axis=0)
        grad_ln_one = matmul_nt(grad_qkv, qkv_ref[...])
        yield
        grad_tokens = grad_middle + layer_norm_back(grad_ln_one, normed_one, inverse_one, gain_one)
        for win in range(WIN_COLS):
            piece = grad_tokens[win * AREA : (win + 1) * AREA].reshape(WIN, WIN, 128)
            grad_tokens_s[top : top + WIN, win * WIN : (win + 1) * WIN, :] = piece
        if chunk:
            gain_one_sum = gain_one_sum + jnp.sum(
                (grad_ln_one * normed_one)[AREA:], axis=0, keepdims=True
            )
            gain_two_sum = gain_two_sum + jnp.sum(
                (grad_ln_two * normed_two)[AREA:], axis=0, keepdims=True
            )
            kept = slice((chunk - 1) * (length - AREA), chunk * (length - AREA))
            ln_one_s[kept, :] = ln_one[AREA:]
            ln_two_s[kept, :] = ln_two[AREA:]
            hidden_s[kept, :] = hidden[AREA:]
            grad_pre_s[kept, :] = grad_pre[AREA:]
            grad_block_s[kept, :] = grad_block_b[AREA:]
            mixed_s[kept, :] = mixed[AREA:]
            grad_att_s[kept, :] = grad_att[AREA:]
            grad_qkv_s[kept, :] = grad_qkv[AREA:]


    running = []
    for chunk in range(WIN_ROWS):
        running.append(chunk_steps(chunk))
        for _ in range(2):
            running = [steps for steps in running if next(steps, running) is not running]
    while running:
        running = [steps for steps in running if next(steps, running) is not running]

    patches = shifted_columns(block_out_s, first_col, lat_total, own_rows, own_cols)
    count = own_rows * own_cols
    grad_own = fields_ref[1].reshape(count, 128)
    for tap in range(3):
        rows = patches[tap * own_cols : tap * own_cols + count]
        rows_s[tap * 384 : (tap + 1) * 384, :] = matmul_tn(rows, grad_own).astype(jnp.bfloat16)
    place = 1152
    for left, right, flipped in (
        (ln_one_s, grad_qkv_s, False),
        (mixed_s, grad_att_s, False),
        (ln_two_s, grad_pre_s, False),
        (hidden_s, grad_block_s, True),
    ):
        product = matmul_tn(left[...], right[...]).astype(jnp.bfloat16)
        if flipped:
            rows_s[place : place + product.shape[0], :] = product
            place = place + product.shape[0]
        else:
            for tile in range(product.shape[1] // 128):
                rows_s[place : place + 128, :] = product[:, tile * 128 : (tile + 1) * 128]
                place = place + 128
    small = [gain_one_sum, gain_two_sum] + table_rows(bias_sum)
    small.append(jnp.zeros((16 - len(small), 128), jnp.float32))
    rows_s[place : place + 16, :] = jnp.concatenate(small, axis=0).astype(jnp.bfloat16)
    place = place + 16
    rows_s[place:, :] = jnp.zeros((ROWS - place, 128), jnp.bfloat16)
    core = lax.axis_index("c")
    half = ROWS // 2
    kept_ref[...] = rows_s[pl.ds(pl.multiple_of(core * half, half), half), :]
    sent_ref[...] = rows_s[pl.ds(pl.multiple_of((1 - core) * half, half), half), :]


def per_device(
    tokens,
    grad_out,
    window_ids,
    qkv_weight,
    proj_weight,
    up_weight,
    down_weight,
    conv_weight,
    gain_one,
    gain_two,
    position_bias,
):
    row_count, col_count, width = tokens.shape
    lat_total = col_count * lax.axis_size(LAT)
    tokens_all = row_count * lat_total * lax.axis_size(LON)
    vmem = pl.BlockSpec(memory_space=pltpu.VMEM)
    params = pltpu.CompilerParams(vmem_limit_bytes=48 * 1024 * 1024)
    bf16 = lambda *shape: jax.ShapeDtypeStruct(shape, jnp.bfloat16)
    f32 = lambda *shape: jax.ShapeDtypeStruct(shape, jnp.float32)
    held = lambda *shape: pltpu.VMEM(shape, jnp.bfloat16)
    wide = lambda *shape: pltpu.VMEM(shape, jnp.float32)
    table = jnp.pad(position_bias, ((0, 0), (0, 1), (0, 1))).reshape(HEADS, 256)
    biases, gains = pl.pallas_call(
        bias_kernel,
        out_shape=(f32(AREA, HEADS * AREA), f32(WIN, width)),
        in_specs=[vmem] * 3,
        out_specs=(vmem,) * 2,
        compiler_params=params,
        cost_estimate=pl.CostEstimate(flops=10_000_000, bytes_accessed=80_000, transcendentals=0),
    )(table, gain_one[None], gain_two[None])
    slabs = TOKEN_RIM + GRAD_RIM + 1
    fields = jnp.stack([tokens, grad_out])
    far, near = pl.pallas_call(
        lon_pack_kernel,
        out_shape=(bf16(slabs, col_count, width),) * 2,
        in_specs=[vmem] * 2,
        out_specs=(vmem,) * 2,
        scratch_shapes=[wide(col_count, width)],
        compiler_params=params,
    )(fields, window_ids)
    lon_far = swapped(far, LON, False)
    lon_near = swapped(near, LON, True)
    far, near = pl.pallas_call(
        lat_pack_kernel,
        out_shape=(bf16(MESSAGE, width),) * 2,
        in_specs=[vmem] * 4,
        out_specs=(vmem,) * 2,
        scratch_shapes=[
            wide(2, TOKEN_ROWS, WIN, width),
            wide(2, GRAD_ROWS, WIN, width),
            wide(32, width),
            wide(2, MESSAGE, width),
        ],
        compiler_params=params,
    )(fields, window_ids, lon_far, lon_near)
    lat_far = swapped(far, LAT, False)
    lat_near = swapped(near, LAT, True)
    count = AREA * (WIN_ROWS - 1) * (WIN_COLS - 1)
    block_out, grad_grid, kept, sent = pl.pallas_call(
        functools.partial(block_kernel, lat_total),
        out_shape=(
            f32(TOKEN_ROWS, 40, width),
            f32(TOKEN_ROWS, 40, width),
            bf16(ROWS // 2, width),
            bf16(ROWS // 2, width),
        ),
        in_specs=[vmem] * 13,
        out_specs=(vmem,) * 4,
        scratch_shapes=[
            wide(TOKEN_ROWS, 48, width),
            wide(GRAD_ROWS, 56, width),
            wide(32, width),
            held(GRAD_ROWS * PAD_COLS, 3 * width),
            held(ROWS, width),
            held(count, width),
            held(count, width),
            held(count, 4 * width),
            held(count, 4 * width),
            held(count, width),
            held(count, width),
            held(count, width),
            held(count, 3 * width),
            wide(2, MESSAGE, width),
        ],
        compiler_params=params,
        cost_estimate=pl.CostEstimate(
            flops=3_000_000_000, bytes_accessed=8_000_000, transcendentals=2_000_000
        ),
    )(
        fields,
        window_ids,
        lon_far,
        lon_near,
        lat_far,
        lat_near,
        biases,
        gains,
        qkv_weight,
        proj_weight,
        up_weight,
        down_weight,
        conv_weight,
    )
    downscaled, grad_tokens = pl.pallas_call(
        functools.partial(finish_kernel, lat_total),
        out_shape=(bf16(*tokens.shape),) * 2,
        in_specs=[vmem] * 3,
        out_specs=(vmem,) * 2,
        compiler_params=params,
        cost_estimate=pl.CostEstimate(
            flops=160_000_000, bytes_accessed=1_600_000, transcendentals=0
        ),
    )(block_out, grad_grid, conv_weight)
    own, other = total_over_devices(kept, sent, 1.0 / math.sqrt(tokens_all))
    results = pl.pallas_call(
        unpack_kernel,
        out_shape=(
            f32(width, 3 * width),
            f32(width, width),
            f32(width, 4 * width),
            f32(4 * width, width),
            f32(9, width, width),
            f32(1, width),
            f32(1, width),
            f32(SPAN, HEADS, SPAN),
        ),
        in_specs=[vmem] * 2,
        out_specs=(vmem,) * 8,
        scratch_shapes=[held(ROWS, width)],
        compiler_params=params,
    )(own, other)
    return (downscaled, grad_tokens) + results[:5] + (
        results[5][0],
        results[6][0],
        results[7].swapaxes(0, 1),
    )


def solution(mesh):
    lon_count, lat_count = mesh.devices.shape
    near = math.gcd(lon_count, 8)
    parts = (lon_count // near, near // 2, 2, 2, lat_count // 2)
    fine = Mesh(mesh.devices.reshape(parts), ("zl", "x", "c", "zh", "y"))
    grid = P(LON, LAT, None)
    return jax.shard_map(
        per_device,
        mesh=fine,
        in_specs=(grid, grid, P(LON, LAT)) + (P(),) * 8,
        out_specs=(grid, grid) + (P(),) * 8,
        check_vma=False,
    )
```
